512 devices in a mesh: blk: 32 (over y, x), col: 16 (over z, core).
Axes of the slice: x: 4, y: 8, z: 8, core: 2. Of those that a mesh axis runs over, the one named last changes fastest.
Arguments:
- visit_cov: bfloat16 [32768, 128], P('blk'), may hold values from -6 to 6
- tumor_size: bfloat16 [32768], P('blk'), may hold values from -6 to 6
- visit_weight: bfloat16 [32768], P('blk'), may hold values from 0.5 to 2
- visit_owner: int32 [32768, 1], P('blk'), may hold values from 0 to 31; in each aligned block of 1024 rows (0 to 1023, 1024 to 2047, ...) at most 64 rows name the same one
- visit_patient: int32 [32768], P('blk'), may hold values from 0 to 127
- inducing_freq: bfloat16 [128, 2048], P(None, 'col'), may hold values from -1.5 to 1.5
- inducing_phase: bfloat16 [2048], P('col'), may hold values from -3.140625 to 3.140625
- node_cov: bfloat16 [4096, 16, 128], P('blk'), may hold values from -6 to 6
- event_time: float32 [4096], P('blk'), may hold values from 0.2 to 2
- event_flag: int32 [4096], P('blk'), may hold values 0 or 1
Outputs:
- loglik: float32 [4096], P('blk')
- mean_weights: float32 [2048], P('col')
The draws below stay inside these ranges and needn't reach their ends.
Inputs may be any that keep to these rules, and one draw needn't show every extreme that they name: `visit_owner`: among the visits entering one index of blk, no owner is named more than 64 times, a bound that some block reaches.
All inputs are finite; a program needn't handle non-finite values. No bound on the sum of `event_flag` on one device may be relied on, other than what follows from the above.
Results may differ from the reference program's by a relative error of at most 0.003.
Values may be sent and summed in bfloat16 or wider, within the bound.
No kernel may reach another device: no remote copies, remote signals or barrier semaphores. Data moves between devices by JAX's collectives and lax.ppermute only.
A program may use at most 64 MiB of HBM per device.

```python
import math
import jax
import jax.numpy as jnp
import numpy as np
from jax import lax

M = 2048
P_SIZE = 128
VIS_DEV = 1024
PAT_DEV = 128
QN = 16
ITERS = 3
VISITS = 32768
PATIENTS = 4096
CAP = 64
N_BLK = 32


def with_ends(array, stream_key, least, high):
    shape = array.shape
    place = [jax.random.randint(jax.random.fold_in(stream_key, axis), (), 0, shape[axis]) for axis in range(len(shape))]
    array = array.at[tuple(place)].set(least)
    longest = shape.index(max(shape))
    place[longest] = (place[longest] + 1) % shape[longest]
    return array.at[tuple(place)].set(high)


def levels(key, dims, shards, smallest, largest):
    loudness, own = 1.0, jax.random.fold_in(key, 6)
    for axis_at, parts in shards:
        steps = jnp.exp(jax.random.uniform(jax.random.fold_in(own, axis_at), (parts,), jnp.float32, smallest / len(shards), largest / len(shards)))
        loudness = loudness * jnp.repeat(steps, dims[axis_at] // parts).reshape([-1 if axis == axis_at else 1 for axis in range(len(dims))])
    return loudness


def shared_out(stream_key, own, number, rows, count, top, bound, lean):
    order = jax.random.permutation(stream_key, count)
    heavy_load, usual = portions_of(count, rows * top, bound, lean, True), portions_of(count, rows * top, bound, lean, False)
    places = jnp.arange(count)

    def named(sizes, turn):
        used = int((sizes > 0).sum())
        fixed = max(1, used // 4)
        moved = fixed + (places - fixed + turn * (used - fixed)) % max(1, count - fixed)
        return jnp.zeros((count,), jnp.int32).at[order[jnp.where(places < fixed, places, moved)]].set(jnp.asarray(sizes, jnp.int32))

    sizes = jnp.where(number % 4 == 0, named(heavy_load, number // 4), named(usual, number - number // 4 - 1))
    mixed = jax.random.permutation(jax.random.fold_in(own, 3), count)
    giver, sink = mixed[0:count // 2 * 2:2], mixed[1:count // 2 * 2:2]
    room = jnp.minimum(sizes[giver] - 1, bound - sizes[sink]) // 2
    room = jnp.where((giver == order[0]) | (sink == order[0]) | (sizes[sink] == 0), 0, jnp.maximum(room, 0))
    moved = jax.random.randint(jax.random.fold_in(own, 4), (count // 2,), 0, 1 << 20) % (room + 1)
    sizes = sizes.at[giver].add(-moved).at[sink].add(moved)
    labels = jnp.searchsorted(jnp.cumsum(sizes), jnp.arange(rows * top), side="right").astype(jnp.int32)
    table = labels.reshape(top, rows).T
    table = table[jax.random.permutation(jax.random.fold_in(own, 1), rows)]
    turn = jax.random.randint(jax.random.fold_in(own, 2), (rows, 1), 0, top)
    return jnp.take_along_axis(table, (jnp.arange(top)[None, :] + turn) % top, axis=1)


def portions_of(count, total, bound, skew, full):
    weights = [(1 << 20) // math.isqrt(standing ** skew) + 1 for standing in range(1, count + 1)]
    largest = bound if full else min(bound, max(-(-total // count), total * weights[0] // sum(weights)))
    least = 1 if total - largest >= count - 1 else 0
    holding, rest = [largest] + [least] * (count - 1), total - largest - least * (count - 1)
    while rest > 0:
        movable = [i for i in range(1, count) if holding[i] < largest] or [i for i in range(1, count) if holding[i] < bound]
        whole, budget = sum([weights[i] for i in movable]), rest
        for i in movable:
            extra = min(bound - holding[i], max(1, budget * weights[i] // whole), rest)
            holding[i] = holding[i] + extra
            rest = rest - extra
    return np.array(holding)


def normal_values(rng, dims, spread, limit, cuts=(), held_as=jnp.bfloat16):
    level = levels(rng, dims, cuts, -0.22, 0.18) if cuts else 1.0
    array = jax.random.normal(rng, dims, jnp.float32) * spread * level
    return jnp.minimum(jnp.maximum(array, -limit), limit).astype(held_as)


def setup_inputs(seed: int = 0) -> dict:
    key_list = jax.random.split(jax.random.key(seed), 11)
    visit_cov = normal_values(key_list[0], (VISITS, P_SIZE), 1.0, 6.0, ((0, 32),))
    tumor_size = normal_values(key_list[1], (VISITS,), 1.0, 6.0, ((0, 32),))
    visit_weight = jnp.clip(jnp.exp(math.log(2.0) - 1.3862944 * jax.random.uniform(key_list[2], (VISITS,), jnp.float32) ** levels(key_list[2], (VISITS,), ((0, 32),), -0.2, 0.2)), 0.5, 2.0).astype(jnp.bfloat16)
    visit_owner_keys = jax.random.split(jax.random.fold_in(key_list[3], 1), VISITS // VIS_DEV)
    visit_owner_turns = jax.random.permutation(jax.random.fold_in(key_list[3], 3), VISITS // VIS_DEV)
    visit_owner = jax.vmap(lambda own, number: shared_out(jax.random.fold_in(key_list[3], 2), own, number, VIS_DEV, N_BLK, 1, CAP, 2))(visit_owner_keys, visit_owner_turns).reshape((VISITS, 1))
    visit_patient = with_ends(jax.random.randint(key_list[4], (VISITS,), 0, PAT_DEV), jax.random.fold_in(key_list[4], 1), 0, PAT_DEV - 1).astype(jnp.int32)
    inducing_freq = normal_values(key_list[5], (P_SIZE, M), 0.25, 1.5, ((1, 16),))
    inducing_phase = jnp.clip(jax.random.uniform(key_list[6], (M,), jnp.float32, -3.140625, 3.140625), -3.140625, 3.140625).astype(jnp.bfloat16)
    node_cov = normal_values(key_list[7], (PATIENTS, QN, P_SIZE), 1.0, 6.0, ((0, 32),))
    event_time = jnp.clip(0.2 + 1.8 * jax.random.uniform(key_list[8], (PATIENTS,), jnp.float32) ** levels(key_list[8], (PATIENTS,), ((0, 32),), -0.2, 0.2), 0.2, 2.0)
    event_flag = with_ends((jax.random.randint(key_list[9], (PATIENTS,), 0, 2) < 1).astype(jnp.int32), jax.random.fold_in(key_list[9], 1), 0, 1)
    return {"visit_cov": visit_cov, "tumor_size": tumor_size, "visit_weight": visit_weight, "visit_owner": visit_owner, "visit_patient": visit_patient, "inducing_freq": inducing_freq, "inducing_phase": inducing_phase, "node_cov": node_cov, "event_time": event_time, "event_flag": event_flag}


SQRT_TWO = math.sqrt(2.0)
LOG_SHAPE = math.log(1.5)
LINK = 0.4

def features(covariates, frequency, phases):
    angles = jnp.dot(covariates, frequency, preferred_element_type=jnp.float32) + phases.astype(jnp.float32)
    return (SQRT_TWO * jnp.cos(angles)).astype(jnp.bfloat16)

def reference(visit_cov, tumor_size, visit_weight, visit_owner, visit_patient, inducing_freq, inducing_phase, node_cov, event_time, event_flag):
    cov_blocks = visit_cov.reshape(N_BLK, VIS_DEV, P_SIZE)
    weight_blocks = visit_weight.reshape(N_BLK, VIS_DEV)
    size_blocks = tumor_size.reshape(N_BLK, VIS_DEV)

    def accumulate(carry, inputs):
        gram, rhs = carry
        covariates, weights, sizes = inputs
        phi = features(covariates, inducing_freq, inducing_phase)
        weight_wide = weights.astype(jnp.float32)
        weighted = (weight_wide[:, None] * phi.astype(jnp.float32)).astype(jnp.bfloat16)
        gram = gram + jnp.dot(weighted.T, phi, preferred_element_type=jnp.float32)
        rhs = rhs + jnp.dot(weight_wide * sizes.astype(jnp.float32), phi.astype(jnp.float32), precision=lax.Precision.HIGHEST)
        return ((gram, rhs), None)
    start = (jnp.zeros((M, M), jnp.float32), jnp.zeros((M,), jnp.float32))
    (gram, rhs), _ = lax.scan(accumulate, start, (cov_blocks, weight_blocks, size_blocks))
    gram = gram / VISITS
    rhs = rhs / math.sqrt(VISITS)
    solution = jnp.zeros((M,), jnp.float32)
    residual = rhs
    direction = rhs
    norm_now = jnp.sum(residual * residual)
    for turn in range(ITERS):
        image = direction + jnp.dot(gram, direction, precision=lax.Precision.HIGHEST)
        alpha = norm_now / jnp.sum(direction * image)
        solution = solution + alpha * direction
        residual = residual - alpha * image
        norm_next = jnp.sum(residual * residual)
        direction = residual + norm_next / norm_now * direction
        norm_now = norm_next

    def fit_block(covariates):
        phi = features(covariates, inducing_freq, inducing_phase)
        return jnp.dot(phi.astype(jnp.float32), solution, precision=lax.Precision.HIGHEST)
    fitted = lax.map(fit_block, cov_blocks).reshape(VISITS) / math.sqrt(M)
    weights = visit_weight.astype(jnp.float32)
    patient_ids = (visit_owner[:, 0] * PAT_DEV + visit_patient).astype(jnp.int32)
    numer = jax.ops.segment_sum(weights * (tumor_size.astype(jnp.float32) - fitted), patient_ids, num_segments=PATIENTS)
    denom = 1.0 + jax.ops.segment_sum(weights, patient_ids, num_segments=PATIENTS)
    effect = numer / denom
    node_blocks = node_cov.reshape(N_BLK, PAT_DEV * QN, P_SIZE)
    node_value = lax.map(fit_block, node_blocks).reshape(PATIENTS, QN) / math.sqrt(M)
    grid = event_time[:, None] * (jnp.arange(QN).astype(jnp.float32)[None, :] + 1.0) / QN
    eta = LOG_SHAPE + 0.5 * jnp.log(grid) + LINK * (node_value + effect[:, None])
    loglik = event_flag.astype(jnp.float32) * eta[:, -1] - event_time / QN * lax.optimization_barrier(jnp.sum(jnp.exp(eta), axis=1))
    return (loglik, solution)
```

```python
import functools
import math

import jax
import jax.numpy as jnp
import numpy as np
from jax import lax
from jax.experimental import pallas as pl
from jax.experimental.pallas import tpu as pltpu
from jax.sharding import PartitionSpec as P

F32 = jnp.float32
BF16 = jnp.bfloat16
LOG_SHAPE = math.log(1.5)
LINK = 0.4
LANES = 128
LIMIT = 20 * 1024 * 1024


def cosine_table():
    nodes = 0.125 + 0.125 * np.cos(np.pi * (np.arange(400) + 0.5) / 400)
    values = math.sqrt(2.0) * np.cos(2.0 * np.pi * np.sqrt(nodes))
    fit = np.polynomial.chebyshev.Chebyshev.fit(nodes, values, 5, domain=[0.0, 0.25])
    return [float(c) for c in fit.convert(kind=np.polynomial.Polynomial).coef]


COEFS = cosine_table()
PER_TURN = 1.0 / (2.0 * math.pi)


def feature(angles):
    turns = angles * PER_TURN
    turns = turns - jnp.round(turns)
    square = turns * turns
    total = COEFS[-1]
    for coef in COEFS[-2::-1]:
        total = total * square + coef
    return total.astype(BF16)


def split3(value):
    high = value.astype(BF16).astype(F32)
    rest = value - high
    middle = rest.astype(BF16).astype(F32)
    low = (rest - middle).astype(BF16).astype(F32)
    return high, middle, low


def stack_rows(rows, height):
    at = lax.broadcasted_iota(jnp.int32, (height, rows[0].shape[1]), 0)
    total = jnp.zeros((height, rows[0].shape[1]), F32)
    for index, row in enumerate(rows):
        total = jnp.where(at == index, row, total)
    return total.astype(BF16)


def as_row(tiles):
    return jnp.concatenate([tiles[j : j + 1, :] for j in range(tiles.shape[0])], axis=1)


def dot_nt(a, b):
    return lax.dot_general(a, b, (((1,), (1,)), ((), ())), preferred_element_type=F32)


def dot_nn(a, b):
    return jnp.dot(a, b, preferred_element_type=F32)


VMEM = pl.BlockSpec(memory_space=pltpu.VMEM)
SMEM = pl.BlockSpec(memory_space=pltpu.SMEM)
BLOCK = 256
PHASE_ROWS = 8


def rows_at(index, size):
    return pl.ds(pl.multiple_of(index * size, size), size)


def total_of(x):
    return jnp.sum(jnp.sum(x, axis=0, keepdims=True), axis=1, keepdims=True)


def params():
    return pltpu.CompilerParams(vmem_limit_bytes=LIMIT)


def cost(flops, size, hard=0):
    return pl.CostEstimate(flops=flops, bytes_accessed=size, transcendentals=hard)


def pack_kernel(freq, phase, out):
    depth = freq.shape[0]
    values = freq[...]
    last = jnp.broadcast_to(phase[...], (PHASE_ROWS, phase.shape[1]))
    for copy in range(out.shape[0]):
        out[copy, 0:depth, :] = values
        out[copy, depth : depth + PHASE_ROWS, :] = last


def feature_block(rows, freq, store):
    depth = rows.shape[1]
    for j in range(0, freq.shape[0], 2):
        both = jnp.concatenate([freq[j, :depth, :], freq[j + 1, :depth, :]], axis=1)
        phase = jnp.concatenate(
            [freq[j, depth : depth + 1, :], freq[j + 1, depth : depth + 1, :]], axis=1
        )
        store(j * LANES, feature(dot_nn(rows, both) + phase.astype(F32)))


FEATURE_ROWS = 128


def features_kernel(cov, *rest):
    freqs, out = rest[:-1], rest[-1]

    def step(i, carry):
        at = rows_at(i, FEATURE_ROWS)
        base = 0
        for freq in freqs:

            def store(column, value, base=base):
                out[at, base + column : base + column + value.shape[1]] = value

            feature_block(cov[at, :], freq, store)
            base += freq.shape[0] * LANES
        return carry

    lax.fori_loop(0, cov.shape[0] // FEATURE_ROWS, step, 0)


def features(cov, freqs, name):
    rows, depth = cov.shape
    columns = sum(f.shape[0] * f.shape[2] for f in freqs)
    return pl.pallas_call(
        features_kernel,
        in_specs=[VMEM] * (1 + len(freqs)),
        out_specs=VMEM,
        out_shape=jax.ShapeDtypeStruct((rows, columns), BF16),
        compiler_params=params(),
        cost_estimate=cost(2 * rows * depth * columns + 20 * rows * columns, 2 * rows * columns),
        name=name,
    )(cov, *freqs)


def near_kernel(cov, freq, weight, size, phi, out, gathered, tiles):
    product = weight[...].astype(F32) * size[...].astype(F32)
    split = stack_rows(split3(product), 16)
    gathered[...] = jnp.zeros_like(gathered)
    for i in range(cov.shape[0] // BLOCK):
        at = slice(i * BLOCK, (i + 1) * BLOCK)
        left = split[:, at]

        def store(column, value, at=at, left=left):
            where = slice(column, column + value.shape[1])
            phi[at, where] = value
            gathered[:, where] += dot_nn(left, value)

        feature_block(cov[at, :], freq, store)
    send_whole(gathered, tiles, out)


def rows_of(vector):
    return stack_rows(split3(as_row(vector)), 16)


def send_whole(gathered, tiles, out):
    total = jnp.sum(gathered[...], axis=0, keepdims=True)
    for j in range(tiles.shape[0]):
        tiles[j : j + 1, :] = total[:, j * LANES : (j + 1) * LANES]
    whole = tiles[...]
    for copy in range(out.shape[0]):
        out[copy] = whole


def forward(direction, phis):
    split = rows_of(direction)
    total, base = 0.0, 0
    for phi in phis:
        total = total + dot_nt(split[:, base : base + phi.shape[1]], phi[...])
        base += phi.shape[1]
    return jnp.sum(total, axis=0, keepdims=True)


def product(direction, phis, weight, gathered, tiles, out, scale):
    values = forward(direction, phis)
    split = stack_rows(split3(weight[...].astype(F32) * values * scale), 16)
    base = 0
    for phi in phis:
        gathered[:, base : base + phi.shape[1]] = dot_nn(split, phi[...])
        base += phi.shape[1]
    send_whole(gathered, tiles, out)
    return values


def first_kernel(scale, core, halves, near, far, weight, out, values_out, rhs_out, gathered, tiles):
    low, high = halves[0], halves[1]
    swap = core[0] == 1
    half = low.shape[0]
    rhs_out[0:half, :] = jnp.where(swap, high, low)
    rhs_out[half : 2 * half, :] = jnp.where(swap, low, high)
    values_out[...] = product(rhs_out[...], (near, far), weight, gathered, tiles, out, scale)


def second_kernel(
    scale, arrived, rhs, before, near, far, weight,
    out, fit_out, solution_out, residual_out, direction_out,
    gathered, tiles,
):
    direction = rhs[...]
    norm = total_of(direction * direction)
    image = direction + jnp.sum(arrived[...], axis=0)
    length = norm / total_of(direction * image)
    residual = direction - length * image
    later = residual + total_of(residual * residual) / norm * direction
    solution_out[...] = length * direction
    residual_out[...] = residual
    direction_out[...] = later
    fit_out[0:1, :] = length * before[...]
    fit_out[1:2, :] = product(later, (near, far), weight, gathered, tiles, out, scale)


def third_kernel(
    scale, fit_scale, arrived, solution, residual, direction, fit, near, far, weight, size, owner, patient,
    out, both_out, norm_out,
):
    before = direction[...]
    left = residual[...]
    norm = total_of(left * left)
    image = before + jnp.sum(arrived[...], axis=0)
    length = norm / total_of(before * image)
    left = left - length * image
    norm_next = total_of(left * left)
    later = left + norm_next / norm * before
    both_out[0] = solution[...] + length * before
    both_out[1] = later
    norm_out[...] = jnp.broadcast_to(norm_next, norm_out.shape)
    values = forward(later, (near, far))
    fitted = fit[0:1, :] + length * fit[1:2, :]
    weights = weight[...].astype(F32)
    weighted = weights * values
    energy = total_of(weighted * values) * scale
    rest = weights * (size[...].astype(F32) - fitted * fit_scale)
    owners, patients = out.shape[0], out.shape[2]
    here = values.shape[1]
    to_owner = (owner[...] == lax.broadcasted_iota(jnp.int32, (owners, here), 0)).astype(F32)
    to_patient = (patient[...] == lax.broadcasted_iota(jnp.int32, (patients, here), 0)).astype(F32)
    parts = split3(rest) + split3(weighted * fit_scale) + (weights,)
    tall = jnp.concatenate([to_owner * part for part in parts], axis=0).astype(BF16)
    sums = dot_nt(tall, to_patient.astype(BF16))
    part = [sums[i * owners : (i + 1) * owners, :] for i in range(len(parts))]
    out[:, 0, :] = part[0] + part[1] + part[2]
    out[:, 1, :] = part[3] + part[4] + part[5]
    out[:, 2, :] = part[6]
    out[:, 3, :] = jnp.broadcast_to(energy, (owners, patients))


def nodes_kernel(both, first, second, out):
    rows = split3(as_row(both[0])) + split3(as_row(both[1]))
    split = stack_rows(rows, 16)
    base = 0
    for phi in (first, second):
        products = dot_nt(split, phi[...])
        where = slice(base, base + phi.shape[0])
        out[0:1, where] = products[0:1] + products[1:2] + products[2:3]
        out[1:2, where] = products[3:4] + products[4:5] + products[5:6]
        base += phi.shape[0]


def last_kernel(fit_scale, mine, arrived, both, norm, node_values, time, flag, loglik, weights_out, tiles):
    sums = jnp.sum(arrived[...], axis=0)
    direction = both[1]
    denominator = total_of(direction * direction) + sums[3:4, 0:1]
    length = norm[0:1, 0:1] / denominator
    tiles[...] = both[0] + length * direction
    weights_out[...] = tiles[pl.ds(mine[0], 1), :]
    effect = (sums[0:1, :] - length * sums[1:2, :]) / (1.0 + sums[2:3, :])
    values = (node_values[0:1, :] + length * node_values[1:2, :]) * fit_scale
    patients = loglik.shape[1]
    nodes = values.shape[1] // patients
    total = jnp.zeros_like(effect)
    eta = total
    when = time[...]
    for q in range(nodes):
        grid = when * (q + 1.0) / nodes
        eta = (
            LOG_SHAPE
            + 0.5 * jnp.log(grid)
            + LINK * (values[:, q * patients : (q + 1) * patients] + effect)
        )
        total = total + jnp.exp(eta)
    loglik[...] = flag[...].astype(F32) * eta - when / nodes * total


def on_device(
    visit_cov,
    tumor_size,
    visit_weight,
    visit_owner,
    visit_patient,
    inducing_freq,
    inducing_phase,
    node_cov,
    event_time,
    event_flag,
):
    blocks, cols = lax.axis_size("blk"), lax.axis_size("col")
    rows, depth = visit_cov.shape
    own = inducing_freq.shape[1]
    inducing = own * cols
    tall = inducing // LANES
    layers = cols // 2
    patients, nodes = node_cov.shape[:2]
    scale = 1.0 / (rows * blocks)
    fit_scale = 1.0 / math.sqrt(inducing)
    weight = visit_weight.reshape(1, rows)
    size = tumor_size.reshape(1, rows)
    owner = visit_owner.reshape(1, rows)
    patient = visit_patient.reshape(1, rows)
    place = lax.axis_index("col").astype(jnp.int32)
    core = (place % 2).reshape(1)
    layer = (place // 2).reshape(1)
    together = lax.optimization_barrier
    same_core = [[2 * z + c for z in range(layers)] for c in range(2)]
    pairs = [[2 * z, 2 * z + 1] for z in range(layers)]
    swap = [(i, i ^ 1) for i in range(cols)]

    packed = pl.pallas_call(
        pack_kernel,
        in_specs=[VMEM, VMEM],
        out_specs=VMEM,
        out_shape=jax.ShapeDtypeStruct((layers, depth + PHASE_ROWS, own), BF16),
        compiler_params=params(),
        name="pack",
    )(inducing_freq, inducing_phase.reshape(1, own))
    near_freq = lax.all_to_all(packed, "col", 0, 0, tiled=True, axis_index_groups=same_core)

    half = inducing // 2
    near, sent = pl.pallas_call(
        near_kernel,
        in_specs=[VMEM] * 4,
        out_specs=[VMEM] * 2,
        out_shape=[
            jax.ShapeDtypeStruct((rows, half), BF16),
            jax.ShapeDtypeStruct((blocks, tall // 2, LANES), F32),
        ],
        scratch_shapes=[pltpu.VMEM((16, half), F32), pltpu.VMEM((tall // 2, LANES), F32)],
        compiler_params=params(),
        name="near_features",
    )(visit_cov, near_freq, weight, size)
    sent, late_freq = together((sent, near_freq))
    arrived = lax.all_to_all(sent, "blk", 0, 0, tiled=True)
    far_freq = lax.ppermute(late_freq, "col", swap)
    far = features(visit_cov, (far_freq,), "far_features")
    arrived, far = together((arrived, far))
    rhs = jnp.sum(arrived, axis=0) * (1.0 / math.sqrt(rows * blocks))
    halves = lax.all_gather(rhs, "col", axis_index_groups=pairs)

    by_node = node_cov.transpose(1, 0, 2).reshape(nodes * patients, depth)
    count = nodes * patients // 2
    message = jax.ShapeDtypeStruct((blocks, tall, LANES), F32)
    vector = jax.ShapeDtypeStruct((tall, LANES), F32)
    scratch = [pltpu.VMEM((16, inducing), F32), pltpu.VMEM((tall, LANES), F32)]
    work = cost(64 * rows * inducing, 2 * rows * inducing)

    sent, before, rhs = pl.pallas_call(
        functools.partial(first_kernel, scale),
        in_specs=[SMEM] + [VMEM] * 4,
        out_specs=[VMEM] * 3,
        out_shape=[message, jax.ShapeDtypeStruct((1, rows), F32), vector],
        scratch_shapes=scratch,
        compiler_params=params(),
        cost_estimate=work,
        name="first_product",
    )(core, halves, near, far, weight)
    sent, node_cov_now = together((sent, by_node[:count]))
    arrived = lax.all_to_all(sent, "blk", 0, 0, tiled=True)
    node_first = features(node_cov_now, (near_freq, far_freq), "node_features_a")
    arrived, node_first = together((arrived, node_first))

    sent, fit, solution, residual, direction = pl.pallas_call(
        functools.partial(second_kernel, scale),
        in_specs=[VMEM] * 6,
        out_specs=[VMEM] * 5,
        out_shape=[message, jax.ShapeDtypeStruct((2, rows), F32), vector, vector, vector],
        scratch_shapes=scratch,
        compiler_params=params(),
        cost_estimate=work,
        name="second_product",
    )(arrived, rhs, before, near, far, weight)
    sent, node_cov_now = together((sent, by_node[count:]))
    arrived = lax.all_to_all(sent, "blk", 0, 0, tiled=True)
    node_second = features(node_cov_now, (near_freq, far_freq), "node_features_b")
    arrived, node_second = together((arrived, node_second))

    sent, both, norm = pl.pallas_call(
        functools.partial(third_kernel, scale, fit_scale),
        in_specs=[VMEM] * 11,
        out_specs=[VMEM] * 3,
        out_shape=[
            jax.ShapeDtypeStruct((blocks, 4, patients), F32),
            jax.ShapeDtypeStruct((2, tall, LANES), F32),
            jax.ShapeDtypeStruct((8, LANES), F32),
        ],
        compiler_params=params(),
        cost_estimate=work,
        name="third_product",
    )(arrived, solution, residual, direction, fit, near, far, weight, size, owner, patient)
    sent, both = together((sent, both))
    arrived = lax.all_to_all(sent, "blk", 0, 0, tiled=True)
    node_values = pl.pallas_call(
        nodes_kernel,
        in_specs=[VMEM] * 3,
        out_specs=VMEM,
        out_shape=jax.ShapeDtypeStruct((2, 2 * count), F32),
        compiler_params=params(),
        cost_estimate=cost(64 * 2 * count * inducing, 4 * count * inducing),
        name="node_values",
    )(both, node_first, node_second)
    arrived, node_values = together((arrived, node_values))

    loglik, weights = pl.pallas_call(
        functools.partial(last_kernel, fit_scale),
        in_specs=[SMEM] + [VMEM] * 6,
        out_specs=[VMEM, VMEM],
        out_shape=[
            jax.ShapeDtypeStruct((1, patients), F32),
            jax.ShapeDtypeStruct((1, own), F32),
        ],
        scratch_shapes=[pltpu.VMEM((tall, LANES), F32)],
        compiler_params=params(),
        name="last",
    )(
        layer,
        arrived,
        both,
        norm,
        node_values,
        event_time.reshape(1, patients),
        event_flag.reshape(1, patients),
    )
    return loglik.reshape(patients), weights.reshape(own)


def solution(mesh):
    in_specs = (
        P("blk", None),
        P("blk"),
        P("blk"),
        P("blk", None),
        P("blk"),
        P(None, "col"),
        P("col"),
        P("blk", None, None),
        P("blk"),
        P("blk"),
    )
    out_specs = (P("blk"), P("col"))
    return jax.shard_map(
        on_device, mesh=mesh, in_specs=in_specs, out_specs=out_specs, check_vma=False
    )
```

```python
import functools
import math

import jax
import jax.numpy as jnp
import numpy as np
from jax import lax
from jax.experimental import pallas as pl
from jax.experimental.pallas import tpu as pltpu
from jax.sharding import PartitionSpec as P

F32 = jnp.float32
BF16 = jnp.bfloat16
LOG_SHAPE = math.log(1.5)
LINK = 0.4
LANES = 128
MIB = 1024 * 1024


def cosine_table():
    nodes = 0.125 + 0.125 * np.cos(np.pi * (np.arange(400) + 0.5) / 400)
    values = math.sqrt(2.0) * np.cos(2.0 * np.pi * np.sqrt(nodes))
    fit = np.polynomial.chebyshev.Chebyshev.fit(nodes, values, 5, domain=[0.0, 0.25])
    return [float(c) for c in fit.convert(kind=np.polynomial.Polynomial).coef]


COEFS = cosine_table()
PER_TURN = 1.0 / (2.0 * math.pi)


def feature(angles):
    turns = angles * PER_TURN
    turns = turns - jnp.round(turns)
    square = turns * turns
    total = COEFS[-1]
    for coef in COEFS[-2::-1]:
        total = total * square + coef
    return total.astype(BF16)


def split3(value):
    high = value.astype(BF16).astype(F32)
    rest = value - high
    middle = rest.astype(BF16).astype(F32)
    low = (rest - middle).astype(BF16).astype(F32)
    return high, middle, low


def stack_rows(rows, height):
    at = lax.broadcasted_iota(jnp.int32, (height, rows[0].shape[1]), 0)
    total = jnp.zeros((height, rows[0].shape[1]), F32)
    for index, row in enumerate(rows):
        total = jnp.where(at == index, row, total)
    return total.astype(BF16)


def as_row(tiles):
    return jnp.concatenate([tiles[j : j + 1, :] for j in range(tiles.shape[0])], axis=1)


def dot_nt(a, b):
    return lax.dot_general(a, b, (((1,), (1,)), ((), ())), preferred_element_type=F32)


def dot_nn(a, b):
    return jnp.dot(a, b, preferred_element_type=F32)


VMEM = pl.BlockSpec(memory_space=pltpu.VMEM)
SMEM = pl.BlockSpec(memory_space=pltpu.SMEM)
HBM = pl.BlockSpec(memory_space=pltpu.HBM)
PARTS = 4
SPARE = 9
PHASE_ROWS = 8


def rows_at(index, size):
    return pl.ds(pl.multiple_of(index * size, size), size)


def total_of(x):
    return jnp.sum(jnp.sum(x, axis=0, keepdims=True), axis=1, keepdims=True)


def params(mebibytes=48):
    return pltpu.CompilerParams(vmem_limit_bytes=mebibytes * MIB)


def cost(flops, size, hard=0):
    return pl.CostEstimate(flops=flops, bytes_accessed=size, transcendentals=hard)


def pack_kernel(freq, phase, out, packed, row, sems):
    depth = freq.shape[0]
    loads = [
        pltpu.make_async_copy(freq, packed.at[0:depth], sems.at[0]),
        pltpu.make_async_copy(phase, row, sems.at[1]),
    ]
    for load in loads:
        load.start()
    for load in loads:
        load.wait()
    packed[depth : depth + PHASE_ROWS, :] = jnp.broadcast_to(
        row[...], (PHASE_ROWS, row.shape[1])
    )
    stores = [
        pltpu.make_async_copy(packed, out.at[copy], sems.at[2 + copy])
        for copy in range(out.shape[0])
    ]
    for store in stores:
        store.start()
    for store in stores:
        store.wait()


def stage_kernel(value, out):
    out[...] = value[...]


def stage(value, name):
    return pl.pallas_call(
        stage_kernel,
        in_specs=[VMEM],
        out_specs=VMEM,
        out_shape=jax.ShapeDtypeStruct(value.shape, value.dtype),
        compiler_params=params(),
        cost_estimate=cost(value.size, 4 * value.size),
        name=name,
    )(value)


def feature_block(rows, freq, store):
    depth = rows.shape[1]
    for j in range(0, freq.shape[0], 2):
        both = jnp.concatenate([freq[j, :depth, :], freq[j + 1, :depth, :]], axis=1)
        phase = jnp.concatenate(
            [freq[j, depth : depth + 1, :], freq[j + 1, depth : depth + 1, :]], axis=1
        )
        store(j * LANES, feature(dot_nn(rows, both) + phase.astype(F32)))


FEATURE_ROWS = 256


def features_kernel(order, core, cov, freq, out):
    half = freq.shape[1] * LANES

    def step(i, carry):
        at = rows_at(i, FEATURE_ROWS)
        for index, other in enumerate(order):
            source = 1 - core[0] if other else core[0]

            def store(column, value, base=index * half):
                out[at, base + column : base + column + value.shape[1]] = value

            feature_block(cov[at, :], freq.at[source], store)
        return carry

    lax.fori_loop(0, cov.shape[0] // FEATURE_ROWS, step, 0)


def features(core, cov, freq, order, name):
    rows, depth = cov.shape
    columns = len(order) * freq.shape[1] * LANES
    return pl.pallas_call(
        functools.partial(features_kernel, order),
        in_specs=[SMEM, VMEM, VMEM],
        out_specs=VMEM,
        out_shape=jax.ShapeDtypeStruct((rows, columns), BF16),
        compiler_params=params(),
        cost_estimate=cost(2 * rows * depth * columns + 20 * rows * columns, 2 * rows * columns),
        name=name,
    )(core, cov, freq)


def near_kernel(cov, freq, weight, size, phi_out, out, phi, gathered, tiles, sems):
    def part(i):
        at = rows_at(i, FEATURE_ROWS)
        return pltpu.make_async_copy(phi.at[at], phi_out.at[at], sems.at[i])

    def step(i, carry):
        at = rows_at(i, FEATURE_ROWS)

        def store(column, value):
            phi[at, column : column + value.shape[1]] = value

        feature_block(cov[at, :], freq, store)
        part(i).start()
        return carry

    steps = cov.shape[0] // FEATURE_ROWS
    lax.fori_loop(0, steps, step, 0)
    product = weight[...].astype(F32) * size[...].astype(F32)
    gathered[...] = dot_nn(stack_rows(split3(product), 16), phi[...])
    send_whole(gathered, tiles, out)
    for i in range(steps):
        part(i).wait()


def rows_of(vector):
    return stack_rows(split3(as_row(vector)), 16)


def send_whole(gathered, tiles, out):
    total = jnp.sum(gathered[...], axis=0, keepdims=True)
    for j in range(tiles.shape[0]):
        tiles[j : j + 1, :] = total[:, j * LANES : (j + 1) * LANES]
    whole = tiles[...]
    for copy in range(out.shape[0]):
        out[copy] = whole


def fetch(near, held, sems):
    part = held.shape[0] // PARTS
    copies = []
    for k in range(PARTS):
        at = slice(k * part, (k + 1) * part)
        copy = pltpu.make_async_copy(near.at[at], held.at[at], sems.at[k])
        copy.start()
        copies.append((at, copy))
    return copies


def forward(direction, held, copies, far):
    split = rows_of(direction)
    half = far.shape[1]
    total = jnp.sum(dot_nt(split[:, half:], far[...]), axis=0, keepdims=True)
    values = []
    for at, copy in copies:
        copy.wait()
        part = jnp.sum(dot_nt(split[:, :half], held[at]), axis=0, keepdims=True)
        values.append(part + total[:, at])
    return jnp.concatenate(values, axis=1)


def product(direction, held, copies, far, weight, gathered, tiles, out, scale):
    values = forward(direction, held, copies, far)
    split = stack_rows(split3(weight[...].astype(F32) * values * scale), 16)
    half = far.shape[1]
    gathered[:, :half] = dot_nn(split, held[...])
    gathered[:, half:] = dot_nn(split, far[...])
    send_whole(gathered, tiles, out)
    return values


def first_kernel(
    scale, core, halves, near, far, weight, out, values_out, rhs_out, gathered, tiles, held, sems
):
    copies = fetch(near, held, sems)
    low, high = halves[0], halves[1]
    swap = core[0] == 1
    half = low.shape[0]
    rhs_out[0:half, :] = jnp.where(swap, high, low)
    rhs_out[half : 2 * half, :] = jnp.where(swap, low, high)
    values_out[...] = product(
        rhs_out[...], held, copies, far, weight, gathered, tiles, out, scale
    )


def second_kernel(
    scale, arrived, rhs, before, near, far, weight,
    out, fit_out, solution_out, residual_out, direction_out,
    gathered, tiles, held, sems,
):
    copies = fetch(near, held, sems)
    direction = rhs[...]
    norm = total_of(direction * direction)
    image = direction + jnp.sum(arrived[...], axis=0)
    length = norm / total_of(direction * image)
    residual = direction - length * image
    later = residual + total_of(residual * residual) / norm * direction
    solution_out[...] = length * direction
    residual_out[...] = residual
    direction_out[...] = later
    fit_out[0:1, :] = length * before[...]
    fit_out[1:2, :] = product(
        later, held, copies, far, weight, gathered, tiles, out, scale
    )


def third_kernel(
    scale, fit_scale, arrived, solution, residual, direction, fit, near, far, weight, size, owner, patient,
    out, both_out, norm_out,
    held, sems,
):
    copies = fetch(near, held, sems)
    before = direction[...]
    left = residual[...]
    norm = total_of(left * left)
    image = before + jnp.sum(arrived[...], axis=0)
    length = norm / total_of(before * image)
    left = left - length * image
    norm_next = total_of(left * left)
    later = left + norm_next / norm * before
    both_out[0] = solution[...] + length * before
    both_out[1] = later
    norm_out[...] = jnp.broadcast_to(norm_next, norm_out.shape)
    values = forward(later, held, copies, far)
    fitted = fit[0:1, :] + length * fit[1:2, :]
    weights = weight[...].astype(F32)
    weighted = weights * values
    energy = total_of(weighted * values) * scale
    rest = weights * (size[...].astype(F32) - fitted * fit_scale)
    owners, patients = out.shape[0], out.shape[2]
    here = values.shape[1]
    to_owner = (owner[...] == lax.broadcasted_iota(jnp.int32, (owners, here), 0)).astype(F32)
    to_patient = (patient[...] == lax.broadcasted_iota(jnp.int32, (patients, here), 0)).astype(F32)
    parts = split3(rest) + split3(weighted * fit_scale) + (weights,)
    tall = jnp.concatenate([to_owner * part for part in parts], axis=0).astype(BF16)
    sums = dot_nt(tall, to_patient.astype(BF16))
    part = [sums[i * owners : (i + 1) * owners, :] for i in range(len(parts))]
    out[:, 0, :] = part[0] + part[1] + part[2]
    out[:, 1, :] = part[3] + part[4] + part[5]
    out[:, 2, :] = part[6]
    out[:, 3, :] = jnp.broadcast_to(energy, (owners, patients))


def nodes_kernel(both, first, second, out):
    rows = split3(as_row(both[0])) + split3(as_row(both[1]))
    split = stack_rows(rows, 16)
    base = 0
    for phi in (first, second):
        products = dot_nt(split, phi[...])
        where = slice(base, base + phi.shape[0])
        out[0:1, where] = products[0:1] + products[1:2] + products[2:3]
        out[1:2, where] = products[3:4] + products[4:5] + products[5:6]
        base += phi.shape[0]


def last_kernel(fit_scale, mine, arrived, both, norm, node_values, time, flag, loglik, weights_out, tiles):
    sums = jnp.sum(arrived[...], axis=0)
    direction = both[1]
    denominator = total_of(direction * direction) + sums[3:4, 0:1]
    length = norm[0:1, 0:1] / denominator
    tiles[...] = both[0] + length * direction
    weights_out[...] = tiles[pl.ds(mine[0], 1), :]
    effect = (sums[0:1, :] - length * sums[1:2, :]) / (1.0 + sums[2:3, :])
    values = (node_values[0:1, :] + length * node_values[1:2, :]) * fit_scale
    patients = loglik.shape[1]
    nodes = values.shape[1] // patients
    total = jnp.zeros_like(effect)
    eta = total
    when = time[...]
    for q in range(nodes):
        grid = when * (q + 1.0) / nodes
        eta = (
            LOG_SHAPE
            + 0.5 * jnp.log(grid)
            + LINK * (values[:, q * patients : (q + 1) * patients] + effect)
        )
        total = total + jnp.exp(eta)
    loglik[...] = flag[...].astype(F32) * eta - when / nodes * total


def on_device(
    visit_cov,
    tumor_size,
    visit_weight,
    visit_owner,
    visit_patient,
    inducing_freq,
    inducing_phase,
    node_cov,
    event_time,
    event_flag,
):
    blocks, cols = lax.axis_size("blk"), lax.axis_size("col")
    rows, depth = visit_cov.shape
    own = inducing_freq.shape[1]
    inducing = own * cols
    tall = inducing // LANES
    layers = cols // 2
    patients, nodes = node_cov.shape[:2]
    scale = 1.0 / (rows * blocks)
    fit_scale = 1.0 / math.sqrt(inducing)
    weight = visit_weight.reshape(1, rows)
    size = tumor_size.reshape(1, rows)
    owner = visit_owner.reshape(1, rows)
    patient = visit_patient.reshape(1, rows)
    place = lax.axis_index("col").astype(jnp.int32)
    core = (place % 2).reshape(1)
    layer = (place // 2).reshape(1)
    together = lax.optimization_barrier
    same_core = [[2 * z + c for z in range(layers)] for c in range(2)]
    pairs = [[2 * z, 2 * z + 1] for z in range(layers)]

    packed = pl.pallas_call(
        pack_kernel,
        in_specs=[HBM, HBM],
        out_specs=HBM,
        out_shape=jax.ShapeDtypeStruct((layers, depth + PHASE_ROWS, own), BF16),
        scratch_shapes=[
            pltpu.VMEM((depth + PHASE_ROWS, own), BF16),
            pltpu.VMEM((1, own), BF16),
            pltpu.SemaphoreType.DMA((2 + layers,)),
        ],
        compiler_params=params(60),
        name="pack",
    )(inducing_freq, inducing_phase.reshape(1, own))
    packed, cov = together((packed, visit_cov))
    near_freq = lax.all_to_all(packed, "col", 0, 0, tiled=True, axis_index_groups=same_core)
    cov = stage(cov, "stage_cov")
    near_freq, cov = together((near_freq, cov))

    half = inducing // 2
    near, sent = pl.pallas_call(
        near_kernel,
        in_specs=[VMEM] * 4,
        out_specs=[HBM, VMEM],
        out_shape=[
            jax.ShapeDtypeStruct((SPARE * rows, half), BF16),
            jax.ShapeDtypeStruct((blocks, tall // 2, LANES), F32),
        ],
        scratch_shapes=[
            pltpu.VMEM((rows, half), BF16),
            pltpu.VMEM((16, half), F32),
            pltpu.VMEM((tall // 2, LANES), F32),
            pltpu.SemaphoreType.DMA((rows // FEATURE_ROWS,)),
        ],
        compiler_params=params(),
        name="near_features",
    )(cov, near_freq, weight, size)
    sent, late_freq = together((sent, near_freq))
    arrived = lax.all_to_all(sent, "blk", 0, 0, tiled=True)
    freq = lax.all_gather(late_freq, "col", axis_index_groups=pairs)
    far = features(core, cov, freq, (1,), "far_features")
    by_node = node_cov.transpose(1, 0, 2).reshape(nodes * patients, depth)
    count = nodes * patients // 2
    node_covs = (by_node[:count], by_node[count:])
    arrived, far, node_covs = together((arrived, far, node_covs))
    rhs = jnp.sum(arrived, axis=0) * (1.0 / math.sqrt(rows * blocks))
    halves = lax.all_gather(rhs, "col", axis_index_groups=pairs)

    message = jax.ShapeDtypeStruct((blocks, tall, LANES), F32)
    vector = jax.ShapeDtypeStruct((tall, LANES), F32)
    fetched = [pltpu.VMEM((rows, half), BF16), pltpu.SemaphoreType.DMA((PARTS,))]
    scratch = [pltpu.VMEM((16, inducing), F32), pltpu.VMEM((tall, LANES), F32)] + fetched
    work = cost(64 * rows * inducing, 2 * rows * inducing)

    sent, before, rhs = pl.pallas_call(
        functools.partial(first_kernel, scale),
        in_specs=[SMEM, VMEM, HBM, VMEM, VMEM],
        out_specs=[VMEM] * 3,
        out_shape=[message, jax.ShapeDtypeStruct((1, rows), F32), vector],
        scratch_shapes=scratch,
        compiler_params=params(),
        cost_estimate=work,
        name="first_product",
    )(core, halves, near, far, weight)
    sent, node_cov_now = together((sent, node_covs[0]))
    arrived = lax.all_to_all(sent, "blk", 0, 0, tiled=True)
    node_first = features(core, node_cov_now, freq, (0, 1), "node_features_a")
    arrived, node_first = together((arrived, node_first))

    sent, fit, solution, residual, direction = pl.pallas_call(
        functools.partial(second_kernel, scale),
        in_specs=[VMEM, VMEM, VMEM, HBM, VMEM, VMEM],
        out_specs=[VMEM] * 5,
        out_shape=[message, jax.ShapeDtypeStruct((2, rows), F32), vector, vector, vector],
        scratch_shapes=scratch,
        compiler_params=params(),
        cost_estimate=work,
        name="second_product",
    )(arrived, rhs, before, near, far, weight)
    sent, node_cov_now = together((sent, node_covs[1]))
    arrived = lax.all_to_all(sent, "blk", 0, 0, tiled=True)
    node_second = features(core, node_cov_now, freq, (0, 1), "node_features_b")
    arrived, node_second = together((arrived, node_second))

    sent, both, norm = pl.pallas_call(
        functools.partial(third_kernel, scale, fit_scale),
        in_specs=[VMEM] * 5 + [HBM] + [VMEM] * 5,
        out_specs=[VMEM] * 3,
        out_shape=[
            jax.ShapeDtypeStruct((blocks, 4, patients), F32),
            jax.ShapeDtypeStruct((2, tall, LANES), F32),
            jax.ShapeDtypeStruct((8, LANES), F32),
        ],
        scratch_shapes=fetched,
        compiler_params=params(),
        cost_estimate=work,
        name="third_product",
    )(arrived, solution, residual, direction, fit, near, far, weight, size, owner, patient)
    sent, both = together((sent, both))
    arrived = lax.all_to_all(sent, "blk", 0, 0, tiled=True)
    node_values = pl.pallas_call(
        nodes_kernel,
        in_specs=[VMEM] * 3,
        out_specs=VMEM,
        out_shape=jax.ShapeDtypeStruct((2, 2 * count), F32),
        compiler_params=params(),
        cost_estimate=cost(64 * 2 * count * inducing, 4 * count * inducing),
        name="node_values",
    )(both, node_first, node_second)
    arrived, node_values = together((arrived, node_values))

    loglik, weights = pl.pallas_call(
        functools.partial(last_kernel, fit_scale),
        in_specs=[SMEM] + [VMEM] * 6,
        out_specs=[VMEM, VMEM],
        out_shape=[
            jax.ShapeDtypeStruct((1, patients), F32),
            jax.ShapeDtypeStruct((1, own), F32),
        ],
        scratch_shapes=[pltpu.VMEM((tall, LANES), F32)],
        compiler_params=params(),
        name="last",
    )(
        layer,
        arrived,
        both,
        norm,
        node_values,
        event_time.reshape(1, patients),
        event_flag.reshape(1, patients),
    )
    return loglik.reshape(patients), weights.reshape(own)


def solution(mesh):
    in_specs = (
        P("blk", None),
        P("blk"),
        P("blk"),
        P("blk", None),
        P("blk"),
        P(None, "col"),
        P("col"),
        P("blk", None, None),
        P("blk"),
        P("blk"),
    )
    out_specs = (P("blk"), P("col"))
    return jax.shard_map(
        on_device, mesh=mesh, in_specs=in_specs, out_specs=out_specs, check_vma=False
    )
```

```python
import functools
import math

import jax
import jax.numpy as jnp
import numpy as np
from jax import lax
from jax.experimental import pallas as pl
from jax.experimental.pallas import tpu as pltpu
from jax.sharding import PartitionSpec as P

F32 = jnp.float32
BF16 = jnp.bfloat16
LOG_SHAPE = math.log(1.5)
LINK = 0.4
LANES = 128
MIB = 1024 * 1024


def cosine_table():
    nodes = 0.125 + 0.125 * np.cos(np.pi * (np.arange(400) + 0.5) / 400)
    values = math.sqrt(2.0) * np.cos(2.0 * np.pi * np.sqrt(nodes))
    fit = np.polynomial.chebyshev.Chebyshev.fit(nodes, values, 5, domain=[0.0, 0.25])
    return [float(c) for c in fit.convert(kind=np.polynomial.Polynomial).coef]


COEFS = cosine_table()
PER_TURN = 1.0 / (2.0 * math.pi)


def feature(angles):
    turns = angles * PER_TURN
    turns = turns - jnp.round(turns)
    square = turns * turns
    total = COEFS[-1]
    for coef in COEFS[-2::-1]:
        total = total * square + coef
    return total.astype(BF16)


def split3(value):
    high = value.astype(BF16).astype(F32)
    rest = value - high
    middle = rest.astype(BF16).astype(F32)
    low = (rest - middle).astype(BF16).astype(F32)
    return high, middle, low


def stack_rows(rows, height):
    at = lax.broadcasted_iota(jnp.int32, (height, rows[0].shape[1]), 0)
    total = jnp.zeros((height, rows[0].shape[1]), F32)
    for index, row in enumerate(rows):
        total = jnp.where(at == index, row, total)
    return total.astype(BF16)


def as_row(tiles):
    return jnp.concatenate([tiles[j : j + 1, :] for j in range(tiles.shape[0])], axis=1)


def dot_nt(a, b):
    return lax.dot_general(a, b, (((1,), (1,)), ((), ())), preferred_element_type=F32)


def dot_nn(a, b):
    return jnp.dot(a, b, preferred_element_type=F32)


VMEM = pl.BlockSpec(memory_space=pltpu.VMEM)
SMEM = pl.BlockSpec(memory_space=pltpu.SMEM)
HBM = pl.BlockSpec(memory_space=pltpu.HBM)
PARTS = 2
KEPT = 0.25
SPARE = 9
PHASE_ROWS = 8


def rows_at(index, size):
    return pl.ds(pl.multiple_of(index * size, size), size)


def total_of(x):
    return jnp.sum(jnp.sum(x, axis=0, keepdims=True), axis=1, keepdims=True)


def params(mebibytes=48):
    return pltpu.CompilerParams(vmem_limit_bytes=mebibytes * MIB)


def cost(flops, size, hard=0):
    return pl.CostEstimate(flops=flops, bytes_accessed=size, transcendentals=hard)


def pack_kernel(freq, phase, out, packed, row, sems):
    depth = freq.shape[0]
    loads = [
        pltpu.make_async_copy(freq, packed.at[0:depth], sems.at[0]),
        pltpu.make_async_copy(phase, row, sems.at[1]),
    ]
    for load in loads:
        load.start()
    for load in loads:
        load.wait()
    packed[depth : depth + PHASE_ROWS, :] = jnp.broadcast_to(
        row[...], (PHASE_ROWS, row.shape[1])
    )
    stores = [
        pltpu.make_async_copy(packed, out.at[copy], sems.at[2 + copy])
        for copy in range(out.shape[0])
    ]
    for store in stores:
        store.start()
    for store in stores:
        store.wait()


def stage_kernel(value, out):
    out[...] = value[...]


def stage(value, name):
    return pl.pallas_call(
        stage_kernel,
        in_specs=[VMEM],
        out_specs=VMEM,
        out_shape=jax.ShapeDtypeStruct(value.shape, value.dtype),
        compiler_params=params(),
        cost_estimate=cost(value.size, 4 * value.size),
        name=name,
    )(value)


def feature_block(rows, freq, store):
    depth = rows.shape[1]
    for j in range(0, freq.shape[0], 2):
        both = jnp.concatenate([freq[j, :depth, :], freq[j + 1, :depth, :]], axis=1)
        phase = jnp.concatenate(
            [freq[j, depth : depth + 1, :], freq[j + 1, depth : depth + 1, :]], axis=1
        )
        store(j * LANES, feature(dot_nn(rows, both) + phase.astype(F32)))


FEATURE_ROWS = 256


def half_features(cov, freq, target, base):
    def step(i, carry):
        at = rows_at(i, FEATURE_ROWS)

        def store(column, value):
            target[at, base + column : base + column + value.shape[1]] = value

        feature_block(cov[at, :], freq, store)
        return carry

    lax.fori_loop(0, cov.shape[0] // FEATURE_ROWS, step, 0)


def far_kernel(core, cov, freq, out):
    half_features(cov, freq.at[1 - core[0]], out, 0)


def far_features(core, cov, freq):
    rows, depth = cov.shape
    columns = freq.shape[1] * LANES
    return pl.pallas_call(
        far_kernel,
        in_specs=[SMEM, VMEM, VMEM],
        out_specs=VMEM,
        out_shape=jax.ShapeDtypeStruct((rows, columns), BF16),
        compiler_params=params(),
        cost_estimate=cost(2 * rows * depth * columns + 20 * rows * columns, 2 * rows * columns),
        name="far_features",
    )(core, cov, freq)


def node_kernel(first, core, cov, freq, *rest):
    out, held, sems = rest[-3:]
    half = freq.shape[1] * LANES
    steps = cov.shape[0] // FEATURE_ROWS

    def leave(i):
        at, to = rows_at(i, FEATURE_ROWS), rows_at(i + first // FEATURE_ROWS, FEATURE_ROWS)
        return pltpu.make_async_copy(held.at[at], out.at[to], sems.at[i])

    def step(i, carry):
        at = rows_at(i, FEATURE_ROWS)
        for index in range(2):
            source = core[0] if index == 0 else 1 - core[0]

            def store(column, value, base=index * half):
                held[at, base + column : base + column + value.shape[1]] = value

            feature_block(cov[at, :], freq.at[source], store)
        leave(i).start()
        return carry

    lax.fori_loop(0, steps, step, 0)
    for i in range(steps):
        leave(i).wait()


def node_features(core, cov, freq, before, first, height, name):
    rows, depth = cov.shape
    columns = 2 * freq.shape[1] * LANES
    earlier = () if before is None else (before,)
    return pl.pallas_call(
        functools.partial(node_kernel, first),
        in_specs=[SMEM, VMEM, VMEM] + [HBM] * len(earlier),
        out_specs=HBM,
        out_shape=jax.ShapeDtypeStruct((height, columns), BF16),
        scratch_shapes=[
            pltpu.VMEM((rows, columns), BF16),
            pltpu.SemaphoreType.DMA((rows // FEATURE_ROWS,)),
        ],
        input_output_aliases={3: 0} if earlier else {},
        compiler_params=params(),
        cost_estimate=cost(2 * rows * depth * columns + 20 * rows * columns, 2 * rows * columns),
        name=name,
    )(core, cov, freq, *earlier)


def near_kernel(
    core, cov, freq, weight, size, kept, rest_out, out, rest, gathered, tiles, sems
):
    first = kept.shape[0]

    def fill(target, base, count, after=None):
        group = target.shape[0] // count

        def step(i, carry):
            at = rows_at(i, group)

            def store(column, value):
                target[at, column : column + value.shape[1]] = value

            rows = cov[pl.ds(pl.multiple_of(base + i * group, 64), group), :]
            feature_block(rows, freq.at[core[0]], store)
            if after is not None:
                after(i, group).start()
            return carry

        lax.fori_loop(0, count, step, 0)

    def leave(i, group):
        at = rows_at(i, group)
        return pltpu.make_async_copy(rest.at[at], rest_out.at[at], sems.at[i])

    fill(rest, first, PARTS, leave)
    fill(kept, 0, PARTS)
    product = weight[...].astype(F32) * size[...].astype(F32)
    split = stack_rows(split3(product), 16)
    gathered[...] = dot_nn(split[:, :first], kept[...]) + dot_nn(split[:, first:], rest[...])
    send_whole(gathered, tiles, out)
    for i in range(PARTS):
        leave(i, rest.shape[0] // PARTS).wait()


def rows_of(vector):
    return stack_rows(split3(as_row(vector)), 16)


def send_whole(gathered, tiles, out):
    total = jnp.sum(gathered[...], axis=0, keepdims=True)
    for j in range(tiles.shape[0]):
        tiles[j : j + 1, :] = total[:, j * LANES : (j + 1) * LANES]
    whole = tiles[...]
    for copy in range(out.shape[0]):
        out[copy] = whole


def fetch(rest, held, sems):
    part = held.shape[0] // PARTS
    copies = []
    for k in range(PARTS):
        at = slice(k * part, (k + 1) * part)
        copy = pltpu.make_async_copy(rest.at[at], held.at[at], sems.at[k])
        copy.start()
        copies.append((at, copy))
    return copies


def forward(direction, kept, held, copies, far):
    split = rows_of(direction)
    half = far.shape[1]
    near = split[:, :half]
    total = jnp.sum(dot_nt(split[:, half:], far[...]), axis=0, keepdims=True)
    values = [jnp.sum(dot_nt(near, kept[...]), axis=0, keepdims=True)]
    for at, copy in copies:
        copy.wait()
        values.append(jnp.sum(dot_nt(near, held[at]), axis=0, keepdims=True))
    return jnp.concatenate(values, axis=1) + total


def product(direction, kept, held, copies, far, weight, gathered, tiles, out, scale):
    values = forward(direction, kept, held, copies, far)
    split = stack_rows(split3(weight[...].astype(F32) * values * scale), 16)
    half, first = far.shape[1], kept.shape[0]
    gathered[:, half:] = dot_nn(split, far[...])
    gathered[:, :half] = dot_nn(split[:, :first], kept[...]) + dot_nn(split[:, first:], held[...])
    send_whole(gathered, tiles, out)
    return values


def first_kernel(
    scale, core, halves, kept, rest, far, weight, out, values_out, rhs_out, gathered, tiles, held, sems
):
    copies = fetch(rest, held, sems)
    low, high = halves[0], halves[1]
    swap = core[0] == 1
    half = low.shape[0]
    rhs_out[0:half, :] = jnp.where(swap, high, low)
    rhs_out[half : 2 * half, :] = jnp.where(swap, low, high)
    values_out[...] = product(
        rhs_out[...], kept, held, copies, far, weight, gathered, tiles, out, scale
    )


def second_kernel(
    scale, arrived, rhs, before, kept, rest, far, weight,
    out, fit_out, solution_out, residual_out, direction_out,
    gathered, tiles, held, sems,
):
    copies = fetch(rest, held, sems)
    direction = rhs[...]
    norm = total_of(direction * direction)
    image = direction + jnp.sum(arrived[...], axis=0)
    length = norm / total_of(direction * image)
    residual = direction - length * image
    later = residual + total_of(residual * residual) / norm * direction
    solution_out[...] = length * direction
    residual_out[...] = residual
    direction_out[...] = later
    fit_out[0:1, :] = length * before[...]
    fit_out[1:2, :] = product(
        later, kept, held, copies, far, weight, gathered, tiles, out, scale
    )


def third_kernel(
    scale, fit_scale, arrived, solution, residual, direction, fit, kept, rest, far, weight, size, owner, patient,
    out, both_out, norm_out,
    held, sems,
):
    copies = fetch(rest, held, sems)
    before = direction[...]
    left = residual[...]
    norm = total_of(left * left)
    image = before + jnp.sum(arrived[...], axis=0)
    length = norm / total_of(before * image)
    left = left - length * image
    norm_next = total_of(left * left)
    later = left + norm_next / norm * before
    both_out[0] = solution[...] + length * before
    both_out[1] = later
    norm_out[...] = jnp.broadcast_to(norm_next, norm_out.shape)
    values = forward(later, kept, held, copies, far)
    fitted = fit[0:1, :] + length * fit[1:2, :]
    weights = weight[...].astype(F32)
    weighted = weights * values
    energy = total_of(weighted * values) * scale
    part = weights * (size[...].astype(F32) - fitted * fit_scale)
    owners, patients = out.shape[0], out.shape[2]
    here = values.shape[1]
    to_owner = (owner[...] == lax.broadcasted_iota(jnp.int32, (owners, here), 0)).astype(F32)
    to_patient = (patient[...] == lax.broadcasted_iota(jnp.int32, (patients, here), 0)).astype(F32)
    parts = split3(part) + split3(weighted * fit_scale) + (weights,)
    tall = jnp.concatenate([to_owner * part for part in parts], axis=0).astype(BF16)
    sums = dot_nt(tall, to_patient.astype(BF16))
    part = [sums[i * owners : (i + 1) * owners, :] for i in range(len(parts))]
    out[:, 0, :] = part[0] + part[1] + part[2]
    out[:, 1, :] = part[3] + part[4] + part[5]
    out[:, 2, :] = part[6]
    out[:, 3, :] = jnp.broadcast_to(energy, (owners, patients))


NODE_ROWS = 512


def nodes_kernel(both, phi, out, split):
    @pl.when(pl.program_id(0) == 0)
    def _():
        rows = split3(as_row(both[0])) + split3(as_row(both[1]))
        split[...] = stack_rows(rows, 16)

    products = dot_nt(split[...], phi[...])
    out[0:1, :] = products[0:1] + products[1:2] + products[2:3]
    out[1:2, :] = products[3:4] + products[4:5] + products[5:6]


def last_kernel(fit_scale, mine, arrived, both, norm, node_values, time, flag, loglik, weights_out, tiles):
    sums = jnp.sum(arrived[...], axis=0)
    direction = both[1]
    denominator = total_of(direction * direction) + sums[3:4, 0:1]
    length = norm[0:1, 0:1] / denominator
    tiles[...] = both[0] + length * direction
    weights_out[...] = tiles[pl.ds(mine[0], 1), :]
    effect = (sums[0:1, :] - length * sums[1:2, :]) / (1.0 + sums[2:3, :])
    values = (node_values[0:1, :] + length * node_values[1:2, :]) * fit_scale
    patients = loglik.shape[1]
    nodes = values.shape[1] // patients
    total = jnp.zeros_like(effect)
    eta = total
    when = time[...]
    for q in range(nodes):
        grid = when * (q + 1.0) / nodes
        eta = (
            LOG_SHAPE
            + 0.5 * jnp.log(grid)
            + LINK * (values[:, q * patients : (q + 1) * patients] + effect)
        )
        total = total + jnp.exp(eta)
    loglik[...] = flag[...].astype(F32) * eta - when / nodes * total


def on_device(
    visit_cov,
    tumor_size,
    visit_weight,
    visit_owner,
    visit_patient,
    inducing_freq,
    inducing_phase,
    node_cov,
    event_time,
    event_flag,
):
    blocks, cols = lax.axis_size("blk"), lax.axis_size("col")
    rows, depth = visit_cov.shape
    own = inducing_freq.shape[1]
    inducing = own * cols
    tall = inducing // LANES
    layers = cols // 2
    patients, nodes = node_cov.shape[:2]
    scale = 1.0 / (rows * blocks)
    fit_scale = 1.0 / math.sqrt(inducing)
    weight = visit_weight.reshape(1, rows)
    size = tumor_size.reshape(1, rows)
    owner = visit_owner.reshape(1, rows)
    patient = visit_patient.reshape(1, rows)
    place = lax.axis_index("col").astype(jnp.int32)
    core = (place % 2).reshape(1)
    layer = (place // 2).reshape(1)
    together = lax.optimization_barrier
    same_core = [[2 * z + c for z in range(layers)] for c in range(2)]
    pairs = [[2 * z, 2 * z + 1] for z in range(layers)]

    packed = pl.pallas_call(
        pack_kernel,
        in_specs=[HBM, HBM],
        out_specs=HBM,
        out_shape=jax.ShapeDtypeStruct((layers, depth + PHASE_ROWS, own), BF16),
        scratch_shapes=[
            pltpu.VMEM((depth + PHASE_ROWS, own), BF16),
            pltpu.VMEM((1, own), BF16),
            pltpu.SemaphoreType.DMA((2 + layers,)),
        ],
        compiler_params=params(60),
        name="pack",
    )(inducing_freq, inducing_phase.reshape(1, own))
    packed, cov, turned = together((packed, visit_cov, node_cov))
    near_freq = lax.all_to_all(packed, "col", 0, 0, tiled=True, axis_index_groups=same_core)
    cov = stage(cov, "stage_cov")
    by_node = turned.transpose(1, 0, 2).reshape(nodes * patients, depth)
    count = nodes * patients // 2
    height = (SPARE * nodes * patients) // 4
    node_covs = (by_node[:count], by_node[count:])
    near_freq, cov, node_covs = together((near_freq, cov, node_covs))
    freq = lax.all_gather(near_freq, "col", axis_index_groups=pairs)

    half = inducing // 2
    first = int(rows * KEPT)
    kept, rest, sent = pl.pallas_call(
        near_kernel,
        in_specs=[SMEM] + [VMEM] * 4,
        out_specs=[VMEM, HBM, VMEM],
        out_shape=[
            jax.ShapeDtypeStruct((first, half), BF16),
            jax.ShapeDtypeStruct((SPARE * rows, half), BF16),
            jax.ShapeDtypeStruct((blocks, tall // 2, LANES), F32),
        ],
        scratch_shapes=[
            pltpu.VMEM((rows - first, half), BF16),
            pltpu.VMEM((16, half), F32),
            pltpu.VMEM((tall // 2, LANES), F32),
            pltpu.SemaphoreType.DMA((PARTS,)),
        ],
        compiler_params=params(),
        name="near_features",
    )(core, cov, freq, weight, size)
    sent, late_freq = together((sent, freq))
    arrived = lax.all_to_all(sent, "blk", 0, 0, tiled=True)
    far = far_features(core, cov, late_freq)
    arrived, far = together((arrived, far))
    rhs = jnp.sum(arrived, axis=0) * (1.0 / math.sqrt(rows * blocks))
    halves = lax.all_gather(rhs, "col", axis_index_groups=pairs)

    message = jax.ShapeDtypeStruct((blocks, tall, LANES), F32)
    vector = jax.ShapeDtypeStruct((tall, LANES), F32)
    fetched = [pltpu.VMEM((rows - first, half), BF16), pltpu.SemaphoreType.DMA((PARTS,))]
    scratch = [pltpu.VMEM((16, inducing), F32), pltpu.VMEM((tall, LANES), F32)] + fetched
    work = cost(64 * rows * inducing, 2 * rows * inducing)

    sent, before, rhs = pl.pallas_call(
        functools.partial(first_kernel, scale),
        in_specs=[SMEM, VMEM, VMEM, HBM, VMEM, VMEM],
        out_specs=[VMEM] * 3,
        out_shape=[message, jax.ShapeDtypeStruct((1, rows), F32), vector],
        scratch_shapes=scratch,
        compiler_params=params(),
        cost_estimate=work,
        name="first_product",
    )(core, halves, kept, rest, far, weight)
    sent, node_cov_now = together((sent, node_covs[0]))
    arrived = lax.all_to_all(sent, "blk", 0, 0, tiled=True)
    node_phi = node_features(core, node_cov_now, freq, None, 0, height, "node_features_a")
    arrived, node_phi = together((arrived, node_phi))

    sent, fit, solution, residual, direction = pl.pallas_call(
        functools.partial(second_kernel, scale),
        in_specs=[VMEM] * 4 + [HBM, VMEM, VMEM],
        out_specs=[VMEM] * 5,
        out_shape=[message, jax.ShapeDtypeStruct((2, rows), F32), vector, vector, vector],
        scratch_shapes=scratch,
        compiler_params=params(),
        cost_estimate=work,
        name="second_product",
    )(arrived, rhs, before, kept, rest, far, weight)
    sent, node_cov_now = together((sent, node_covs[1]))
    arrived = lax.all_to_all(sent, "blk", 0, 0, tiled=True)
    node_phi = node_features(core, node_cov_now, freq, node_phi, count, height, "node_features_b")
    arrived, node_phi = together((arrived, node_phi))

    sent, both, norm = pl.pallas_call(
        functools.partial(third_kernel, scale, fit_scale),
        in_specs=[VMEM] * 6 + [HBM] + [VMEM] * 5,
        out_specs=[VMEM] * 3,
        out_shape=[
            jax.ShapeDtypeStruct((blocks, 4, patients), F32),
            jax.ShapeDtypeStruct((2, tall, LANES), F32),
            jax.ShapeDtypeStruct((8, LANES), F32),
        ],
        scratch_shapes=fetched,
        compiler_params=params(),
        cost_estimate=work,
        name="third_product",
    )(arrived, solution, residual, direction, fit, kept, rest, far, weight, size, owner, patient)
    sent, both = together((sent, both))
    arrived = lax.all_to_all(sent, "blk", 0, 0, tiled=True)
    node_values = pl.pallas_call(
        nodes_kernel,
        grid=(2 * count // NODE_ROWS,),
        in_specs=[
            pl.BlockSpec(both.shape, lambda i: (0, 0, 0)),
            pl.BlockSpec((NODE_ROWS, inducing), lambda i: (i, 0)),
        ],
        out_specs=pl.BlockSpec((2, NODE_ROWS), lambda i: (0, i)),
        out_shape=jax.ShapeDtypeStruct((2, 2 * count), F32),
        scratch_shapes=[pltpu.VMEM((16, inducing), BF16)],
        compiler_params=params(),
        cost_estimate=cost(64 * 2 * count * inducing, 4 * count * inducing),
        name="node_values",
    )(both, node_phi)
    arrived, node_values = together((arrived, node_values))

    loglik, weights = pl.pallas_call(
        functools.partial(last_kernel, fit_scale),
        in_specs=[SMEM] + [VMEM] * 6,
        out_specs=[VMEM, VMEM],
        out_shape=[
            jax.ShapeDtypeStruct((1, patients), F32),
            jax.ShapeDtypeStruct((1, own), F32),
        ],
        scratch_shapes=[pltpu.VMEM((tall, LANES), F32)],
        compiler_params=params(),
        name="last",
    )(
        layer,
        arrived,
        both,
        norm,
        node_values,
        event_time.reshape(1, patients),
        event_flag.reshape(1, patients),
    )
    return loglik.reshape(patients), weights.reshape(own)


def solution(mesh):
    in_specs = (
        P("blk", None),
        P("blk"),
        P("blk"),
        P("blk", None),
        P("blk"),
        P(None, "col"),
        P("col"),
        P("blk", None, None),
        P("blk"),
        P("blk"),
    )
    out_specs = (P("blk"), P("col"))
    return jax.shard_map(
        on_device, mesh=mesh, in_specs=in_specs, out_specs=out_specs, check_vma=False
    )
```

```python
import functools
import math

import jax
import jax.numpy as jnp
import numpy as np
from jax import lax
from jax.experimental import pallas as pl
from jax.experimental.pallas import tpu as pltpu
from jax.sharding import PartitionSpec as P

F32 = jnp.float32
BF16 = jnp.bfloat16
LOG_SHAPE = math.log(1.5)
LINK = 0.4
LANES = 128
MIB = 1024 * 1024


def cosine_table():
    nodes = 0.125 + 0.125 * np.cos(np.pi * (np.arange(400) + 0.5) / 400)
    values = math.sqrt(2.0) * np.cos(2.0 * np.pi * np.sqrt(nodes))
    fit = np.polynomial.chebyshev.Chebyshev.fit(nodes, values, 5, domain=[0.0, 0.25])
    return [float(c) for c in fit.convert(kind=np.polynomial.Polynomial).coef]


COEFS = cosine_table()
PER_TURN = 1.0 / (2.0 * math.pi)


def feature(angles):
    turns = angles * PER_TURN
    turns = turns - jnp.round(turns)
    square = turns * turns
    total = COEFS[-1]
    for coef in COEFS[-2::-1]:
        total = total * square + coef
    return total.astype(BF16)


def split3(value):
    high = value.astype(BF16).astype(F32)
    rest = value - high
    middle = rest.astype(BF16).astype(F32)
    low = (rest - middle).astype(BF16).astype(F32)
    return high, middle, low


def stack_rows(rows, height):
    at = lax.broadcasted_iota(jnp.int32, (height, rows[0].shape[1]), 0)
    total = jnp.zeros((height, rows[0].shape[1]), F32)
    for index, row in enumerate(rows):
        total = jnp.where(at == index, row, total)
    return total.astype(BF16)


def as_row(tiles):
    return jnp.concatenate([tiles[j : j + 1, :] for j in range(tiles.shape[0])], axis=1)


def dot_nt(a, b):
    return lax.dot_general(a, b, (((1,), (1,)), ((), ())), preferred_element_type=F32)


def dot_nn(a, b):
    return jnp.dot(a, b, preferred_element_type=F32)


VMEM = pl.BlockSpec(memory_space=pltpu.VMEM)
SMEM = pl.BlockSpec(memory_space=pltpu.SMEM)
HBM = pl.BlockSpec(memory_space=pltpu.HBM)
PARTS = 2
KEPT = 0.5
SPARE = 9
PHASE_ROWS = 8


def rows_at(index, size):
    return pl.ds(pl.multiple_of(index * size, size), size)


def total_of(x):
    return jnp.sum(jnp.sum(x, axis=0, keepdims=True), axis=1, keepdims=True)


def params(mebibytes=48):
    return pltpu.CompilerParams(vmem_limit_bytes=mebibytes * MIB)


def cost(flops, size, hard=0):
    return pl.CostEstimate(flops=flops, bytes_accessed=size, transcendentals=hard)


def pack_kernel(freq, phase, out, packed, row, sems):
    depth = freq.shape[0]
    loads = [
        pltpu.make_async_copy(freq, packed.at[0:depth], sems.at[0]),
        pltpu.make_async_copy(phase, row, sems.at[1]),
    ]
    for load in loads:
        load.start()
    for load in loads:
        load.wait()
    packed[depth : depth + PHASE_ROWS, :] = jnp.broadcast_to(
        row[...], (PHASE_ROWS, row.shape[1])
    )
    stores = [
        pltpu.make_async_copy(packed, out.at[copy], sems.at[2 + copy])
        for copy in range(out.shape[0])
    ]
    for store in stores:
        store.start()
    for store in stores:
        store.wait()


def stage_kernel(value, out):
    out[...] = value[...]


def stage(value, name):
    return pl.pallas_call(
        stage_kernel,
        in_specs=[VMEM],
        out_specs=VMEM,
        out_shape=jax.ShapeDtypeStruct(value.shape, value.dtype),
        compiler_params=params(),
        cost_estimate=cost(value.size, 4 * value.size),
        name=name,
    )(value)


def feature_block(rows, freq, store):
    depth = rows.shape[1]
    for j in range(0, freq.shape[0], 2):
        both = jnp.concatenate([freq[j, :depth, :], freq[j + 1, :depth, :]], axis=1)
        phase = jnp.concatenate(
            [freq[j, depth : depth + 1, :], freq[j + 1, depth : depth + 1, :]], axis=1
        )
        store(j * LANES, feature(dot_nn(rows, both) + phase.astype(F32)))


FEATURE_ROWS = 256


def half_features(cov, freq, target, base):
    def step(i, carry):
        at = rows_at(i, FEATURE_ROWS)

        def store(column, value):
            target[at, base + column : base + column + value.shape[1]] = value

        feature_block(cov[at, :], freq, store)
        return carry

    lax.fori_loop(0, cov.shape[0] // FEATURE_ROWS, step, 0)


def far_kernel(core, cov, freq, out):
    half_features(cov, freq.at[1 - core[0]], out, 0)


def far_features(core, cov, freq):
    rows, depth = cov.shape
    columns = freq.shape[1] * LANES
    return pl.pallas_call(
        far_kernel,
        in_specs=[SMEM, VMEM, VMEM],
        out_specs=VMEM,
        out_shape=jax.ShapeDtypeStruct((rows, columns), BF16),
        compiler_params=params(),
        cost_estimate=cost(2 * rows * depth * columns + 20 * rows * columns, 2 * rows * columns),
        name="far_features",
    )(core, cov, freq)


def node_kernel(first, core, cov, freq, *rest):
    out, held, sems = rest[-3:]
    half = freq.shape[1] * LANES
    steps = cov.shape[0] // FEATURE_ROWS

    def leave(i):
        at, to = rows_at(i, FEATURE_ROWS), rows_at(i + first // FEATURE_ROWS, FEATURE_ROWS)
        return pltpu.make_async_copy(held.at[at], out.at[to], sems.at[i])

    def step(i, carry):
        at = rows_at(i, FEATURE_ROWS)
        for index in range(2):
            source = core[0] if index == 0 else 1 - core[0]

            def store(column, value, base=index * half):
                held[at, base + column : base + column + value.shape[1]] = value

            feature_block(cov[at, :], freq.at[source], store)
        leave(i).start()
        return carry

    lax.fori_loop(0, steps, step, 0)
    for i in range(steps):
        leave(i).wait()


def node_features(core, cov, freq, before, first, height, name):
    rows, depth = cov.shape
    columns = 2 * freq.shape[1] * LANES
    earlier = () if before is None else (before,)
    return pl.pallas_call(
        functools.partial(node_kernel, first),
        in_specs=[SMEM, VMEM, VMEM] + [HBM] * len(earlier),
        out_specs=HBM,
        out_shape=jax.ShapeDtypeStruct((height, columns), BF16),
        scratch_shapes=[
            pltpu.VMEM((rows, columns), BF16),
            pltpu.SemaphoreType.DMA((rows // FEATURE_ROWS,)),
        ],
        input_output_aliases={3: 0} if earlier else {},
        compiler_params=params(),
        cost_estimate=cost(2 * rows * depth * columns + 20 * rows * columns, 2 * rows * columns),
        name=name,
    )(core, cov, freq, *earlier)


def near_kernel(
    cov, freq, weight, size, kept, rest_out, out, rest, gathered, tiles, sems
):
    first = kept.shape[0]

    def fill(target, base, count, after=None):
        group = target.shape[0] // count

        def step(i, carry):
            at = rows_at(i, group)

            def store(column, value):
                target[at, column : column + value.shape[1]] = value

            rows = cov[pl.ds(pl.multiple_of(base + i * group, 64), group), :]
            feature_block(rows, freq, store)
            if after is not None:
                after(i, group).start()
            return carry

        lax.fori_loop(0, count, step, 0)

    def leave(i, group):
        at = rows_at(i, group)
        return pltpu.make_async_copy(rest.at[at], rest_out.at[at], sems.at[i])

    fill(rest, first, PARTS, leave)
    fill(kept, 0, PARTS)
    product = weight[...].astype(F32) * size[...].astype(F32)
    split = stack_rows(split3(product), 16)
    gathered[...] = dot_nn(split[:, :first], kept[...]) + dot_nn(split[:, first:], rest[...])
    send_whole(gathered, tiles, out)
    for i in range(PARTS):
        leave(i, rest.shape[0] // PARTS).wait()


def rows_of(vector):
    return stack_rows(split3(as_row(vector)), 16)


def send_whole(gathered, tiles, out):
    total = jnp.sum(gathered[...], axis=0, keepdims=True)
    for j in range(tiles.shape[0]):
        tiles[j : j + 1, :] = total[:, j * LANES : (j + 1) * LANES]
    whole = tiles[...]
    for copy in range(out.shape[0]):
        out[copy] = whole


def fetch(rest, held, sems):
    part = held.shape[0] // PARTS
    copies = []
    for k in range(PARTS):
        at = slice(k * part, (k + 1) * part)
        copy = pltpu.make_async_copy(rest.at[at], held.at[at], sems.at[k])
        copy.start()
        copies.append((at, copy))
    return copies


def forward(direction, kept, held, copies, far):
    split = rows_of(direction)
    half = far.shape[1]
    near = split[:, :half]
    total = jnp.sum(dot_nt(split[:, half:], far[...]), axis=0, keepdims=True)
    values = [jnp.sum(dot_nt(near, kept[...]), axis=0, keepdims=True)]
    for at, copy in copies:
        copy.wait()
        values.append(jnp.sum(dot_nt(near, held[at]), axis=0, keepdims=True))
    return jnp.concatenate(values, axis=1) + total


def product(direction, kept, held, copies, far, weight, gathered, tiles, out, scale):
    values = forward(direction, kept, held, copies, far)
    split = stack_rows(split3(weight[...].astype(F32) * values * scale), 16)
    half, first = far.shape[1], kept.shape[0]
    gathered[:, half:] = dot_nn(split, far[...])
    gathered[:, :half] = dot_nn(split[:, :first], kept[...]) + dot_nn(split[:, first:], held[...])
    send_whole(gathered, tiles, out)
    return values


def first_kernel(
    scale, rhs_scale, core, halves, kept, rest, far, weight, out, values_out, rhs_out, gathered, tiles, held, sems
):
    copies = fetch(rest, held, sems)
    low, high = (jnp.sum(halves[h], axis=0) * rhs_scale for h in range(2))
    swap = core[0] == 1
    half = low.shape[0]
    rhs_out[0:half, :] = jnp.where(swap, high, low)
    rhs_out[half : 2 * half, :] = jnp.where(swap, low, high)
    values_out[...] = product(
        rhs_out[...], kept, held, copies, far, weight, gathered, tiles, out, scale
    )


def second_kernel(
    scale, arrived, rhs, before, kept, rest, far, weight,
    out, fit_out, solution_out, residual_out, direction_out,
    gathered, tiles, held, sems,
):
    copies = fetch(rest, held, sems)
    direction = rhs[...]
    norm = total_of(direction * direction)
    image = direction + jnp.sum(arrived[...], axis=0)
    length = norm / total_of(direction * image)
    residual = direction - length * image
    later = residual + total_of(residual * residual) / norm * direction
    solution_out[...] = length * direction
    residual_out[...] = residual
    direction_out[...] = later
    fit_out[0:1, :] = length * before[...]
    fit_out[1:2, :] = product(
        later, kept, held, copies, far, weight, gathered, tiles, out, scale
    )


def third_kernel(
    scale, fit_scale, arrived, solution, residual, direction, fit, kept, rest, far, weight, size, owner, patient,
    out, both_out, norm_out,
    held, sems,
):
    copies = fetch(rest, held, sems)
    before = direction[...]
    left = residual[...]
    norm = total_of(left * left)
    image = before + jnp.sum(arrived[...], axis=0)
    length = norm / total_of(before * image)
    left = left - length * image
    norm_next = total_of(left * left)
    later = left + norm_next / norm * before
    both_out[0] = solution[...] + length * before
    both_out[1] = later
    norm_out[...] = jnp.broadcast_to(norm_next, norm_out.shape)
    values = forward(later, kept, held, copies, far)
    fitted = fit[0:1, :] + length * fit[1:2, :]
    weights = weight[...].astype(F32)
    weighted = weights * values
    energy = total_of(weighted * values) * scale
    part = weights * (size[...].astype(F32) - fitted * fit_scale)
    owners, patients = out.shape[0], out.shape[2]
    here = values.shape[1]
    to_owner = (owner[...] == lax.broadcasted_iota(jnp.int32, (owners, here), 0)).astype(F32)
    to_patient = (patient[...] == lax.broadcasted_iota(jnp.int32, (patients, here), 0)).astype(F32)
    parts = split3(part) + split3(weighted * fit_scale) + (weights,)
    tall = jnp.concatenate([to_owner * part for part in parts], axis=0).astype(BF16)
    sums = dot_nt(tall, to_patient.astype(BF16))
    part = [sums[i * owners : (i + 1) * owners, :] for i in range(len(parts))]
    out[:, 0, :] = part[0] + part[1] + part[2]
    out[:, 1, :] = part[3] + part[4] + part[5]
    out[:, 2, :] = part[6]
    out[:, 3, :] = jnp.broadcast_to(energy, (owners, patients))


NODE_ROWS = 512


def nodes_kernel(both, phi, out, split):
    @pl.when(pl.program_id(0) == 0)
    def _():
        rows = split3(as_row(both[0])) + split3(as_row(both[1]))
        split[...] = stack_rows(rows, 16)

    products = dot_nt(split[...], phi[...])
    out[0:1, :] = products[0:1] + products[1:2] + products[2:3]
    out[1:2, :] = products[3:4] + products[4:5] + products[5:6]


def last_kernel(fit_scale, mine, arrived, both, norm, node_values, time, flag, loglik, weights_out, tiles):
    sums = jnp.sum(arrived[...], axis=0)
    direction = both[1]
    denominator = total_of(direction * direction) + sums[3:4, 0:1]
    length = norm[0:1, 0:1] / denominator
    tiles[...] = both[0] + length * direction
    weights_out[...] = tiles[pl.ds(mine[0], 1), :]
    effect = (sums[0:1, :] - length * sums[1:2, :]) / (1.0 + sums[2:3, :])
    values = (node_values[0:1, :] + length * node_values[1:2, :]) * fit_scale
    patients = loglik.shape[1]
    nodes = values.shape[1] // patients
    total = jnp.zeros_like(effect)
    eta = total
    when = time[...]
    for q in range(nodes):
        grid = when * (q + 1.0) / nodes
        eta = (
            LOG_SHAPE
            + 0.5 * jnp.log(grid)
            + LINK * (values[:, q * patients : (q + 1) * patients] + effect)
        )
        total = total + jnp.exp(eta)
    loglik[...] = flag[...].astype(F32) * eta - when / nodes * total


def on_device(
    visit_cov,
    tumor_size,
    visit_weight,
    visit_owner,
    visit_patient,
    inducing_freq,
    inducing_phase,
    node_cov,
    event_time,
    event_flag,
):
    blocks, cols = lax.axis_size("blk"), lax.axis_size("col")
    rows, depth = visit_cov.shape
    own = inducing_freq.shape[1]
    inducing = own * cols
    tall = inducing // LANES
    layers = cols // 2
    patients, nodes = node_cov.shape[:2]
    scale = 1.0 / (rows * blocks)
    fit_scale = 1.0 / math.sqrt(inducing)
    weight = visit_weight.reshape(1, rows)
    size = tumor_size.reshape(1, rows)
    owner = visit_owner.reshape(1, rows)
    patient = visit_patient.reshape(1, rows)
    place = lax.axis_index("col").astype(jnp.int32)
    core = (place % 2).reshape(1)
    layer = (place // 2).reshape(1)
    together = lax.optimization_barrier
    same_core = [[2 * z + c for z in range(layers)] for c in range(2)]
    pairs = [[2 * z, 2 * z + 1] for z in range(layers)]

    packed = pl.pallas_call(
        pack_kernel,
        in_specs=[HBM, HBM],
        out_specs=HBM,
        out_shape=jax.ShapeDtypeStruct((layers, depth + PHASE_ROWS, own), BF16),
        scratch_shapes=[
            pltpu.VMEM((depth + PHASE_ROWS, own), BF16),
            pltpu.VMEM((1, own), BF16),
            pltpu.SemaphoreType.DMA((2 + layers,)),
        ],
        compiler_params=params(60),
        name="pack",
    )(inducing_freq, inducing_phase.reshape(1, own))
    packed, cov, turned = together((packed, visit_cov, node_cov))
    near_freq = lax.all_to_all(packed, "col", 0, 0, tiled=True, axis_index_groups=same_core)
    cov = stage(cov, "stage_cov")
    by_node = turned.transpose(1, 0, 2).reshape(nodes * patients, depth)
    count = nodes * patients // 2
    height = (SPARE * nodes * patients) // 4
    node_covs = (by_node[:count], by_node[count:])
    near_freq, cov, node_covs = together((near_freq, cov, node_covs))

    half = inducing // 2
    first = int(rows * KEPT)
    kept, rest, sent = pl.pallas_call(
        near_kernel,
        in_specs=[VMEM] * 4,
        out_specs=[VMEM, HBM, VMEM],
        out_shape=[
            jax.ShapeDtypeStruct((first, half), BF16),
            jax.ShapeDtypeStruct((SPARE * rows, half), BF16),
            jax.ShapeDtypeStruct((blocks, tall // 2, LANES), F32),
        ],
        scratch_shapes=[
            pltpu.VMEM((rows - first, half), BF16),
            pltpu.VMEM((16, half), F32),
            pltpu.VMEM((tall // 2, LANES), F32),
            pltpu.SemaphoreType.DMA((PARTS,)),
        ],
        compiler_params=params(),
        name="near_features",
    )(cov, near_freq, weight, size)
    sent, late_freq = together((sent, near_freq))
    arrived = lax.all_to_all(sent, "blk", 0, 0, tiled=True)
    freq = lax.all_gather(late_freq, "col", axis_index_groups=pairs)
    far = far_features(core, cov, freq)
    arrived, far = together((arrived, far))
    halves = lax.all_gather(arrived, "col", axis_index_groups=pairs)

    message = jax.ShapeDtypeStruct((blocks, tall, LANES), F32)
    vector = jax.ShapeDtypeStruct((tall, LANES), F32)
    fetched = [pltpu.VMEM((rows - first, half), BF16), pltpu.SemaphoreType.DMA((PARTS,))]
    scratch = [pltpu.VMEM((16, inducing), F32), pltpu.VMEM((tall, LANES), F32)] + fetched
    work = cost(64 * rows * inducing, 2 * rows * inducing)

    sent, before, rhs = pl.pallas_call(
        functools.partial(first_kernel, scale, 1.0 / math.sqrt(rows * blocks)),
        in_specs=[SMEM, VMEM, VMEM, HBM, VMEM, VMEM],
        out_specs=[VMEM] * 3,
        out_shape=[message, jax.ShapeDtypeStruct((1, rows), F32), vector],
        scratch_shapes=scratch,
        compiler_params=params(),
        cost_estimate=work,
        name="first_product",
    )(core, halves, kept, rest, far, weight)
    sent, node_cov_now = together((sent, node_covs[0]))
    arrived = lax.all_to_all(sent, "blk", 0, 0, tiled=True)
    node_phi = node_features(core, node_cov_now, freq, None, 0, height, "node_features_a")
    arrived, node_phi = together((arrived, node_phi))

    sent, fit, solution, residual, direction = pl.pallas_call(
        functools.partial(second_kernel, scale),
        in_specs=[VMEM] * 4 + [HBM, VMEM, VMEM],
        out_specs=[VMEM] * 5,
        out_shape=[message, jax.ShapeDtypeStruct((2, rows), F32), vector, vector, vector],
        scratch_shapes=scratch,
        compiler_params=params(),
        cost_estimate=work,
        name="second_product",
    )(arrived, rhs, before, kept, rest, far, weight)
    sent, node_cov_now = together((sent, node_covs[1]))
    arrived = lax.all_to_all(sent, "blk", 0, 0, tiled=True)
    node_phi = node_features(core, node_cov_now, freq, node_phi, count, height, "node_features_b")
    arrived, node_phi = together((arrived, node_phi))

    sent, both, norm = pl.pallas_call(
        functools.partial(third_kernel, scale, fit_scale),
        in_specs=[VMEM] * 6 + [HBM] + [VMEM] * 5,
        out_specs=[VMEM] * 3,
        out_shape=[
            jax.ShapeDtypeStruct((blocks, 4, patients), F32),
            jax.ShapeDtypeStruct((2, tall, LANES), F32),
            jax.ShapeDtypeStruct((8, LANES), F32),
        ],
        scratch_shapes=fetched,
        compiler_params=params(),
        cost_estimate=work,
        name="third_product",
    )(arrived, solution, residual, direction, fit, kept, rest, far, weight, size, owner, patient)
    sent, both = together((sent, both))
    arrived = lax.all_to_all(sent, "blk", 0, 0, tiled=True)
    node_values = pl.pallas_call(
        nodes_kernel,
        grid=(2 * count // NODE_ROWS,),
        in_specs=[
            pl.BlockSpec(both.shape, lambda i: (0, 0, 0)),
            pl.BlockSpec((NODE_ROWS, inducing), lambda i: (i, 0)),
        ],
        out_specs=pl.BlockSpec((2, NODE_ROWS), lambda i: (0, i)),
        out_shape=jax.ShapeDtypeStruct((2, 2 * count), F32),
        scratch_shapes=[pltpu.VMEM((16, inducing), BF16)],
        compiler_params=params(),
        cost_estimate=cost(64 * 2 * count * inducing, 4 * count * inducing),
        name="node_values",
    )(both, node_phi)
    arrived, node_values = together((arrived, node_values))

    loglik, weights = pl.pallas_call(
        functools.partial(last_kernel, fit_scale),
        in_specs=[SMEM] + [VMEM] * 6,
        out_specs=[VMEM, VMEM],
        out_shape=[
            jax.ShapeDtypeStruct((1, patients), F32),
            jax.ShapeDtypeStruct((1, own), F32),
        ],
        scratch_shapes=[pltpu.VMEM((tall, LANES), F32)],
        compiler_params=params(),
        name="last",
    )(
        layer,
        arrived,
        both,
        norm,
        node_values,
        event_time.reshape(1, patients),
        event_flag.reshape(1, patients),
    )
    return loglik.reshape(patients), weights.reshape(own)


def solution(mesh):
    in_specs = (
        P("blk", None),
        P("blk"),
        P("blk"),
        P("blk", None),
        P("blk"),
        P(None, "col"),
        P("col"),
        P("blk", None, None),
        P("blk"),
        P("blk"),
    )
    out_specs = (P("blk"), P("col"))
    return jax.shard_map(
        on_device, mesh=mesh, in_specs=in_specs, out_specs=out_specs, check_vma=False
    )
```

```python
import functools
import math

import jax
import jax.numpy as jnp
import numpy as np
from jax import lax
from jax.experimental import pallas as pl
from jax.experimental.pallas import tpu as pltpu
from jax.sharding import PartitionSpec as P

F32 = jnp.float32
BF16 = jnp.bfloat16
LOG_SHAPE = math.log(1.5)
LINK = 0.4
LANES = 128
MIB = 1024 * 1024


def cosine_table():
    nodes = 0.125 + 0.125 * np.cos(np.pi * (np.arange(400) + 0.5) / 400)
    values = math.sqrt(2.0) * np.cos(2.0 * np.pi * np.sqrt(nodes))
    fit = np.polynomial.chebyshev.Chebyshev.fit(nodes, values, 5, domain=[0.0, 0.25])
    return [float(c) for c in fit.convert(kind=np.polynomial.Polynomial).coef]


COEFS = cosine_table()
PER_TURN = 1.0 / (2.0 * math.pi)


def feature(angles):
    turns = angles * PER_TURN
    turns = turns - jnp.round(turns)
    square = turns * turns
    total = COEFS[-1]
    for coef in COEFS[-2::-1]:
        total = total * square + coef
    return total.astype(BF16)


def split3(value):
    high = value.astype(BF16).astype(F32)
    rest = value - high
    middle = rest.astype(BF16).astype(F32)
    low = (rest - middle).astype(BF16).astype(F32)
    return high, middle, low


def stack_rows(rows, height):
    at = lax.broadcasted_iota(jnp.int32, (height, rows[0].shape[1]), 0)
    total = jnp.zeros((height, rows[0].shape[1]), F32)
    for index, row in enumerate(rows):
        total = jnp.where(at == index, row, total)
    return total.astype(BF16)


def as_row(tiles):
    return jnp.concatenate([tiles[j : j + 1, :] for j in range(tiles.shape[0])], axis=1)


def dot_nt(a, b):
    return lax.dot_general(a, b, (((1,), (1,)), ((), ())), preferred_element_type=F32)


def dot_nn(a, b):
    return jnp.dot(a, b, preferred_element_type=F32)


VMEM = pl.BlockSpec(memory_space=pltpu.VMEM)
SMEM = pl.BlockSpec(memory_space=pltpu.SMEM)
HBM = pl.BlockSpec(memory_space=pltpu.HBM)
PARTS = 2
KEPT = 0.5
SPARE = 9
PHASE_ROWS = 8


def rows_at(index, size):
    return pl.ds(pl.multiple_of(index * size, size), size)


def total_of(x):
    return jnp.sum(jnp.sum(x, axis=0, keepdims=True), axis=1, keepdims=True)


def params(mebibytes=48):
    return pltpu.CompilerParams(vmem_limit_bytes=mebibytes * MIB)


def cost(flops, size, hard=0):
    return pl.CostEstimate(flops=flops, bytes_accessed=size, transcendentals=hard)


def pack_kernel(freq, phase, out, packed, row, sems):
    depth = freq.shape[0]
    loads = [
        pltpu.make_async_copy(freq, packed.at[0:depth], sems.at[0]),
        pltpu.make_async_copy(phase, row, sems.at[1]),
    ]
    for load in loads:
        load.start()
    for load in loads:
        load.wait()
    packed[depth : depth + PHASE_ROWS, :] = jnp.broadcast_to(
        row[...], (PHASE_ROWS, row.shape[1])
    )
    stores = [
        pltpu.make_async_copy(packed, out.at[copy], sems.at[2 + copy])
        for copy in range(out.shape[0])
    ]
    for store in stores:
        store.start()
    for store in stores:
        store.wait()


def stage_kernel(value, out):
    out[...] = value[...]


def stage(value, name):
    return pl.pallas_call(
        stage_kernel,
        in_specs=[VMEM],
        out_specs=VMEM,
        out_shape=jax.ShapeDtypeStruct(value.shape, value.dtype),
        compiler_params=params(),
        cost_estimate=cost(value.size, 4 * value.size),
        name=name,
    )(value)


def feature_block(rows, freq, store):
    depth = rows.shape[1]
    for j in range(0, freq.shape[0], 2):
        both = jnp.concatenate([freq[j, :depth, :], freq[j + 1, :depth, :]], axis=1)
        phase = jnp.concatenate(
            [freq[j, depth : depth + 1, :], freq[j + 1, depth : depth + 1, :]], axis=1
        )
        store(j * LANES, feature(dot_nn(rows, both) + phase.astype(F32)))


FEATURE_ROWS = 256


def half_features(cov, freq, target, base):
    def step(i, carry):
        at = rows_at(i, FEATURE_ROWS)

        def store(column, value):
            target[at, base + column : base + column + value.shape[1]] = value

        feature_block(cov[at, :], freq, store)
        return carry

    lax.fori_loop(0, cov.shape[0] // FEATURE_ROWS, step, 0)


def far_kernel(core, cov, freq, out):
    half_features(cov, freq.at[1 - core[0]], out, 0)


def far_features(core, cov, freq):
    rows, depth = cov.shape
    columns = freq.shape[1] * LANES
    return pl.pallas_call(
        far_kernel,
        in_specs=[SMEM, VMEM, VMEM],
        out_specs=VMEM,
        out_shape=jax.ShapeDtypeStruct((rows, columns), BF16),
        compiler_params=params(),
        cost_estimate=cost(2 * rows * depth * columns + 20 * rows * columns, 2 * rows * columns),
        name="far_features",
    )(core, cov, freq)


def node_kernel(first, core, cov, freq, *rest):
    out, held, sems = rest[-3:]
    half = freq.shape[1] * LANES
    steps = cov.shape[0] // FEATURE_ROWS

    def leave(i):
        at, to = rows_at(i, FEATURE_ROWS), rows_at(i + first // FEATURE_ROWS, FEATURE_ROWS)
        return pltpu.make_async_copy(held.at[at], out.at[to], sems.at[i])

    def step(i, carry):
        at = rows_at(i, FEATURE_ROWS)
        for index in range(2):
            source = core[0] if index == 0 else 1 - core[0]

            def store(column, value, base=index * half):
                held[at, base + column : base + column + value.shape[1]] = value

            feature_block(cov[at, :], freq.at[source], store)
        leave(i).start()
        return carry

    lax.fori_loop(0, steps, step, 0)
    for i in range(steps):
        leave(i).wait()


def node_features(core, cov, freq, before, first, height, name):
    rows, depth = cov.shape
    columns = 2 * freq.shape[1] * LANES
    earlier = () if before is None else (before,)
    return pl.pallas_call(
        functools.partial(node_kernel, first),
        in_specs=[SMEM, VMEM, VMEM] + [HBM] * len(earlier),
        out_specs=HBM,
        out_shape=jax.ShapeDtypeStruct((height, columns), BF16),
        scratch_shapes=[
            pltpu.VMEM((rows, columns), BF16),
            pltpu.SemaphoreType.DMA((rows // FEATURE_ROWS,)),
        ],
        input_output_aliases={3: 0} if earlier else {},
        compiler_params=params(60),
        cost_estimate=cost(2 * rows * depth * columns + 20 * rows * columns, 2 * rows * columns),
        name=name,
    )(core, cov, freq, *earlier)


def near_kernel(
    cov, freq, weight, size, kept, rest_out, out, rest, gathered, tiles, sems
):
    first = kept.shape[0]

    def fill(target, base, count, after=None):
        group = target.shape[0] // count

        def step(i, carry):
            at = rows_at(i, group)

            def store(column, value):
                target[at, column : column + value.shape[1]] = value

            rows = cov[pl.ds(pl.multiple_of(base + i * group, 64), group), :]
            feature_block(rows, freq, store)
            if after is not None:
                after(i, group).start()
            return carry

        lax.fori_loop(0, count, step, 0)

    def leave(i, group):
        at = rows_at(i, group)
        return pltpu.make_async_copy(rest.at[at], rest_out.at[at], sems.at[i])

    fill(rest, first, PARTS, leave)
    fill(kept, 0, PARTS)
    product = weight[...].astype(F32) * size[...].astype(F32)
    split = stack_rows(split3(product), 16)
    gathered[...] = dot_nn(split[:, :first], kept[...]) + dot_nn(split[:, first:], rest[...])
    send_whole(gathered, tiles, out)
    for i in range(PARTS):
        leave(i, rest.shape[0] // PARTS).wait()


def rows_of(vector):
    return stack_rows(split3(as_row(vector)), 16)


def send_whole(gathered, tiles, out):
    total = jnp.sum(gathered[...], axis=0, keepdims=True)
    for j in range(tiles.shape[0]):
        tiles[j : j + 1, :] = total[:, j * LANES : (j + 1) * LANES]
    whole = tiles[...]
    for copy in range(out.shape[0]):
        out[copy] = whole


def fetch(rest, held, sems):
    part = held.shape[0] // PARTS
    copies = []
    for k in range(PARTS):
        at = slice(k * part, (k + 1) * part)
        copy = pltpu.make_async_copy(rest.at[at], held.at[at], sems.at[k])
        copy.start()
        copies.append((at, copy))
    return copies


def forward(direction, kept, held, copies, far):
    split = rows_of(direction)
    half = far.shape[1]
    near = split[:, :half]
    total = jnp.sum(dot_nt(split[:, half:], far[...]), axis=0, keepdims=True)
    values = [jnp.sum(dot_nt(near, kept[...]), axis=0, keepdims=True)]
    for at, copy in copies:
        copy.wait()
        values.append(jnp.sum(dot_nt(near, held[at]), axis=0, keepdims=True))
    return jnp.concatenate(values, axis=1) + total


def product(direction, kept, held, copies, far, weight, gathered, tiles, out, scale):
    values = forward(direction, kept, held, copies, far)
    split = stack_rows(split3(weight[...].astype(F32) * values * scale), 16)
    half, first = far.shape[1], kept.shape[0]
    gathered[:, half:] = dot_nn(split, far[...])
    gathered[:, :half] = dot_nn(split[:, :first], kept[...]) + dot_nn(split[:, first:], held[...])
    send_whole(gathered, tiles, out)
    return values


def first_kernel(
    scale, rhs_scale, core, halves, kept, rest, far, weight, out, values_out, rhs_out, gathered, tiles, held, sems
):
    copies = fetch(rest, held, sems)
    low, high = (jnp.sum(halves[h], axis=0) * rhs_scale for h in range(2))
    swap = core[0] == 1
    half = low.shape[0]
    rhs_out[0:half, :] = jnp.where(swap, high, low)
    rhs_out[half : 2 * half, :] = jnp.where(swap, low, high)
    values_out[...] = product(
        rhs_out[...], kept, held, copies, far, weight, gathered, tiles, out, scale
    )


def second_kernel(
    scale, arrived, rhs, before, kept, rest, far, weight,
    out, fit_out, solution_out, residual_out, direction_out,
    gathered, tiles, held, sems,
):
    copies = fetch(rest, held, sems)
    direction = rhs[...]
    norm = total_of(direction * direction)
    image = direction + jnp.sum(arrived[...], axis=0)
    length = norm / total_of(direction * image)
    residual = direction - length * image
    later = residual + total_of(residual * residual) / norm * direction
    solution_out[...] = length * direction
    residual_out[...] = residual
    direction_out[...] = later
    fit_out[0:1, :] = length * before[...]
    fit_out[1:2, :] = product(
        later, kept, held, copies, far, weight, gathered, tiles, out, scale
    )


def third_kernel(
    scale, fit_scale, arrived, solution, residual, direction, fit, kept, rest, far, weight, size, owner, patient,
    out, both_out, norm_out,
    held, sems,
):
    copies = fetch(rest, held, sems)
    before = direction[...]
    left = residual[...]
    norm = total_of(left * left)
    image = before + jnp.sum(arrived[...], axis=0)
    length = norm / total_of(before * image)
    left = left - length * image
    norm_next = total_of(left * left)
    later = left + norm_next / norm * before
    both_out[0] = solution[...] + length * before
    both_out[1] = later
    norm_out[...] = jnp.broadcast_to(norm_next, norm_out.shape)
    values = forward(later, kept, held, copies, far)
    fitted = fit[0:1, :] + length * fit[1:2, :]
    weights = weight[...].astype(F32)
    weighted = weights * values
    energy = total_of(weighted * values) * scale
    part = weights * (size[...].astype(F32) - fitted * fit_scale)
    owners, patients = out.shape[0], out.shape[2]
    here = values.shape[1]
    to_owner = (owner[...] == lax.broadcasted_iota(jnp.int32, (owners, here), 0)).astype(F32)
    to_patient = (patient[...] == lax.broadcasted_iota(jnp.int32, (patients, here), 0)).astype(F32)
    parts = split3(part) + split3(weighted * fit_scale) + (weights,)
    tall = jnp.concatenate([to_owner * part for part in parts], axis=0).astype(BF16)
    sums = dot_nt(tall, to_patient.astype(BF16))
    part = [sums[i * owners : (i + 1) * owners, :] for i in range(len(parts))]
    out[:, 0, :] = part[0] + part[1] + part[2]
    out[:, 1, :] = part[3] + part[4] + part[5]
    out[:, 2, :] = part[6]
    out[:, 3, :] = jnp.broadcast_to(energy, (owners, patients))


NODE_ROWS = 512


def nodes_kernel(both, phi, out, split):
    @pl.when(pl.program_id(0) == 0)
    def _():
        rows = split3(as_row(both[0])) + split3(as_row(both[1]))
        split[...] = stack_rows(rows, 16)

    products = dot_nt(split[...], phi[...])
    out[0:1, :] = products[0:1] + products[1:2] + products[2:3]
    out[1:2, :] = products[3:4] + products[4:5] + products[5:6]


def last_kernel(fit_scale, mine, arrived, both, norm, node_values, time, flag, loglik, weights_out, tiles):
    sums = jnp.sum(arrived[...], axis=0)
    direction = both[1]
    denominator = total_of(direction * direction) + sums[3:4, 0:1]
    length = norm[0:1, 0:1] / denominator
    tiles[...] = both[0] + length * direction
    weights_out[...] = tiles[pl.ds(mine[0], 1), :]
    effect = (sums[0:1, :] - length * sums[1:2, :]) / (1.0 + sums[2:3, :])
    values = (node_values[0:1, :] + length * node_values[1:2, :]) * fit_scale
    patients = loglik.shape[1]
    nodes = values.shape[1] // patients
    total = jnp.zeros_like(effect)
    eta = total
    when = time[...]
    for q in range(nodes):
        grid = when * (q + 1.0) / nodes
        eta = (
            LOG_SHAPE
            + 0.5 * jnp.log(grid)
            + LINK * (values[:, q * patients : (q + 1) * patients] + effect)
        )
        total = total + jnp.exp(eta)
    loglik[...] = flag[...].astype(F32) * eta - when / nodes * total


def on_device(
    visit_cov,
    tumor_size,
    visit_weight,
    visit_owner,
    visit_patient,
    inducing_freq,
    inducing_phase,
    node_cov,
    event_time,
    event_flag,
):
    blocks, cols = lax.axis_size("blk"), lax.axis_size("col")
    rows, depth = visit_cov.shape
    own = inducing_freq.shape[1]
    inducing = own * cols
    tall = inducing // LANES
    layers = cols // 2
    patients, nodes = node_cov.shape[:2]
    scale = 1.0 / (rows * blocks)
    fit_scale = 1.0 / math.sqrt(inducing)
    weight = visit_weight.reshape(1, rows)
    size = tumor_size.reshape(1, rows)
    owner = visit_owner.reshape(1, rows)
    patient = visit_patient.reshape(1, rows)
    place = lax.axis_index("col").astype(jnp.int32)
    core = (place % 2).reshape(1)
    layer = (place // 2).reshape(1)
    together = lax.optimization_barrier
    same_core = [[2 * z + c for z in range(layers)] for c in range(2)]
    pairs = [[2 * z, 2 * z + 1] for z in range(layers)]

    packed = pl.pallas_call(
        pack_kernel,
        in_specs=[HBM, HBM],
        out_specs=HBM,
        out_shape=jax.ShapeDtypeStruct((layers, depth + PHASE_ROWS, own), BF16),
        scratch_shapes=[
            pltpu.VMEM((depth + PHASE_ROWS, own), BF16),
            pltpu.VMEM((1, own), BF16),
            pltpu.SemaphoreType.DMA((2 + layers,)),
        ],
        compiler_params=params(60),
        name="pack",
    )(inducing_freq, inducing_phase.reshape(1, own))
    packed, cov, turned = together((packed, visit_cov, node_cov))
    near_freq = lax.all_to_all(packed, "col", 0, 0, tiled=True, axis_index_groups=same_core)
    cov = stage(cov, "stage_cov")
    by_node = turned.transpose(1, 0, 2).reshape(nodes * patients, depth)
    count = nodes * patients // 2
    height = (SPARE * nodes * patients) // 4
    node_covs = (by_node[:count], by_node[count:])
    near_freq, cov, node_covs = together((near_freq, cov, node_covs))

    half = inducing // 2
    first = int(rows * KEPT)
    kept, rest, sent = pl.pallas_call(
        near_kernel,
        in_specs=[VMEM] * 4,
        out_specs=[VMEM, HBM, VMEM],
        out_shape=[
            jax.ShapeDtypeStruct((first, half), BF16),
            jax.ShapeDtypeStruct((SPARE * rows, half), BF16),
            jax.ShapeDtypeStruct((blocks, tall // 2, LANES), F32),
        ],
        scratch_shapes=[
            pltpu.VMEM((rows - first, half), BF16),
            pltpu.VMEM((16, half), F32),
            pltpu.VMEM((tall // 2, LANES), F32),
            pltpu.SemaphoreType.DMA((PARTS,)),
        ],
        compiler_params=params(),
        name="near_features",
    )(cov, near_freq, weight, size)
    sent, late_freq = together((sent, near_freq))
    arrived = lax.all_to_all(sent, "blk", 0, 0, tiled=True)
    freq = lax.all_gather(late_freq, "col", axis_index_groups=pairs)
    far = far_features(core, cov, freq)
    arrived, far = together((arrived, far))
    halves = lax.all_gather(arrived, "col", axis_index_groups=pairs)

    message = jax.ShapeDtypeStruct((blocks, tall, LANES), F32)
    vector = jax.ShapeDtypeStruct((tall, LANES), F32)
    fetched = [pltpu.VMEM((rows - first, half), BF16), pltpu.SemaphoreType.DMA((PARTS,))]
    scratch = [pltpu.VMEM((16, inducing), F32), pltpu.VMEM((tall, LANES), F32)] + fetched
    work = cost(64 * rows * inducing, 2 * rows * inducing)

    sent, before, rhs = pl.pallas_call(
        functools.partial(first_kernel, scale, 1.0 / math.sqrt(rows * blocks)),
        in_specs=[SMEM, VMEM, VMEM, HBM, VMEM, VMEM],
        out_specs=[VMEM] * 3,
        out_shape=[message, jax.ShapeDtypeStruct((1, rows), F32), vector],
        scratch_shapes=scratch,
        compiler_params=params(),
        cost_estimate=work,
        name="first_product",
    )(core, halves, kept, rest, far, weight)
    sent, node_cov_now = together((sent, node_covs[0]))
    arrived = lax.all_to_all(sent, "blk", 0, 0, tiled=True)
    node_phi = node_features(core, node_cov_now, freq, None, 0, height, "node_features_a")
    arrived, node_phi = together((arrived, node_phi))

    sent, fit, solution, residual, direction = pl.pallas_call(
        functools.partial(second_kernel, scale),
        in_specs=[VMEM] * 4 + [HBM, VMEM, VMEM],
        out_specs=[VMEM] * 5,
        out_shape=[message, jax.ShapeDtypeStruct((2, rows), F32), vector, vector, vector],
        scratch_shapes=scratch,
        compiler_params=params(),
        cost_estimate=work,
        name="second_product",
    )(arrived, rhs, before, kept, rest, far, weight)
    sent, node_cov_now = together((sent, node_covs[1]))
    arrived = lax.all_to_all(sent, "blk", 0, 0, tiled=True)
    node_phi = node_features(core, node_cov_now, freq, node_phi, count, height, "node_features_b")
    arrived, node_phi = together((arrived, node_phi))

    sent, both, norm = pl.pallas_call(
        functools.partial(third_kernel, scale, fit_scale),
        in_specs=[VMEM] * 6 + [HBM] + [VMEM] * 5,
        out_specs=[VMEM] * 3,
        out_shape=[
            jax.ShapeDtypeStruct((blocks, 4, patients), F32),
            jax.ShapeDtypeStruct((2, tall, LANES), F32),
            jax.ShapeDtypeStruct((8, LANES), F32),
        ],
        scratch_shapes=fetched,
        compiler_params=params(),
        cost_estimate=work,
        name="third_product",
    )(arrived, solution, residual, direction, fit, kept, rest, far, weight, size, owner, patient)
    sent, both = together((sent, both))
    arrived = lax.all_to_all(sent, "blk", 0, 0, tiled=True)
    node_values = pl.pallas_call(
        nodes_kernel,
        grid=(2 * count // NODE_ROWS,),
        in_specs=[
            pl.BlockSpec(both.shape, lambda i: (0, 0, 0)),
            pl.BlockSpec((NODE_ROWS, inducing), lambda i: (i, 0)),
        ],
        out_specs=pl.BlockSpec((2, NODE_ROWS), lambda i: (0, i)),
        out_shape=jax.ShapeDtypeStruct((2, 2 * count), F32),
        scratch_shapes=[pltpu.VMEM((16, inducing), BF16)],
        compiler_params=params(),
        cost_estimate=cost(64 * 2 * count * inducing, 4 * count * inducing),
        name="node_values",
    )(both, node_phi)
    arrived, node_values = together((arrived, node_values))

    loglik, weights = pl.pallas_call(
        functools.partial(last_kernel, fit_scale),
        in_specs=[SMEM] + [VMEM] * 6,
        out_specs=[VMEM, VMEM],
        out_shape=[
            jax.ShapeDtypeStruct((1, patients), F32),
            jax.ShapeDtypeStruct((1, own), F32),
        ],
        scratch_shapes=[pltpu.VMEM((tall, LANES), F32)],
        compiler_params=params(),
        name="last",
    )(
        layer,
        arrived,
        both,
        norm,
        node_values,
        event_time.reshape(1, patients),
        event_flag.reshape(1, patients),
    )
    return loglik.reshape(patients), weights.reshape(own)


def solution(mesh):
    in_specs = (
        P("blk", None),
        P("blk"),
        P("blk"),
        P("blk", None),
        P("blk"),
        P(None, "col"),
        P("col"),
        P("blk", None, None),
        P("blk"),
        P("blk"),
    )
    out_specs = (P("blk"), P("col"))
    return jax.shard_map(
        on_device, mesh=mesh, in_specs=in_specs, out_specs=out_specs, check_vma=False
    )
```

```python
import functools
import math

import jax
import jax.numpy as jnp
import numpy as np
from jax import lax
from jax.experimental import pallas as pl
from jax.experimental.pallas import tpu as pltpu
from jax.sharding import PartitionSpec as P

F32 = jnp.float32
BF16 = jnp.bfloat16
LOG_SHAPE = math.log(1.5)
LINK = 0.4
LANES = 128
MIB = 1024 * 1024


def cosine_table():
    nodes = 0.125 + 0.125 * np.cos(np.pi * (np.arange(400) + 0.5) / 400)
    values = math.sqrt(2.0) * np.cos(2.0 * np.pi * np.sqrt(nodes))
    fit = np.polynomial.chebyshev.Chebyshev.fit(nodes, values, 5, domain=[0.0, 0.25])
    return [float(c) for c in fit.convert(kind=np.polynomial.Polynomial).coef]


COEFS = cosine_table()
PER_TURN = 1.0 / (2.0 * math.pi)


def feature(angles):
    turns = angles * PER_TURN
    turns = turns - jnp.round(turns)
    square = turns * turns
    total = COEFS[-1]
    for coef in COEFS[-2::-1]:
        total = total * square + coef
    return total.astype(BF16)


def split3(value):
    high = value.astype(BF16).astype(F32)
    rest = value - high
    middle = rest.astype(BF16).astype(F32)
    low = (rest - middle).astype(BF16).astype(F32)
    return high, middle, low


def stack_rows(rows, height):
    at = lax.broadcasted_iota(jnp.int32, (height, rows[0].shape[1]), 0)
    total = jnp.zeros((height, rows[0].shape[1]), F32)
    for index, row in enumerate(rows):
        total = jnp.where(at == index, row, total)
    return total.astype(BF16)


def as_row(tiles):
    return jnp.concatenate([tiles[j : j + 1, :] for j in range(tiles.shape[0])], axis=1)


def dot_nt(a, b):
    return lax.dot_general(a, b, (((1,), (1,)), ((), ())), preferred_element_type=F32)


def dot_nn(a, b):
    return jnp.dot(a, b, preferred_element_type=F32)


VMEM = pl.BlockSpec(memory_space=pltpu.VMEM)
SMEM = pl.BlockSpec(memory_space=pltpu.SMEM)
HBM = pl.BlockSpec(memory_space=pltpu.HBM)
PARTS = 2
KEPT = 0.5
SPARE = 9
PHASE_ROWS = 16


def rows_at(index, size):
    return pl.ds(pl.multiple_of(index * size, size), size)


def total_of(x):
    return jnp.sum(jnp.sum(x, axis=0, keepdims=True), axis=1, keepdims=True)


def params(mebibytes=48):
    return pltpu.CompilerParams(vmem_limit_bytes=mebibytes * MIB)


def cost(flops, size, hard=0):
    return pl.CostEstimate(flops=flops, bytes_accessed=size, transcendentals=hard)


def pack_kernel(freq, phase, out, row, last, sems):
    depth = freq.shape[0]
    copies = out.shape[0]
    load = pltpu.make_async_copy(phase, row, sems.at[2 * copies])
    load.start()
    stores = [
        pltpu.make_async_copy(freq, out.at[copy, 0:depth], sems.at[copy]) for copy in range(copies)
    ]
    for store in stores:
        store.start()
    load.wait()
    last[...] = jnp.broadcast_to(row[...], last.shape)
    tails = [
        pltpu.make_async_copy(
            last, out.at[copy, depth : depth + PHASE_ROWS], sems.at[copies + copy]
        )
        for copy in range(copies)
    ]
    for tail in tails:
        tail.start()
    for store in stores + tails:
        store.wait()


def stage_kernel(value, out):
    out[...] = value[...]


def stage(value, name):
    return pl.pallas_call(
        stage_kernel,
        in_specs=[VMEM],
        out_specs=VMEM,
        out_shape=jax.ShapeDtypeStruct(value.shape, value.dtype),
        compiler_params=params(),
        cost_estimate=cost(value.size, 4 * value.size),
        name=name,
    )(value)


def feature_block(rows, freq, store):
    depth = rows.shape[1]
    for j in range(0, freq.shape[0], 2):
        both = jnp.concatenate([freq[j, :depth, :], freq[j + 1, :depth, :]], axis=1)
        phase = jnp.concatenate(
            [freq[j, depth : depth + 1, :], freq[j + 1, depth : depth + 1, :]], axis=1
        )
        store(j * LANES, feature(dot_nn(rows, both) + phase.astype(F32)))


FEATURE_ROWS = 256


def half_features(cov, freq, target, base):
    def step(i, carry):
        at = rows_at(i, FEATURE_ROWS)

        def store(column, value):
            target[at, base + column : base + column + value.shape[1]] = value

        feature_block(cov[at, :], freq, store)
        return carry

    lax.fori_loop(0, cov.shape[0] // FEATURE_ROWS, step, 0)


def far_kernel(core, cov, freq, out):
    half_features(cov, freq.at[1 - core[0]], out, 0)


def far_features(core, cov, freq):
    rows, depth = cov.shape
    columns = freq.shape[1] * LANES
    return pl.pallas_call(
        far_kernel,
        in_specs=[SMEM, VMEM, VMEM],
        out_specs=VMEM,
        out_shape=jax.ShapeDtypeStruct((rows, columns), BF16),
        compiler_params=params(),
        cost_estimate=cost(2 * rows * depth * columns + 20 * rows * columns, 2 * rows * columns),
        name="far_features",
    )(core, cov, freq)


def node_kernel(first, core, cov, freq, *rest):
    out, held, sems = rest[-3:]
    half = freq.shape[1] * LANES
    steps = cov.shape[0] // FEATURE_ROWS

    def leave(i):
        at, to = rows_at(i, FEATURE_ROWS), rows_at(i + first // FEATURE_ROWS, FEATURE_ROWS)
        return pltpu.make_async_copy(held.at[at], out.at[to], sems.at[i])

    def step(i, carry):
        at = rows_at(i, FEATURE_ROWS)
        for index in range(2):
            source = core[0] if index == 0 else 1 - core[0]

            def store(column, value, base=index * half):
                held[at, base + column : base + column + value.shape[1]] = value

            feature_block(cov[at, :], freq.at[source], store)
        leave(i).start()
        return carry

    lax.fori_loop(0, steps, step, 0)
    for i in range(steps):
        leave(i).wait()


def node_features(core, cov, freq, before, first, height, name):
    rows, depth = cov.shape
    columns = 2 * freq.shape[1] * LANES
    earlier = () if before is None else (before,)
    return pl.pallas_call(
        functools.partial(node_kernel, first),
        in_specs=[SMEM, VMEM, VMEM] + [HBM] * len(earlier),
        out_specs=HBM,
        out_shape=jax.ShapeDtypeStruct((height, columns), BF16),
        scratch_shapes=[
            pltpu.VMEM((rows, columns), BF16),
            pltpu.SemaphoreType.DMA((rows // FEATURE_ROWS,)),
        ],
        input_output_aliases={3: 0} if earlier else {},
        compiler_params=params(60),
        cost_estimate=cost(2 * rows * depth * columns + 20 * rows * columns, 2 * rows * columns),
        name=name,
    )(core, cov, freq, *earlier)


def near_kernel(
    cov, freq, weight, size, kept, rest_out, out, rest, gathered, tiles, sems
):
    first = kept.shape[0]

    def fill(target, base, count, after=None):
        group = target.shape[0] // count

        def step(i, carry):
            at = rows_at(i, group)

            def store(column, value):
                target[at, column : column + value.shape[1]] = value

            rows = cov[pl.ds(pl.multiple_of(base + i * group, 64), group), :]
            feature_block(rows, freq, store)
            if after is not None:
                after(i, group).start()
            return carry

        lax.fori_loop(0, count, step, 0)

    def leave(i, group):
        at = rows_at(i, group)
        return pltpu.make_async_copy(rest.at[at], rest_out.at[at], sems.at[i])

    fill(rest, first, 1, leave)
    fill(kept, 0, 1)
    product = weight[...].astype(F32) * size[...].astype(F32)
    split = stack_rows(split3(product), 16)
    gathered[...] = dot_nn(split[:, :first], kept[...]) + dot_nn(split[:, first:], rest[...])
    send_whole(gathered, tiles, out)
    leave(0, rest.shape[0]).wait()


def rows_of(vector):
    return stack_rows(split3(as_row(vector)), 16)


def send_whole(gathered, tiles, out):
    total = jnp.sum(gathered[...], axis=0, keepdims=True)
    for j in range(tiles.shape[0]):
        tiles[j : j + 1, :] = total[:, j * LANES : (j + 1) * LANES]
    whole = tiles[...]
    for copy in range(out.shape[0]):
        out[copy] = whole


def fetch(rest, held, sems):
    part = held.shape[0] // PARTS
    copies = []
    for k in range(PARTS):
        at = slice(k * part, (k + 1) * part)
        copy = pltpu.make_async_copy(rest.at[at], held.at[at], sems.at[k])
        copy.start()
        copies.append((at, copy))
    return copies


def forward(direction, kept, held, copies, far):
    split = rows_of(direction)
    half = far.shape[1]
    near = split[:, :half]
    total = jnp.sum(dot_nt(split[:, half:], far[...]), axis=0, keepdims=True)
    values = [jnp.sum(dot_nt(near, kept[...]), axis=0, keepdims=True)]
    for at, copy in copies:
        copy.wait()
        values.append(jnp.sum(dot_nt(near, held[at]), axis=0, keepdims=True))
    return jnp.concatenate(values, axis=1) + total


def product(direction, kept, held, copies, far, weight, gathered, tiles, out, scale):
    values = forward(direction, kept, held, copies, far)
    split = stack_rows(split3(weight[...].astype(F32) * values * scale), 16)
    half, first = far.shape[1], kept.shape[0]
    gathered[:, half:] = dot_nn(split, far[...])
    gathered[:, :half] = dot_nn(split[:, :first], kept[...]) + dot_nn(split[:, first:], held[...])
    send_whole(gathered, tiles, out)
    return values


def first_kernel(
    scale, rhs_scale, core, halves, kept, rest, far, weight, out, values_out, rhs_out, gathered, tiles, held, sems
):
    copies = fetch(rest, held, sems)
    low, high = (jnp.sum(halves[h], axis=0) * rhs_scale for h in range(2))
    swap = core[0] == 1
    half = low.shape[0]
    rhs_out[0:half, :] = jnp.where(swap, high, low)
    rhs_out[half : 2 * half, :] = jnp.where(swap, low, high)
    values_out[...] = product(
        rhs_out[...], kept, held, copies, far, weight, gathered, tiles, out, scale
    )


def second_kernel(
    scale, arrived, rhs, before, kept, rest, far, weight,
    out, fit_out, solution_out, residual_out, direction_out,
    gathered, tiles, held, sems,
):
    copies = fetch(rest, held, sems)
    direction = rhs[...]
    norm = total_of(direction * direction)
    image = direction + jnp.sum(arrived[...], axis=0)
    length = norm / total_of(direction * image)
    residual = direction - length * image
    later = residual + total_of(residual * residual) / norm * direction
    solution_out[...] = length * direction
    residual_out[...] = residual
    direction_out[...] = later
    fit_out[0:1, :] = length * before[...]
    fit_out[1:2, :] = product(
        later, kept, held, copies, far, weight, gathered, tiles, out, scale
    )


def third_kernel(
    scale, fit_scale, arrived, solution, residual, direction, fit, kept, rest, far, weight, size, owner, patient,
    out, both_out, norm_out,
    held, sems,
):
    copies = fetch(rest, held, sems)
    before = direction[...]
    left = residual[...]
    norm = total_of(left * left)
    image = before + jnp.sum(arrived[...], axis=0)
    length = norm / total_of(before * image)
    left = left - length * image
    norm_next = total_of(left * left)
    later = left + norm_next / norm * before
    both_out[0] = solution[...] + length * before
    both_out[1] = later
    norm_out[...] = jnp.broadcast_to(norm_next, norm_out.shape)
    values = forward(later, kept, held, copies, far)
    fitted = fit[0:1, :] + length * fit[1:2, :]
    weights = weight[...].astype(F32)
    weighted = weights * values
    energy = total_of(weighted * values) * scale
    part = weights * (size[...].astype(F32) - fitted * fit_scale)
    owners, patients = out.shape[0], out.shape[2]
    here = values.shape[1]
    to_owner = (owner[...] == lax.broadcasted_iota(jnp.int32, (owners, here), 0)).astype(F32)
    to_patient = (patient[...] == lax.broadcasted_iota(jnp.int32, (patients, here), 0)).astype(F32)
    parts = split3(part)[:2] + split3(weighted * fit_scale)[:2] + (weights,)
    tall = jnp.concatenate([to_owner * part for part in parts], axis=0).astype(BF16)
    sums = dot_nt(tall, to_patient.astype(BF16))
    part = [sums[i * owners : (i + 1) * owners, :] for i in range(len(parts))]
    out[:, 0, :] = part[0] + part[1]
    out[:, 1, :] = part[2] + part[3]
    out[:, 2, :] = part[4]
    out[:, 3, :] = jnp.broadcast_to(energy, (owners, patients))


NODE_ROWS = 512


def nodes_kernel(both, phi, out, split):
    @pl.when(pl.program_id(0) == 0)
    def _():
        rows = split3(as_row(both[0])) + split3(as_row(both[1]))
        split[...] = stack_rows(rows, 16)

    products = dot_nt(split[...], phi[...])
    out[0:1, :] = products[0:1] + products[1:2] + products[2:3]
    out[1:2, :] = products[3:4] + products[4:5] + products[5:6]


def last_kernel(fit_scale, mine, arrived, both, norm, node_values, time, flag, loglik, weights_out, tiles):
    sums = jnp.sum(arrived[...], axis=0)
    direction = both[1]
    denominator = total_of(direction * direction) + sums[3:4, 0:1]
    length = norm[0:1, 0:1] / denominator
    tiles[...] = both[0] + length * direction
    weights_out[...] = tiles[pl.ds(mine[0], 1), :]
    effect = (sums[0:1, :] - length * sums[1:2, :]) / (1.0 + sums[2:3, :])
    values = (node_values[0:1, :] + length * node_values[1:2, :]) * fit_scale
    patients = loglik.shape[1]
    nodes = values.shape[1] // patients
    total = jnp.zeros_like(effect)
    eta = total
    when = time[...]
    for q in range(nodes):
        grid = when * (q + 1.0) / nodes
        eta = (
            LOG_SHAPE
            + 0.5 * jnp.log(grid)
            + LINK * (values[:, q * patients : (q + 1) * patients] + effect)
        )
        total = total + jnp.exp(eta)
    loglik[...] = flag[...].astype(F32) * eta - when / nodes * total


def on_device(
    visit_cov,
    tumor_size,
    visit_weight,
    visit_owner,
    visit_patient,
    inducing_freq,
    inducing_phase,
    node_cov,
    event_time,
    event_flag,
):
    blocks, cols = lax.axis_size("blk"), lax.axis_size("col")
    rows, depth = visit_cov.shape
    own = inducing_freq.shape[1]
    inducing = own * cols
    tall = inducing // LANES
    layers = cols // 2
    patients, nodes = node_cov.shape[:2]
    scale = 1.0 / (rows * blocks)
    fit_scale = 1.0 / math.sqrt(inducing)
    weight = visit_weight.reshape(1, rows)
    size = tumor_size.reshape(1, rows)
    owner = visit_owner.reshape(1, rows)
    patient = visit_patient.reshape(1, rows)
    place = lax.axis_index("col").astype(jnp.int32)
    core = (place % 2).reshape(1)
    layer = (place // 2).reshape(1)
    together = lax.optimization_barrier
    same_core = [[2 * z + c for z in range(layers)] for c in range(2)]
    pairs = [[2 * z, 2 * z + 1] for z in range(layers)]

    packed = pl.pallas_call(
        pack_kernel,
        in_specs=[HBM, HBM],
        out_specs=HBM,
        out_shape=jax.ShapeDtypeStruct((layers, depth + PHASE_ROWS, own), BF16),
        scratch_shapes=[
            pltpu.VMEM((1, own), BF16),
            pltpu.VMEM((PHASE_ROWS, own), BF16),
            pltpu.SemaphoreType.DMA((2 * layers + 1,)),
        ],
        compiler_params=params(60),
        name="pack",
    )(inducing_freq, inducing_phase.reshape(1, own))
    packed, cov, turned = together((packed, visit_cov, node_cov))
    near_freq = lax.all_to_all(packed, "col", 0, 0, tiled=True, axis_index_groups=same_core)
    cov = stage(cov, "stage_cov")
    by_node = turned.transpose(1, 0, 2).reshape(nodes * patients, depth)
    count = nodes * patients // 2
    height = (SPARE * nodes * patients) // 4
    node_covs = (by_node[:count], by_node[count:])
    near_freq, cov, node_covs = together((near_freq, cov, node_covs))

    half = inducing // 2
    first = int(rows * KEPT)
    kept, rest, sent = pl.pallas_call(
        near_kernel,
        in_specs=[VMEM] * 4,
        out_specs=[VMEM, HBM, VMEM],
        out_shape=[
            jax.ShapeDtypeStruct((first, half), BF16),
            jax.ShapeDtypeStruct((SPARE * rows, half), BF16),
            jax.ShapeDtypeStruct((blocks, tall // 2, LANES), F32),
        ],
        scratch_shapes=[
            pltpu.VMEM((rows - first, half), BF16),
            pltpu.VMEM((16, half), F32),
            pltpu.VMEM((tall // 2, LANES), F32),
            pltpu.SemaphoreType.DMA((1,)),
        ],
        compiler_params=params(),
        name="near_features",
    )(cov, near_freq, weight, size)
    sent, late_freq = together((sent, near_freq))
    arrived = lax.all_to_all(sent, "blk", 0, 0, tiled=True)
    freq = lax.all_gather(late_freq, "col", axis_index_groups=pairs)
    far = far_features(core, cov, freq)
    arrived, far = together((arrived, far))
    halves = lax.all_gather(arrived, "col", axis_index_groups=pairs)

    message = jax.ShapeDtypeStruct((blocks, tall, LANES), F32)
    vector = jax.ShapeDtypeStruct((tall, LANES), F32)
    fetched = [pltpu.VMEM((rows - first, half), BF16), pltpu.SemaphoreType.DMA((PARTS,))]
    scratch = [pltpu.VMEM((16, inducing), F32), pltpu.VMEM((tall, LANES), F32)] + fetched
    work = cost(64 * rows * inducing, 2 * rows * inducing)

    sent, before, rhs = pl.pallas_call(
        functools.partial(first_kernel, scale, 1.0 / math.sqrt(rows * blocks)),
        in_specs=[SMEM, VMEM, VMEM, HBM, VMEM, VMEM],
        out_specs=[VMEM] * 3,
        out_shape=[message, jax.ShapeDtypeStruct((1, rows), F32), vector],
        scratch_shapes=scratch,
        compiler_params=params(),
        cost_estimate=work,
        name="first_product",
    )(core, halves, kept, rest, far, weight)
    sent, node_cov_now = together((sent, node_covs[0]))
    arrived = lax.all_to_all(sent, "blk", 0, 0, tiled=True)
    node_phi = node_features(core, node_cov_now, freq, None, 0, height, "node_features_a")
    arrived, node_phi = together((arrived, node_phi))

    sent, fit, solution, residual, direction = pl.pallas_call(
        functools.partial(second_kernel, scale),
        in_specs=[VMEM] * 4 + [HBM, VMEM, VMEM],
        out_specs=[VMEM] * 5,
        out_shape=[message, jax.ShapeDtypeStruct((2, rows), F32), vector, vector, vector],
        scratch_shapes=scratch,
        compiler_params=params(),
        cost_estimate=work,
        name="second_product",
    )(arrived, rhs, before, kept, rest, far, weight)
    sent, node_cov_now = together((sent, node_covs[1]))
    arrived = lax.all_to_all(sent, "blk", 0, 0, tiled=True)
    node_phi = node_features(core, node_cov_now, freq, node_phi, count, height, "node_features_b")
    arrived, node_phi = together((arrived, node_phi))

    sent, both, norm = pl.pallas_call(
        functools.partial(third_kernel, scale, fit_scale),
        in_specs=[VMEM] * 6 + [HBM] + [VMEM] * 5,
        out_specs=[VMEM] * 3,
        out_shape=[
            jax.ShapeDtypeStruct((blocks, 4, patients), F32),
            jax.ShapeDtypeStruct((2, tall, LANES), F32),
            jax.ShapeDtypeStruct((8, LANES), F32),
        ],
        scratch_shapes=fetched,
        compiler_params=params(),
        cost_estimate=work,
        name="third_product",
    )(arrived, solution, residual, direction, fit, kept, rest, far, weight, size, owner, patient)
    sent, both = together((sent, both))
    arrived = lax.all_to_all(sent, "blk", 0, 0, tiled=True)
    node_values = pl.pallas_call(
        nodes_kernel,
        grid=(2 * count // NODE_ROWS,),
        in_specs=[
            pl.BlockSpec(both.shape, lambda i: (0, 0, 0)),
            pl.BlockSpec((NODE_ROWS, inducing), lambda i: (i, 0)),
        ],
        out_specs=pl.BlockSpec((2, NODE_ROWS), lambda i: (0, i)),
        out_shape=jax.ShapeDtypeStruct((2, 2 * count), F32),
        scratch_shapes=[pltpu.VMEM((16, inducing), BF16)],
        compiler_params=params(),
        cost_estimate=cost(64 * 2 * count * inducing, 4 * count * inducing),
        name="node_values",
    )(both, node_phi)
    arrived, node_values = together((arrived, node_values))

    loglik, weights = pl.pallas_call(
        functools.partial(last_kernel, fit_scale),
        in_specs=[SMEM] + [VMEM] * 6,
        out_specs=[VMEM, VMEM],
        out_shape=[
            jax.ShapeDtypeStruct((1, patients), F32),
            jax.ShapeDtypeStruct((1, own), F32),
        ],
        scratch_shapes=[pltpu.VMEM((tall, LANES), F32)],
        compiler_params=params(),
        name="last",
    )(
        layer,
        arrived,
        both,
        norm,
        node_values,
        event_time.reshape(1, patients),
        event_flag.reshape(1, patients),
    )
    return loglik.reshape(patients), weights.reshape(own)


def solution(mesh):
    in_specs = (
        P("blk", None),
        P("blk"),
        P("blk"),
        P("blk", None),
        P("blk"),
        P(None, "col"),
        P("col"),
        P("blk", None, None),
        P("blk"),
        P("blk"),
    )
    out_specs = (P("blk"), P("col"))
    return jax.shard_map(
        on_device, mesh=mesh, in_specs=in_specs, out_specs=out_specs, check_vma=False
    )
```

```python
import functools
import math

import jax
import jax.numpy as jnp
import numpy as np
from jax import lax
from jax.experimental import pallas as pl
from jax.experimental.pallas import tpu as pltpu
from jax.sharding import PartitionSpec as P

F32 = jnp.float32
BF16 = jnp.bfloat16
LOG_SHAPE = math.log(1.5)
LINK = 0.4
LANES = 128
MIB = 1024 * 1024


def cosine_table():
    nodes = 0.125 + 0.125 * np.cos(np.pi * (np.arange(400) + 0.5) / 400)
    values = math.sqrt(2.0) * np.cos(2.0 * np.pi * np.sqrt(nodes))
    fit = np.polynomial.chebyshev.Chebyshev.fit(nodes, values, 5, domain=[0.0, 0.25])
    return [float(c) for c in fit.convert(kind=np.polynomial.Polynomial).coef]


COEFS = cosine_table()
PER_TURN = 1.0 / (2.0 * math.pi)


def feature(angles):
    turns = angles * PER_TURN
    turns = turns - jnp.round(turns)
    square = turns * turns
    total = COEFS[-1]
    for coef in COEFS[-2::-1]:
        total = total * square + coef
    return total.astype(BF16)


def split3(value):
    high = value.astype(BF16).astype(F32)
    rest = value - high
    middle = rest.astype(BF16).astype(F32)
    low = (rest - middle).astype(BF16).astype(F32)
    return high, middle, low


def stack_rows(rows, height):
    at = lax.broadcasted_iota(jnp.int32, (height, rows[0].shape[1]), 0)
    total = jnp.zeros((height, rows[0].shape[1]), F32)
    for index, row in enumerate(rows):
        total = jnp.where(at == index, row, total)
    return total.astype(BF16)


def as_row(tiles):
    return jnp.concatenate([tiles[j : j + 1, :] for j in range(tiles.shape[0])], axis=1)


def dot_nt(a, b):
    return lax.dot_general(a, b, (((1,), (1,)), ((), ())), preferred_element_type=F32)


def dot_nn(a, b):
    return jnp.dot(a, b, preferred_element_type=F32)


VMEM = pl.BlockSpec(memory_space=pltpu.VMEM)
SMEM = pl.BlockSpec(memory_space=pltpu.SMEM)
HBM = pl.BlockSpec(memory_space=pltpu.HBM)
PARTS = 2
KEPT = 0.5
SPARE = 9
PHASE_ROWS = 8


def rows_at(index, size):
    return pl.ds(pl.multiple_of(index * size, size), size)


def total_of(x):
    return jnp.sum(jnp.sum(x, axis=0, keepdims=True), axis=1, keepdims=True)


def params(mebibytes=48):
    return pltpu.CompilerParams(vmem_limit_bytes=mebibytes * MIB)


def cost(flops, size, hard=0):
    return pl.CostEstimate(flops=flops, bytes_accessed=size, transcendentals=hard)


def pack_kernel(freq, phase, out, packed, row, sems):
    depth = freq.shape[0]
    loads = [
        pltpu.make_async_copy(freq, packed.at[0:depth], sems.at[0]),
        pltpu.make_async_copy(phase, row, sems.at[1]),
    ]
    for load in loads:
        load.start()
    for load in loads:
        load.wait()
    packed[depth : depth + PHASE_ROWS, :] = jnp.broadcast_to(
        row[...], (PHASE_ROWS, row.shape[1])
    )
    stores = [
        pltpu.make_async_copy(packed, out.at[copy], sems.at[2 + copy])
        for copy in range(out.shape[0])
    ]
    for store in stores:
        store.start()
    for store in stores:
        store.wait()


def stage_kernel(value, out):
    out[...] = value[...]


def stage(value, name):
    return pl.pallas_call(
        stage_kernel,
        in_specs=[VMEM],
        out_specs=VMEM,
        out_shape=jax.ShapeDtypeStruct(value.shape, value.dtype),
        compiler_params=params(),
        cost_estimate=cost(value.size, 4 * value.size),
        name=name,
    )(value)


def feature_block(rows, freq, store):
    depth = rows.shape[1]
    for j in range(0, freq.shape[0], 2):
        both = jnp.concatenate([freq[j, :depth, :], freq[j + 1, :depth, :]], axis=1)
        phase = jnp.concatenate(
            [freq[j, depth : depth + 1, :], freq[j + 1, depth : depth + 1, :]], axis=1
        )
        store(j * LANES, feature(dot_nn(rows, both) + phase.astype(F32)))


FEATURE_ROWS = 256


def half_features(cov, freq, target, base):
    def step(i, carry):
        at = rows_at(i, FEATURE_ROWS)

        def store(column, value):
            target[at, base + column : base + column + value.shape[1]] = value

        feature_block(cov[at, :], freq, store)
        return carry

    lax.fori_loop(0, cov.shape[0] // FEATURE_ROWS, step, 0)


def far_kernel(core, cov, freq, out):
    half_features(cov, freq.at[1 - core[0]], out, 0)


def far_features(core, cov, freq):
    rows, depth = cov.shape
    columns = freq.shape[1] * LANES
    return pl.pallas_call(
        far_kernel,
        in_specs=[SMEM, VMEM, VMEM],
        out_specs=VMEM,
        out_shape=jax.ShapeDtypeStruct((rows, columns), BF16),
        compiler_params=params(),
        cost_estimate=cost(2 * rows * depth * columns + 20 * rows * columns, 2 * rows * columns),
        name="far_features",
    )(core, cov, freq)


def node_kernel(first, core, cov, freq, *rest):
    out, held, sems = rest[-3:]
    half = freq.shape[1] * LANES
    steps = cov.shape[0] // FEATURE_ROWS

    def leave(i):
        at, to = rows_at(i, FEATURE_ROWS), rows_at(i + first // FEATURE_ROWS, FEATURE_ROWS)
        return pltpu.make_async_copy(held.at[at], out.at[to], sems.at[i])

    def step(i, carry):
        at = rows_at(i, FEATURE_ROWS)
        for index in range(2):
            source = core[0] if index == 0 else 1 - core[0]

            def store(column, value, base=index * half):
                held[at, base + column : base + column + value.shape[1]] = value

            feature_block(cov[at, :], freq.at[source], store)
        leave(i).start()
        return carry

    lax.fori_loop(0, steps, step, 0)
    for i in range(steps):
        leave(i).wait()


def node_features(core, cov, freq, before, first, height, name):
    rows, depth = cov.shape
    columns = 2 * freq.shape[1] * LANES
    earlier = () if before is None else (before,)
    return pl.pallas_call(
        functools.partial(node_kernel, first),
        in_specs=[SMEM, VMEM, VMEM] + [HBM] * len(earlier),
        out_specs=HBM,
        out_shape=jax.ShapeDtypeStruct((height, columns), BF16),
        scratch_shapes=[
            pltpu.VMEM((rows, columns), BF16),
            pltpu.SemaphoreType.DMA((rows // FEATURE_ROWS,)),
        ],
        input_output_aliases={3: 0} if earlier else {},
        compiler_params=params(60),
        cost_estimate=cost(2 * rows * depth * columns + 20 * rows * columns, 2 * rows * columns),
        name=name,
    )(core, cov, freq, *earlier)


def near_kernel(
    cov, freq, weight, size, kept, rest_out, out, rest, gathered, tiles, sems
):
    first = kept.shape[0]

    def fill(target, base, count, after=None):
        group = target.shape[0] // count

        def step(i, carry):
            at = rows_at(i, group)

            def store(column, value):
                target[at, column : column + value.shape[1]] = value

            rows = cov[pl.ds(pl.multiple_of(base + i * group, 64), group), :]
            feature_block(rows, freq, store)
            if after is not None:
                after(i, group).start()
            return carry

        lax.fori_loop(0, count, step, 0)

    def leave(i, group):
        at = rows_at(i, group)
        return pltpu.make_async_copy(rest.at[at], rest_out.at[at], sems.at[i])

    fill(rest, first, PARTS, leave)
    fill(kept, 0, PARTS)
    product = weight[...].astype(F32) * size[...].astype(F32)
    split = stack_rows(split3(product), 16)
    gathered[...] = dot_nn(split[:, :first], kept[...]) + dot_nn(split[:, first:], rest[...])
    send_whole(gathered, tiles, out)
    for i in range(PARTS):
        leave(i, rest.shape[0] // PARTS).wait()


def rows_of(vector):
    return stack_rows(split3(as_row(vector)), 16)


def send_whole(gathered, tiles, out):
    total = jnp.sum(gathered[...], axis=0, keepdims=True)
    for j in range(tiles.shape[0]):
        tiles[j : j + 1, :] = total[:, j * LANES : (j + 1) * LANES]
    whole = tiles[...]
    for copy in range(out.shape[0]):
        out[copy] = whole


def fetch(rest, held, sems):
    part = held.shape[0] // PARTS
    copies = []
    for k in range(PARTS):
        at = slice(k * part, (k + 1) * part)
        copy = pltpu.make_async_copy(rest.at[at], held.at[at], sems.at[k])
        copy.start()
        copies.append((at, copy))
    return copies


def forward(direction, kept, held, copies, far):
    split = rows_of(direction)
    half = far.shape[1]
    near = split[:, :half]
    total = jnp.sum(dot_nt(split[:, half:], far[...]), axis=0, keepdims=True)
    values = [jnp.sum(dot_nt(near, kept[...]), axis=0, keepdims=True)]
    for at, copy in copies:
        copy.wait()
        values.append(jnp.sum(dot_nt(near, held[at]), axis=0, keepdims=True))
    return jnp.concatenate(values, axis=1) + total


def product(direction, kept, held, copies, far, weight, staged, tiles, sends, out, scale):
    values = forward(direction, kept, held, copies, far)
    split = stack_rows(split3(weight[...].astype(F32) * values * scale), 16)
    first, layers = kept.shape[0], tiles.shape[0]

    def leave(half, sums):
        total = jnp.sum(sums, axis=0, keepdims=True)
        for j in range(layers):
            tiles[j : j + 1, :] = total[:, j * LANES : (j + 1) * LANES]
        whole = tiles[...]
        for copy in range(out.shape[0]):
            staged[half, copy] = whole
        send = pltpu.make_async_copy(
            staged.at[half], out.at[:, half * layers : (half + 1) * layers], sends.at[half]
        )
        send.start()
        return send

    late = leave(1, dot_nn(split, far[...]))
    near = dot_nn(split[:, :first], kept[...]) + dot_nn(split[:, first:], held[...])
    early = leave(0, near)
    late.wait()
    early.wait()
    return values


def first_kernel(
    scale, rhs_scale, core, halves, kept, rest, far, weight, out, values_out, rhs_out, staged, tiles, sends, held, sems
):
    copies = fetch(rest, held, sems)
    low, high = (jnp.sum(halves[h], axis=0) * rhs_scale for h in range(2))
    swap = core[0] == 1
    half = low.shape[0]
    rhs_out[0:half, :] = jnp.where(swap, high, low)
    rhs_out[half : 2 * half, :] = jnp.where(swap, low, high)
    values_out[...] = product(
        rhs_out[...], kept, held, copies, far, weight, staged, tiles, sends, out, scale
    )


def second_kernel(
    scale, arrived, rhs, before, kept, rest, far, weight,
    out, fit_out, solution_out, residual_out, direction_out,
    staged, tiles, sends, held, sems,
):
    copies = fetch(rest, held, sems)
    direction = rhs[...]
    norm = total_of(direction * direction)
    image = direction + jnp.sum(arrived[...], axis=0)
    length = norm / total_of(direction * image)
    residual = direction - length * image
    later = residual + total_of(residual * residual) / norm * direction
    solution_out[...] = length * direction
    residual_out[...] = residual
    direction_out[...] = later
    fit_out[0:1, :] = length * before[...]
    fit_out[1:2, :] = product(
        later, kept, held, copies, far, weight, staged, tiles, sends, out, scale
    )


def third_kernel(
    scale, fit_scale, arrived, solution, residual, direction, fit, kept, rest, far, weight, size, owner, patient,
    out, both_out, norm_out,
    held, sems,
):
    copies = fetch(rest, held, sems)
    before = direction[...]
    left = residual[...]
    norm = total_of(left * left)
    image = before + jnp.sum(arrived[...], axis=0)
    length = norm / total_of(before * image)
    left = left - length * image
    norm_next = total_of(left * left)
    later = left + norm_next / norm * before
    both_out[0] = solution[...] + length * before
    both_out[1] = later
    norm_out[...] = jnp.broadcast_to(norm_next, norm_out.shape)
    values = forward(later, kept, held, copies, far)
    fitted = fit[0:1, :] + length * fit[1:2, :]
    weights = weight[...].astype(F32)
    weighted = weights * values
    energy = total_of(weighted * values) * scale
    part = weights * (size[...].astype(F32) - fitted * fit_scale)
    owners, patients = out.shape[0], out.shape[2]
    here = values.shape[1]
    to_owner = (owner[...] == lax.broadcasted_iota(jnp.int32, (owners, here), 0)).astype(F32)
    to_patient = (patient[...] == lax.broadcasted_iota(jnp.int32, (patients, here), 0)).astype(F32)
    parts = split3(part) + split3(weighted * fit_scale) + (weights,)
    tall = jnp.concatenate([to_owner * part for part in parts], axis=0).astype(BF16)
    sums = dot_nt(tall, to_patient.astype(BF16))
    part = [sums[i * owners : (i + 1) * owners, :] for i in range(len(parts))]
    out[:, 0, :] = part[0] + part[1] + part[2]
    out[:, 1, :] = part[3] + part[4] + part[5]
    out[:, 2, :] = part[6]
    out[:, 3, :] = jnp.broadcast_to(energy, (owners, patients))


NODE_ROWS = 512


def nodes_kernel(both, phi, out, split):
    @pl.when(pl.program_id(0) == 0)
    def _():
        rows = split3(as_row(both[0])) + split3(as_row(both[1]))
        split[...] = stack_rows(rows, 16)

    products = dot_nt(split[...], phi[...])
    out[0:1, :] = products[0:1] + products[1:2] + products[2:3]
    out[1:2, :] = products[3:4] + products[4:5] + products[5:6]


def last_kernel(fit_scale, mine, arrived, both, norm, node_values, time, flag, loglik, weights_out, tiles):
    sums = jnp.sum(arrived[...], axis=0)
    direction = both[1]
    denominator = total_of(direction * direction) + sums[3:4, 0:1]
    length = norm[0:1, 0:1] / denominator
    tiles[...] = both[0] + length * direction
    weights_out[...] = tiles[pl.ds(mine[0], 1), :]
    effect = (sums[0:1, :] - length * sums[1:2, :]) / (1.0 + sums[2:3, :])
    values = (node_values[0:1, :] + length * node_values[1:2, :]) * fit_scale
    patients = loglik.shape[1]
    nodes = values.shape[1] // patients
    total = jnp.zeros_like(effect)
    eta = total
    when = time[...]
    for q in range(nodes):
        grid = when * (q + 1.0) / nodes
        eta = (
            LOG_SHAPE
            + 0.5 * jnp.log(grid)
            + LINK * (values[:, q * patients : (q + 1) * patients] + effect)
        )
        total = total + jnp.exp(eta)
    loglik[...] = flag[...].astype(F32) * eta - when / nodes * total


def on_device(
    visit_cov,
    tumor_size,
    visit_weight,
    visit_owner,
    visit_patient,
    inducing_freq,
    inducing_phase,
    node_cov,
    event_time,
    event_flag,
):
    blocks, cols = lax.axis_size("blk"), lax.axis_size("col")
    rows, depth = visit_cov.shape
    own = inducing_freq.shape[1]
    inducing = own * cols
    tall = inducing // LANES
    layers = cols // 2
    patients, nodes = node_cov.shape[:2]
    scale = 1.0 / (rows * blocks)
    fit_scale = 1.0 / math.sqrt(inducing)
    weight = visit_weight.reshape(1, rows)
    size = tumor_size.reshape(1, rows)
    owner = visit_owner.reshape(1, rows)
    patient = visit_patient.reshape(1, rows)
    place = lax.axis_index("col").astype(jnp.int32)
    core = (place % 2).reshape(1)
    layer = (place // 2).reshape(1)
    together = lax.optimization_barrier
    same_core = [[2 * z + c for z in range(layers)] for c in range(2)]
    pairs = [[2 * z, 2 * z + 1] for z in range(layers)]

    packed = pl.pallas_call(
        pack_kernel,
        in_specs=[HBM, HBM],
        out_specs=HBM,
        out_shape=jax.ShapeDtypeStruct((layers, depth + PHASE_ROWS, own), BF16),
        scratch_shapes=[
            pltpu.VMEM((depth + PHASE_ROWS, own), BF16),
            pltpu.VMEM((1, own), BF16),
            pltpu.SemaphoreType.DMA((2 + layers,)),
        ],
        compiler_params=params(60),
        name="pack",
    )(inducing_freq, inducing_phase.reshape(1, own))
    packed, cov, turned = together((packed, visit_cov, node_cov))
    near_freq = lax.all_to_all(packed, "col", 0, 0, tiled=True, axis_index_groups=same_core)
    cov = stage(cov, "stage_cov")
    by_node = turned.transpose(1, 0, 2).reshape(nodes * patients, depth)
    count = nodes * patients // 2
    height = (SPARE * nodes * patients) // 4
    node_covs = (by_node[:count], by_node[count:])
    near_freq, cov, node_covs = together((near_freq, cov, node_covs))

    half = inducing // 2
    first = int(rows * KEPT)
    kept, rest, sent = pl.pallas_call(
        near_kernel,
        in_specs=[VMEM] * 4,
        out_specs=[VMEM, HBM, VMEM],
        out_shape=[
            jax.ShapeDtypeStruct((first, half), BF16),
            jax.ShapeDtypeStruct((SPARE * rows, half), BF16),
            jax.ShapeDtypeStruct((blocks, tall // 2, LANES), F32),
        ],
        scratch_shapes=[
            pltpu.VMEM((rows - first, half), BF16),
            pltpu.VMEM((16, half), F32),
            pltpu.VMEM((tall // 2, LANES), F32),
            pltpu.SemaphoreType.DMA((PARTS,)),
        ],
        compiler_params=params(),
        name="near_features",
    )(cov, near_freq, weight, size)
    sent, late_freq = together((sent, near_freq))
    arrived = lax.all_to_all(sent, "blk", 0, 0, tiled=True)
    freq = lax.all_gather(late_freq, "col", axis_index_groups=pairs)
    far = far_features(core, cov, freq)
    arrived, far = together((arrived, far))
    halves = lax.all_gather(arrived, "col", axis_index_groups=pairs)

    message = pltpu.HBM((blocks, tall, LANES), F32)
    vector = jax.ShapeDtypeStruct((tall, LANES), F32)
    fetched = [pltpu.VMEM((rows - first, half), BF16), pltpu.SemaphoreType.DMA((PARTS,))]
    scratch = [
        pltpu.VMEM((2, blocks, tall // 2, LANES), F32),
        pltpu.VMEM((tall // 2, LANES), F32),
        pltpu.SemaphoreType.DMA((2,)),
    ] + fetched
    work = cost(64 * rows * inducing, 2 * rows * inducing)

    sent, before, rhs = pl.pallas_call(
        functools.partial(first_kernel, scale, 1.0 / math.sqrt(rows * blocks)),
        in_specs=[SMEM, VMEM, VMEM, HBM, VMEM, VMEM],
        out_specs=[HBM, VMEM, VMEM],
        out_shape=[message, jax.ShapeDtypeStruct((1, rows), F32), vector],
        scratch_shapes=scratch,
        compiler_params=params(),
        cost_estimate=work,
        name="first_product",
    )(core, halves, kept, rest, far, weight)
    sent, node_cov_now = together((sent, node_covs[0]))
    arrived = lax.all_to_all(sent, "blk", 0, 0, tiled=True)
    node_phi = node_features(core, node_cov_now, freq, None, 0, height, "node_features_a")
    arrived, node_phi = together((arrived, node_phi))

    sent, fit, solution, residual, direction = pl.pallas_call(
        functools.partial(second_kernel, scale),
        in_specs=[VMEM] * 4 + [HBM, VMEM, VMEM],
        out_specs=[HBM] + [VMEM] * 4,
        out_shape=[message, jax.ShapeDtypeStruct((2, rows), F32), vector, vector, vector],
        scratch_shapes=scratch,
        compiler_params=params(),
        cost_estimate=work,
        name="second_product",
    )(arrived, rhs, before, kept, rest, far, weight)
    sent, node_cov_now = together((sent, node_covs[1]))
    arrived = lax.all_to_all(sent, "blk", 0, 0, tiled=True)
    node_phi = node_features(core, node_cov_now, freq, node_phi, count, height, "node_features_b")
    arrived, node_phi = together((arrived, node_phi))

    sent, both, norm = pl.pallas_call(
        functools.partial(third_kernel, scale, fit_scale),
        in_specs=[VMEM] * 6 + [HBM] + [VMEM] * 5,
        out_specs=[VMEM] * 3,
        out_shape=[
            jax.ShapeDtypeStruct((blocks, 4, patients), F32),
            jax.ShapeDtypeStruct((2, tall, LANES), F32),
            jax.ShapeDtypeStruct((8, LANES), F32),
        ],
        scratch_shapes=fetched,
        compiler_params=params(),
        cost_estimate=work,
        name="third_product",
    )(arrived, solution, residual, direction, fit, kept, rest, far, weight, size, owner, patient)
    sent, both = together((sent, both))
    arrived = lax.all_to_all(sent, "blk", 0, 0, tiled=True)
    node_values = pl.pallas_call(
        nodes_kernel,
        grid=(2 * count // NODE_ROWS,),
        in_specs=[
            pl.BlockSpec(both.shape, lambda i: (0, 0, 0)),
            pl.BlockSpec((NODE_ROWS, inducing), lambda i: (i, 0)),
        ],
        out_specs=pl.BlockSpec((2, NODE_ROWS), lambda i: (0, i)),
        out_shape=jax.ShapeDtypeStruct((2, 2 * count), F32),
        scratch_shapes=[pltpu.VMEM((16, inducing), BF16)],
        compiler_params=params(),
        cost_estimate=cost(64 * 2 * count * inducing, 4 * count * inducing),
        name="node_values",
    )(both, node_phi)
    arrived, node_values = together((arrived, node_values))

    loglik, weights = pl.pallas_call(
        functools.partial(last_kernel, fit_scale),
        in_specs=[SMEM] + [VMEM] * 6,
        out_specs=[VMEM, VMEM],
        out_shape=[
            jax.ShapeDtypeStruct((1, patients), F32),
            jax.ShapeDtypeStruct((1, own), F32),
        ],
        scratch_shapes=[pltpu.VMEM((tall, LANES), F32)],
        compiler_params=params(),
        name="last",
    )(
        layer,
        arrived,
        both,
        norm,
        node_values,
        event_time.reshape(1, patients),
        event_flag.reshape(1, patients),
    )
    return loglik.reshape(patients), weights.reshape(own)


def solution(mesh):
    in_specs = (
        P("blk", None),
        P("blk"),
        P("blk"),
        P("blk", None),
        P("blk"),
        P(None, "col"),
        P("col"),
        P("blk", None, None),
        P("blk"),
        P("blk"),
    )
    out_specs = (P("blk"), P("col"))
    return jax.shard_map(
        on_device, mesh=mesh, in_specs=in_specs, out_specs=out_specs, check_vma=False
    )
```

```python
import functools
import math

import jax
import jax.numpy as jnp
import numpy as np
from jax import lax
from jax.experimental import pallas as pl
from jax.experimental.pallas import tpu as pltpu
from jax.sharding import PartitionSpec as P

F32 = jnp.float32
BF16 = jnp.bfloat16
LOG_SHAPE = math.log(1.5)
LINK = 0.4
LANES = 128
MIB = 1024 * 1024


def cosine_table():
    nodes = 0.125 + 0.125 * np.cos(np.pi * (np.arange(400) + 0.5) / 400)
    values = math.sqrt(2.0) * np.cos(2.0 * np.pi * np.sqrt(nodes))
    fit = np.polynomial.chebyshev.Chebyshev.fit(nodes, values, 5, domain=[0.0, 0.25])
    return [float(c) for c in fit.convert(kind=np.polynomial.Polynomial).coef]


COEFS = cosine_table()
PER_TURN = 1.0 / (2.0 * math.pi)


def feature(angles):
    turns = angles * PER_TURN
    turns = turns - jnp.round(turns)
    square = turns * turns
    total = COEFS[-1]
    for coef in COEFS[-2::-1]:
        total = total * square + coef
    return total.astype(BF16)


def split3(value):
    high = value.astype(BF16).astype(F32)
    rest = value - high
    middle = rest.astype(BF16).astype(F32)
    low = (rest - middle).astype(BF16).astype(F32)
    return high, middle, low


def stack_rows(rows, height):
    at = lax.broadcasted_iota(jnp.int32, (height, rows[0].shape[1]), 0)
    total = jnp.zeros((height, rows[0].shape[1]), F32)
    for index, row in enumerate(rows):
        total = jnp.where(at == index, row, total)
    return total.astype(BF16)


def as_row(tiles):
    return jnp.concatenate([tiles[j : j + 1, :] for j in range(tiles.shape[0])], axis=1)


def dot_nt(a, b):
    return lax.dot_general(a, b, (((1,), (1,)), ((), ())), preferred_element_type=F32)


def dot_nn(a, b):
    return jnp.dot(a, b, preferred_element_type=F32)


VMEM = pl.BlockSpec(memory_space=pltpu.VMEM)
SMEM = pl.BlockSpec(memory_space=pltpu.SMEM)
HBM = pl.BlockSpec(memory_space=pltpu.HBM)
PARTS = 2
KEPT = 0.5
SPARE = 9
PHASE_ROWS = 8


def rows_at(index, size):
    return pl.ds(pl.multiple_of(index * size, size), size)


def total_of(x):
    return jnp.sum(jnp.sum(x, axis=0, keepdims=True), axis=1, keepdims=True)


def params(mebibytes=48):
    return pltpu.CompilerParams(vmem_limit_bytes=mebibytes * MIB)


def cost(flops, size, hard=0):
    return pl.CostEstimate(flops=flops, bytes_accessed=size, transcendentals=hard)


def pack_kernel(freq, phase, out, packed, row, sems):
    depth = freq.shape[0]
    loads = [
        pltpu.make_async_copy(freq, packed.at[0:depth], sems.at[0]),
        pltpu.make_async_copy(phase, row, sems.at[1]),
    ]
    for load in loads:
        load.start()
    for load in loads:
        load.wait()
    packed[depth : depth + PHASE_ROWS, :] = jnp.broadcast_to(
        row[...], (PHASE_ROWS, row.shape[1])
    )
    stores = [
        pltpu.make_async_copy(packed, out.at[copy], sems.at[2 + copy])
        for copy in range(out.shape[0])
    ]
    for store in stores:
        store.start()
    for store in stores:
        store.wait()


def stage_kernel(value, out):
    out[...] = value[...]


def stage(value, name):
    return pl.pallas_call(
        stage_kernel,
        in_specs=[VMEM],
        out_specs=VMEM,
        out_shape=jax.ShapeDtypeStruct(value.shape, value.dtype),
        compiler_params=params(),
        cost_estimate=cost(value.size, 4 * value.size),
        name=name,
    )(value)


def feature_block(rows, freq, store):
    depth = rows.shape[1]
    for j in range(0, freq.shape[0], 2):
        both = jnp.concatenate([freq[j, :depth, :], freq[j + 1, :depth, :]], axis=1)
        phase = jnp.concatenate(
            [freq[j, depth : depth + 1, :], freq[j + 1, depth : depth + 1, :]], axis=1
        )
        store(j * LANES, feature(dot_nn(rows, both) + phase.astype(F32)))


FEATURE_ROWS = 256


def half_features(cov, freq, target, base):
    def step(i, carry):
        at = rows_at(i, FEATURE_ROWS)

        def store(column, value):
            target[at, base + column : base + column + value.shape[1]] = value

        feature_block(cov[at, :], freq, store)
        return carry

    lax.fori_loop(0, cov.shape[0] // FEATURE_ROWS, step, 0)


def far_kernel(core, cov, freq, out):
    half_features(cov, freq.at[1 - core[0]], out, 0)


def far_features(core, cov, freq):
    rows, depth = cov.shape
    columns = freq.shape[1] * LANES
    return pl.pallas_call(
        far_kernel,
        in_specs=[SMEM, VMEM, VMEM],
        out_specs=VMEM,
        out_shape=jax.ShapeDtypeStruct((rows, columns), BF16),
        compiler_params=params(),
        cost_estimate=cost(2 * rows * depth * columns + 20 * rows * columns, 2 * rows * columns),
        name="far_features",
    )(core, cov, freq)


def node_kernel(first, core, cov, freq, *rest):
    out, held, sems = rest[-3:]
    half = freq.shape[1] * LANES
    steps = cov.shape[0] // FEATURE_ROWS

    def leave(i):
        at, to = rows_at(i, FEATURE_ROWS), rows_at(i + first // FEATURE_ROWS, FEATURE_ROWS)
        return pltpu.make_async_copy(held.at[at], out.at[to], sems.at[i])

    def step(i, carry):
        at = rows_at(i, FEATURE_ROWS)
        for index in range(2):
            source = core[0] if index == 0 else 1 - core[0]

            def store(column, value, base=index * half):
                held[at, base + column : base + column + value.shape[1]] = value

            feature_block(cov[at, :], freq.at[source], store)
        leave(i).start()
        return carry

    lax.fori_loop(0, steps, step, 0)
    for i in range(steps):
        leave(i).wait()


def node_features(core, cov, freq, before, first, height, name):
    rows, depth = cov.shape
    columns = 2 * freq.shape[1] * LANES
    earlier = () if before is None else (before,)
    return pl.pallas_call(
        functools.partial(node_kernel, first),
        in_specs=[SMEM, VMEM, VMEM] + [HBM] * len(earlier),
        out_specs=HBM,
        out_shape=jax.ShapeDtypeStruct((height, columns), BF16),
        scratch_shapes=[
            pltpu.VMEM((rows, columns), BF16),
            pltpu.SemaphoreType.DMA((rows // FEATURE_ROWS,)),
        ],
        input_output_aliases={3: 0} if earlier else {},
        compiler_params=params(60),
        cost_estimate=cost(2 * rows * depth * columns + 20 * rows * columns, 2 * rows * columns),
        name=name,
    )(core, cov, freq, *earlier)


def near_kernel(
    cov, freq, weight, size, kept, rest_out, out, rest, gathered, tiles, sems
):
    first = kept.shape[0]

    def fill(target, base, count, after=None):
        group = target.shape[0] // count

        def step(i, carry):
            at = rows_at(i, group)

            def store(column, value):
                target[at, column : column + value.shape[1]] = value

            rows = cov[pl.ds(pl.multiple_of(base + i * group, 64), group), :]
            feature_block(rows, freq, store)
            if after is not None:
                after(i, group).start()
            return carry

        lax.fori_loop(0, count, step, 0)

    def leave(i, group):
        at = rows_at(i, group)
        return pltpu.make_async_copy(rest.at[at], rest_out.at[at], sems.at[i])

    fill(rest, first, PARTS, leave)
    fill(kept, 0, PARTS)
    product = weight[...].astype(F32) * size[...].astype(F32)
    split = stack_rows(split3(product), 16)
    gathered[...] = dot_nn(split[:, :first], kept[...]) + dot_nn(split[:, first:], rest[...])
    send_whole(gathered, tiles, out)
    for i in range(PARTS):
        leave(i, rest.shape[0] // PARTS).wait()


def rows_of(vector):
    return stack_rows(split3(as_row(vector)), 16)


def send_whole(gathered, tiles, out):
    total = jnp.sum(gathered[...], axis=0, keepdims=True)
    for j in range(tiles.shape[0]):
        tiles[j : j + 1, :] = total[:, j * LANES : (j + 1) * LANES]
    whole = tiles[...]
    for copy in range(out.shape[0]):
        out[copy] = whole


def fetch(rest, held, sems):
    part = held.shape[0] // PARTS
    copies = []
    for k in range(PARTS):
        at = slice(k * part, (k + 1) * part)
        copy = pltpu.make_async_copy(rest.at[at], held.at[at], sems.at[k])
        copy.start()
        copies.append((at, copy))
    return copies


def forward(direction, kept, held, copies, far):
    split = rows_of(direction)
    half = far.shape[1]
    near = split[:, :half]
    total = jnp.sum(dot_nt(split[:, half:], far[...]), axis=0, keepdims=True)
    values = [jnp.sum(dot_nt(near, kept[...]), axis=0, keepdims=True)]
    for at, copy in copies:
        copy.wait()
        values.append(jnp.sum(dot_nt(near, held[at]), axis=0, keepdims=True))
    return jnp.concatenate(values, axis=1) + total


def product(direction, kept, held, copies, far, weight, gathered, tiles, out, scale):
    values = forward(direction, kept, held, copies, far)
    split = stack_rows(split3(weight[...].astype(F32) * values * scale), 16)
    half, first = far.shape[1], kept.shape[0]
    gathered[:, half:] = dot_nn(split, far[...])
    gathered[:, :half] = dot_nn(split[:, :first], kept[...]) + dot_nn(split[:, first:], held[...])
    send_whole(gathered, tiles, out)
    return values


def first_kernel(
    scale, rhs_scale, core, halves, kept, rest, far, weight, out, values_out, rhs_out, gathered, tiles, held, sems
):
    copies = fetch(rest, held, sems)
    low, high = (jnp.sum(halves[h], axis=0) * rhs_scale for h in range(2))
    swap = core[0] == 1
    half = low.shape[0]
    rhs_out[0:half, :] = jnp.where(swap, high, low)
    rhs_out[half : 2 * half, :] = jnp.where(swap, low, high)
    values_out[...] = product(
        rhs_out[...], kept, held, copies, far, weight, gathered, tiles, out, scale
    )


def second_kernel(
    scale, arrived, rhs, before, kept, rest, far, weight,
    out, fit_out, solution_out, residual_out, direction_out,
    gathered, tiles, held, sems,
):
    copies = fetch(rest, held, sems)
    direction = rhs[...]
    norm = total_of(direction * direction)
    image = direction + jnp.sum(arrived[...], axis=0)
    length = norm / total_of(direction * image)
    residual = direction - length * image
    later = residual + total_of(residual * residual) / norm * direction
    solution_out[...] = length * direction
    residual_out[...] = residual
    direction_out[...] = later
    fit_out[0:1, :] = length * before[...]
    fit_out[1:2, :] = product(
        later, kept, held, copies, far, weight, gathered, tiles, out, scale
    )


def third_kernel(
    scale, fit_scale, arrived, solution, residual, direction, fit, kept, rest, far, weight, size, owner, patient,
    out, both_out, norm_out,
    held, sems,
):
    copies = fetch(rest, held, sems)
    before = direction[...]
    left = residual[...]
    norm = total_of(left * left)
    image = before + jnp.sum(arrived[...], axis=0)
    length = norm / total_of(before * image)
    left = left - length * image
    norm_next = total_of(left * left)
    later = left + norm_next / norm * before
    both_out[0] = solution[...] + length * before
    both_out[1] = later
    norm_out[...] = jnp.broadcast_to(norm_next, norm_out.shape)
    values = forward(later, kept, held, copies, far)
    fitted = fit[0:1, :] + length * fit[1:2, :]
    weights = weight[...].astype(F32)
    weighted = weights * values
    energy = total_of(weighted * values) * scale
    part = weights * (size[...].astype(F32) - fitted * fit_scale)
    owners, patients = out.shape[0], out.shape[2]
    here = values.shape[1]
    to_owner = (owner[...] == lax.broadcasted_iota(jnp.int32, (owners, here), 0)).astype(F32)
    to_patient = (patient[...] == lax.broadcasted_iota(jnp.int32, (patients, here), 0)).astype(F32)
    parts = split3(part) + split3(weighted * fit_scale) + (weights,)
    tall = jnp.concatenate([to_owner * part for part in parts], axis=0).astype(BF16)
    sums = dot_nt(tall, to_patient.astype(BF16))
    part = [sums[i * owners : (i + 1) * owners, :] for i in range(len(parts))]
    out[:, 0, :] = part[0] + part[1] + part[2]
    out[:, 1, :] = part[3] + part[4] + part[5]
    out[:, 2, :] = part[6]
    out[:, 3, :] = jnp.broadcast_to(energy, (owners, patients))


NODE_ROWS = 512


def nodes_kernel(both, phi, out, split):
    @pl.when(pl.program_id(0) == 0)
    def _():
        rows = split3(as_row(both[0])) + split3(as_row(both[1]))
        split[...] = stack_rows(rows, 16)

    products = dot_nt(split[...], phi[...])
    out[0:1, :] = products[0:1] + products[1:2] + products[2:3]
    out[1:2, :] = products[3:4] + products[4:5] + products[5:6]


def last_kernel(fit_scale, mine, arrived, both, norm, node_values, time, flag, loglik, weights_out, tiles):
    sums = jnp.sum(arrived[...], axis=0)
    direction = both[1]
    denominator = total_of(direction * direction) + sums[3:4, 0:1]
    length = norm[0:1, 0:1] / denominator
    tiles[...] = both[0] + length * direction
    weights_out[...] = tiles[pl.ds(mine[0], 1), :]
    effect = (sums[0:1, :] - length * sums[1:2, :]) / (1.0 + sums[2:3, :])
    halves = [node_values[h, 0:1, :] + length * node_values[h, 1:2, :] for h in range(2)]
    values = jnp.concatenate(halves, axis=1) * fit_scale
    patients = loglik.shape[1]
    nodes = values.shape[1] // patients
    total = jnp.zeros_like(effect)
    eta = total
    when = time[...]
    for q in range(nodes):
        grid = when * (q + 1.0) / nodes
        eta = (
            LOG_SHAPE
            + 0.5 * jnp.log(grid)
            + LINK * (values[:, q * patients : (q + 1) * patients] + effect)
        )
        total = total + jnp.exp(eta)
    loglik[...] = flag[...].astype(F32) * eta - when / nodes * total


def on_device(
    visit_cov,
    tumor_size,
    visit_weight,
    visit_owner,
    visit_patient,
    inducing_freq,
    inducing_phase,
    node_cov,
    event_time,
    event_flag,
):
    blocks, cols = lax.axis_size("blk"), lax.axis_size("col")
    rows, depth = visit_cov.shape
    own = inducing_freq.shape[1]
    inducing = own * cols
    tall = inducing // LANES
    layers = cols // 2
    patients, nodes = node_cov.shape[:2]
    scale = 1.0 / (rows * blocks)
    fit_scale = 1.0 / math.sqrt(inducing)
    weight = visit_weight.reshape(1, rows)
    size = tumor_size.reshape(1, rows)
    owner = visit_owner.reshape(1, rows)
    patient = visit_patient.reshape(1, rows)
    place = lax.axis_index("col").astype(jnp.int32)
    core = (place % 2).reshape(1)
    layer = (place // 2).reshape(1)
    together = lax.optimization_barrier
    same_core = [[2 * z + c for z in range(layers)] for c in range(2)]
    pairs = [[2 * z, 2 * z + 1] for z in range(layers)]

    packed = pl.pallas_call(
        pack_kernel,
        in_specs=[HBM, HBM],
        out_specs=HBM,
        out_shape=jax.ShapeDtypeStruct((layers, depth + PHASE_ROWS, own), BF16),
        scratch_shapes=[
            pltpu.VMEM((depth + PHASE_ROWS, own), BF16),
            pltpu.VMEM((1, own), BF16),
            pltpu.SemaphoreType.DMA((2 + layers,)),
        ],
        compiler_params=params(60),
        name="pack",
    )(inducing_freq, inducing_phase.reshape(1, own))
    packed, cov, turned = together((packed, visit_cov, node_cov))
    near_freq = lax.all_to_all(packed, "col", 0, 0, tiled=True, axis_index_groups=same_core)
    cov = stage(cov, "stage_cov")
    by_node = turned.transpose(1, 0, 2).reshape(nodes * patients, depth)
    count = nodes * patients // 2
    height = (SPARE * nodes * patients) // 4
    by_node = lax.dynamic_slice_in_dim(by_node, core[0] * count, count, 0)
    near_freq, cov, by_node = together((near_freq, cov, by_node))

    half = inducing // 2
    first = int(rows * KEPT)
    kept, rest, sent = pl.pallas_call(
        near_kernel,
        in_specs=[VMEM] * 4,
        out_specs=[VMEM, HBM, VMEM],
        out_shape=[
            jax.ShapeDtypeStruct((first, half), BF16),
            jax.ShapeDtypeStruct((SPARE * rows, half), BF16),
            jax.ShapeDtypeStruct((blocks, tall // 2, LANES), F32),
        ],
        scratch_shapes=[
            pltpu.VMEM((rows - first, half), BF16),
            pltpu.VMEM((16, half), F32),
            pltpu.VMEM((tall // 2, LANES), F32),
            pltpu.SemaphoreType.DMA((PARTS,)),
        ],
        compiler_params=params(),
        name="near_features",
    )(cov, near_freq, weight, size)
    sent, late_freq = together((sent, near_freq))
    arrived = lax.all_to_all(sent, "blk", 0, 0, tiled=True)
    freq = lax.all_gather(late_freq, "col", axis_index_groups=pairs)
    far = far_features(core, cov, freq)
    arrived, far = together((arrived, far))
    halves = lax.all_gather(arrived, "col", axis_index_groups=pairs)

    message = jax.ShapeDtypeStruct((blocks, tall, LANES), F32)
    vector = jax.ShapeDtypeStruct((tall, LANES), F32)
    fetched = [pltpu.VMEM((rows - first, half), BF16), pltpu.SemaphoreType.DMA((PARTS,))]
    scratch = [pltpu.VMEM((16, inducing), F32), pltpu.VMEM((tall, LANES), F32)] + fetched
    work = cost(64 * rows * inducing, 2 * rows * inducing)

    sent, before, rhs = pl.pallas_call(
        functools.partial(first_kernel, scale, 1.0 / math.sqrt(rows * blocks)),
        in_specs=[SMEM, VMEM, VMEM, HBM, VMEM, VMEM],
        out_specs=[VMEM] * 3,
        out_shape=[message, jax.ShapeDtypeStruct((1, rows), F32), vector],
        scratch_shapes=scratch,
        compiler_params=params(),
        cost_estimate=work,
        name="first_product",
    )(core, halves, kept, rest, far, weight)
    sent, node_cov_now = together((sent, by_node))
    arrived = lax.all_to_all(sent, "blk", 0, 0, tiled=True)
    node_phi = node_features(core, node_cov_now, freq, None, 0, height, "node_features_a")
    arrived, node_phi = together((arrived, node_phi))

    sent, fit, solution, residual, direction = pl.pallas_call(
        functools.partial(second_kernel, scale),
        in_specs=[VMEM] * 4 + [HBM, VMEM, VMEM],
        out_specs=[VMEM] * 5,
        out_shape=[message, jax.ShapeDtypeStruct((2, rows), F32), vector, vector, vector],
        scratch_shapes=scratch,
        compiler_params=params(),
        cost_estimate=work,
        name="second_product",
    )(arrived, rhs, before, kept, rest, far, weight)
    arrived = lax.all_to_all(sent, "blk", 0, 0, tiled=True)
    sent, both, norm = pl.pallas_call(
        functools.partial(third_kernel, scale, fit_scale),
        in_specs=[VMEM] * 6 + [HBM] + [VMEM] * 5,
        out_specs=[VMEM] * 3,
        out_shape=[
            jax.ShapeDtypeStruct((blocks, 4, patients), F32),
            jax.ShapeDtypeStruct((2, tall, LANES), F32),
            jax.ShapeDtypeStruct((8, LANES), F32),
        ],
        scratch_shapes=fetched,
        compiler_params=params(),
        cost_estimate=work,
        name="third_product",
    )(arrived, solution, residual, direction, fit, kept, rest, far, weight, size, owner, patient)
    sent, both = together((sent, both))
    arrived = lax.all_to_all(sent, "blk", 0, 0, tiled=True)
    node_values = pl.pallas_call(
        nodes_kernel,
        grid=(count // NODE_ROWS,),
        in_specs=[
            pl.BlockSpec(both.shape, lambda i: (0, 0, 0)),
            pl.BlockSpec((NODE_ROWS, inducing), lambda i: (i, 0)),
        ],
        out_specs=pl.BlockSpec((2, NODE_ROWS), lambda i: (0, i)),
        out_shape=jax.ShapeDtypeStruct((2, count), F32),
        scratch_shapes=[pltpu.VMEM((16, inducing), BF16)],
        compiler_params=params(),
        cost_estimate=cost(64 * 2 * count * inducing, 4 * count * inducing),
        name="node_values",
    )(both, node_phi)
    node_values = lax.all_gather(node_values, "col", axis_index_groups=pairs)
    arrived, node_values = together((arrived, node_values))

    loglik, weights = pl.pallas_call(
        functools.partial(last_kernel, fit_scale),
        in_specs=[SMEM] + [VMEM] * 6,
        out_specs=[VMEM, VMEM],
        out_shape=[
            jax.ShapeDtypeStruct((1, patients), F32),
            jax.ShapeDtypeStruct((1, own), F32),
        ],
        scratch_shapes=[pltpu.VMEM((tall, LANES), F32)],
        compiler_params=params(),
        name="last",
    )(
        layer,
        arrived,
        both,
        norm,
        node_values,
        event_time.reshape(1, patients),
        event_flag.reshape(1, patients),
    )
    return loglik.reshape(patients), weights.reshape(own)


def solution(mesh):
    in_specs = (
        P("blk", None),
        P("blk"),
        P("blk"),
        P("blk", None),
        P("blk"),
        P(None, "col"),
        P("col"),
        P("blk", None, None),
        P("blk"),
        P("blk"),
    )
    out_specs = (P("blk"), P("col"))
    return jax.shard_map(
        on_device, mesh=mesh, in_specs=in_specs, out_specs=out_specs, check_vma=False
    )
```

```python
import functools
import math

import jax
import jax.numpy as jnp
import numpy as np
from jax import lax
from jax.experimental import pallas as pl
from jax.experimental.pallas import tpu as pltpu
from jax.sharding import PartitionSpec as P

F32 = jnp.float32
BF16 = jnp.bfloat16
LOG_SHAPE = math.log(1.5)
LINK = 0.4
LANES = 128
MIB = 1024 * 1024


def cosine_table():
    nodes = 0.125 + 0.125 * np.cos(np.pi * (np.arange(400) + 0.5) / 400)
    values = math.sqrt(2.0) * np.cos(2.0 * np.pi * np.sqrt(nodes))
    fit = np.polynomial.chebyshev.Chebyshev.fit(nodes, values, 5, domain=[0.0, 0.25])
    return [float(c) for c in fit.convert(kind=np.polynomial.Polynomial).coef]


COEFS = cosine_table()
PER_TURN = 1.0 / (2.0 * math.pi)


def feature(angles):
    turns = angles * PER_TURN
    turns = turns - jnp.round(turns)
    square = turns * turns
    total = COEFS[-1]
    for coef in COEFS[-2::-1]:
        total = total * square + coef
    return total.astype(BF16)


def split3(value):
    high = value.astype(BF16).astype(F32)
    rest = value - high
    middle = rest.astype(BF16).astype(F32)
    low = (rest - middle).astype(BF16).astype(F32)
    return high, middle, low


def stack_rows(rows, height):
    at = lax.broadcasted_iota(jnp.int32, (height, rows[0].shape[1]), 0)
    total = jnp.zeros((height, rows[0].shape[1]), F32)
    for index, row in enumerate(rows):
        total = jnp.where(at == index, row, total)
    return total.astype(BF16)


def as_row(tiles):
    return jnp.concatenate([tiles[j : j + 1, :] for j in range(tiles.shape[0])], axis=1)


def dot_nt(a, b):
    return lax.dot_general(a, b, (((1,), (1,)), ((), ())), preferred_element_type=F32)


def dot_nn(a, b):
    return jnp.dot(a, b, preferred_element_type=F32)


VMEM = pl.BlockSpec(memory_space=pltpu.VMEM)
SMEM = pl.BlockSpec(memory_space=pltpu.SMEM)
HBM = pl.BlockSpec(memory_space=pltpu.HBM)
PARTS = 2
KEPT = 0.5
SPARE = 9
PHASE_ROWS = 8


def rows_at(index, size):
    return pl.ds(pl.multiple_of(index * size, size), size)


def total_of(x):
    return jnp.sum(jnp.sum(x, axis=0, keepdims=True), axis=1, keepdims=True)


def params(mebibytes=48):
    return pltpu.CompilerParams(vmem_limit_bytes=mebibytes * MIB)


def cost(flops, size, hard=0):
    return pl.CostEstimate(flops=flops, bytes_accessed=size, transcendentals=hard)


def pack_kernel(freq, phase, out, packed, row, sems):
    depth = freq.shape[0]
    loads = [
        pltpu.make_async_copy(freq, packed.at[0:depth], sems.at[0]),
        pltpu.make_async_copy(phase, row, sems.at[1]),
    ]
    for load in loads:
        load.start()
    for load in loads:
        load.wait()
    packed[depth : depth + PHASE_ROWS, :] = jnp.broadcast_to(
        row[...], (PHASE_ROWS, row.shape[1])
    )
    stores = [
        pltpu.make_async_copy(packed, out.at[copy], sems.at[2 + copy])
        for copy in range(out.shape[0])
    ]
    for store in stores:
        store.start()
    for store in stores:
        store.wait()


def stage_kernel(value, out):
    out[...] = value[...]


def stage(value, name):
    return pl.pallas_call(
        stage_kernel,
        in_specs=[VMEM],
        out_specs=VMEM,
        out_shape=jax.ShapeDtypeStruct(value.shape, value.dtype),
        compiler_params=params(),
        cost_estimate=cost(value.size, 4 * value.size),
        name=name,
    )(value)


def feature_block(rows, freq, store):
    depth = rows.shape[1]
    for j in range(0, freq.shape[0], 2):
        both = jnp.concatenate([freq[j, :depth, :], freq[j + 1, :depth, :]], axis=1)
        phase = jnp.concatenate(
            [freq[j, depth : depth + 1, :], freq[j + 1, depth : depth + 1, :]], axis=1
        )
        store(j * LANES, feature(dot_nn(rows, both) + phase.astype(F32)))


FEATURE_ROWS = 256


def half_features(cov, freq, target, base):
    def step(i, carry):
        at = rows_at(i, FEATURE_ROWS)

        def store(column, value):
            target[at, base + column : base + column + value.shape[1]] = value

        feature_block(cov[at, :], freq, store)
        return carry

    lax.fori_loop(0, cov.shape[0] // FEATURE_ROWS, step, 0)


def far_kernel(core, cov, freq, out):
    half_features(cov, freq.at[1 - core[0]], out, 0)


def far_features(core, cov, freq):
    rows, depth = cov.shape
    columns = freq.shape[1] * LANES
    return pl.pallas_call(
        far_kernel,
        in_specs=[SMEM, VMEM, VMEM],
        out_specs=VMEM,
        out_shape=jax.ShapeDtypeStruct((rows, columns), BF16),
        compiler_params=params(),
        cost_estimate=cost(2 * rows * depth * columns + 20 * rows * columns, 2 * rows * columns),
        name="far_features",
    )(core, cov, freq)


def node_kernel(first, core, cov, freq, *rest):
    out, held, sems = rest[-3:]
    half = freq.shape[1] * LANES
    steps = cov.shape[0] // FEATURE_ROWS

    def leave(i):
        at, to = rows_at(i, FEATURE_ROWS), rows_at(i + first // FEATURE_ROWS, FEATURE_ROWS)
        return pltpu.make_async_copy(held.at[at], out.at[to], sems.at[i])

    def step(i, carry):
        at = rows_at(i, FEATURE_ROWS)
        for index in range(2):
            source = core[0] if index == 0 else 1 - core[0]

            def store(column, value, base=index * half):
                held[at, base + column : base + column + value.shape[1]] = value

            feature_block(cov[at, :], freq.at[source], store)
        leave(i).start()
        return carry

    lax.fori_loop(0, steps, step, 0)
    for i in range(steps):
        leave(i).wait()


def node_features(core, cov, freq, before, first, height, name):
    rows, depth = cov.shape
    columns = 2 * freq.shape[1] * LANES
    earlier = () if before is None else (before,)
    return pl.pallas_call(
        functools.partial(node_kernel, first),
        in_specs=[SMEM, VMEM, VMEM] + [HBM] * len(earlier),
        out_specs=HBM,
        out_shape=jax.ShapeDtypeStruct((height, columns), BF16),
        scratch_shapes=[
            pltpu.VMEM((rows, columns), BF16),
            pltpu.SemaphoreType.DMA((rows // FEATURE_ROWS,)),
        ],
        input_output_aliases={3: 0} if earlier else {},
        compiler_params=params(60),
        cost_estimate=cost(2 * rows * depth * columns + 20 * rows * columns, 2 * rows * columns),
        name=name,
    )(core, cov, freq, *earlier)


def near_kernel(
    cov, freq, weight, size, kept, rest_out, out, rest, gathered, tiles, sems
):
    first = kept.shape[0]

    def fill(target, base, count, after=None):
        group = target.shape[0] // count

        def step(i, carry):
            at = rows_at(i, group)

            def store(column, value):
                target[at, column : column + value.shape[1]] = value

            rows = cov[pl.ds(pl.multiple_of(base + i * group, 64), group), :]
            feature_block(rows, freq, store)
            if after is not None:
                after(i, group).start()
            return carry

        lax.fori_loop(0, count, step, 0)

    def leave(i, group):
        at = rows_at(i, group)
        return pltpu.make_async_copy(rest.at[at], rest_out.at[at], sems.at[i])

    fill(rest, first, PARTS, leave)
    fill(kept, 0, PARTS)
    product = weight[...].astype(F32) * size[...].astype(F32)
    split = stack_rows(split3(product), 16)
    gathered[...] = dot_nn(split[:, :first], kept[...]) + dot_nn(split[:, first:], rest[...])
    send_whole(gathered, tiles, out)
    for i in range(PARTS):
        leave(i, rest.shape[0] // PARTS).wait()


def rows_of(vector):
    return stack_rows(split3(as_row(vector)), 16)


def send_whole(gathered, tiles, out):
    total = jnp.sum(gathered[...], axis=0, keepdims=True)
    for j in range(tiles.shape[0]):
        tiles[j : j + 1, :] = total[:, j * LANES : (j + 1) * LANES]
    whole = tiles[...]
    for copy in range(out.shape[0]):
        out[copy] = whole


def fetch(rest, held, sems):
    part = held.shape[0]
    copies = []
    for k in range(1):
        at = slice(k * part, (k + 1) * part)
        copy = pltpu.make_async_copy(rest.at[at], held.at[at], sems.at[k])
        copy.start()
        copies.append((at, copy))
    return copies


def forward(direction, kept, held, copies, far):
    split = rows_of(direction)
    half = far.shape[1]
    near = split[:, :half]
    total = jnp.sum(dot_nt(split[:, half:], far[...]), axis=0, keepdims=True)
    values = [jnp.sum(dot_nt(near, kept[...]), axis=0, keepdims=True)]
    for at, copy in copies:
        copy.wait()
        values.append(jnp.sum(dot_nt(near, held[at]), axis=0, keepdims=True))
    return jnp.concatenate(values, axis=1) + total


def product(direction, kept, held, copies, far, weight, gathered, tiles, out, scale):
    values = forward(direction, kept, held, copies, far)
    split = stack_rows(split3(weight[...].astype(F32) * values * scale), 16)
    half, first = far.shape[1], kept.shape[0]
    gathered[:, half:] = dot_nn(split, far[...])
    gathered[:, :half] = dot_nn(split[:, :first], kept[...]) + dot_nn(split[:, first:], held[...])
    send_whole(gathered, tiles, out)
    return values


def first_kernel(
    scale, rhs_scale, core, halves, kept, rest, far, weight, out, values_out, rhs_out, gathered, tiles, held, sems
):
    copies = fetch(rest, held, sems)
    low, high = (jnp.sum(halves[h], axis=0) * rhs_scale for h in range(2))
    swap = core[0] == 1
    half = low.shape[0]
    rhs_out[0:half, :] = jnp.where(swap, high, low)
    rhs_out[half : 2 * half, :] = jnp.where(swap, low, high)
    values_out[...] = product(
        rhs_out[...], kept, held, copies, far, weight, gathered, tiles, out, scale
    )


def second_kernel(
    scale, arrived, rhs, before, kept, rest, far, weight,
    out, fit_out, solution_out, residual_out, direction_out,
    gathered, tiles, held, sems,
):
    copies = fetch(rest, held, sems)
    direction = rhs[...]
    norm = total_of(direction * direction)
    image = direction + jnp.sum(arrived[...], axis=0)
    length = norm / total_of(direction * image)
    residual = direction - length * image
    later = residual + total_of(residual * residual) / norm * direction
    solution_out[...] = length * direction
    residual_out[...] = residual
    direction_out[...] = later
    fit_out[0:1, :] = length * before[...]
    fit_out[1:2, :] = product(
        later, kept, held, copies, far, weight, gathered, tiles, out, scale
    )


def third_kernel(
    scale, fit_scale, arrived, solution, residual, direction, fit, kept, rest, far, weight, size, owner, patient,
    out, both_out, norm_out,
    held, sems,
):
    copies = fetch(rest, held, sems)
    before = direction[...]
    left = residual[...]
    norm = total_of(left * left)
    image = before + jnp.sum(arrived[...], axis=0)
    length = norm / total_of(before * image)
    left = left - length * image
    norm_next = total_of(left * left)
    later = left + norm_next / norm * before
    both_out[0] = solution[...] + length * before
    both_out[1] = later
    norm_out[...] = jnp.broadcast_to(norm_next, norm_out.shape)
    values = forward(later, kept, held, copies, far)
    fitted = fit[0:1, :] + length * fit[1:2, :]
    weights = weight[...].astype(F32)
    weighted = weights * values
    energy = total_of(weighted * values) * scale
    part = weights * (size[...].astype(F32) - fitted * fit_scale)
    owners, patients = out.shape[0], out.shape[2]
    here = values.shape[1]
    to_owner = (owner[...] == lax.broadcasted_iota(jnp.int32, (owners, here), 0)).astype(F32)
    to_patient = (patient[...] == lax.broadcasted_iota(jnp.int32, (patients, here), 0)).astype(F32)
    parts = split3(part) + split3(weighted * fit_scale) + (weights,)
    tall = jnp.concatenate([to_owner * part for part in parts], axis=0).astype(BF16)
    sums = dot_nt(tall, to_patient.astype(BF16))
    part = [sums[i * owners : (i + 1) * owners, :] for i in range(len(parts))]
    out[:, 0, :] = part[0] + part[1] + part[2]
    out[:, 1, :] = part[3] + part[4] + part[5]
    out[:, 2, :] = part[6]
    out[:, 3, :] = jnp.broadcast_to(energy, (owners, patients))


NODE_ROWS = 512


def nodes_kernel(both, phi, out, split):
    @pl.when(pl.program_id(0) == 0)
    def _():
        rows = split3(as_row(both[0])) + split3(as_row(both[1]))
        split[...] = stack_rows(rows, 16)

    products = dot_nt(split[...], phi[...])
    out[0:1, :] = products[0:1] + products[1:2] + products[2:3]
    out[1:2, :] = products[3:4] + products[4:5] + products[5:6]


def last_kernel(fit_scale, mine, arrived, both, norm, node_values, time, flag, loglik, weights_out, tiles):
    sums = jnp.sum(arrived[...], axis=0)
    direction = both[1]
    denominator = total_of(direction * direction) + sums[3:4, 0:1]
    length = norm[0:1, 0:1] / denominator
    tiles[...] = both[0] + length * direction
    weights_out[...] = tiles[pl.ds(mine[0], 1), :]
    effect = (sums[0:1, :] - length * sums[1:2, :]) / (1.0 + sums[2:3, :])
    halves = [node_values[h, 0:1, :] + length * node_values[h, 1:2, :] for h in range(2)]
    values = jnp.concatenate(halves, axis=1) * fit_scale
    patients = loglik.shape[1]
    nodes = values.shape[1] // patients
    total = jnp.zeros_like(effect)
    eta = total
    when = time[...]
    for q in range(nodes):
        grid = when * (q + 1.0) / nodes
        eta = (
            LOG_SHAPE
            + 0.5 * jnp.log(grid)
            + LINK * (values[:, q * patients : (q + 1) * patients] + effect)
        )
        total = total + jnp.exp(eta)
    loglik[...] = flag[...].astype(F32) * eta - when / nodes * total


def on_device(
    visit_cov,
    tumor_size,
    visit_weight,
    visit_owner,
    visit_patient,
    inducing_freq,
    inducing_phase,
    node_cov,
    event_time,
    event_flag,
):
    blocks, cols = lax.axis_size("blk"), lax.axis_size("col")
    rows, depth = visit_cov.shape
    own = inducing_freq.shape[1]
    inducing = own * cols
    tall = inducing // LANES
    layers = cols // 2
    patients, nodes = node_cov.shape[:2]
    scale = 1.0 / (rows * blocks)
    fit_scale = 1.0 / math.sqrt(inducing)
    weight = visit_weight.reshape(1, rows)
    size = tumor_size.reshape(1, rows)
    owner = visit_owner.reshape(1, rows)
    patient = visit_patient.reshape(1, rows)
    place = lax.axis_index("col").astype(jnp.int32)
    core = (place % 2).reshape(1)
    layer = (place // 2).reshape(1)
    together = lax.optimization_barrier
    same_core = [[2 * z + c for z in range(layers)] for c in range(2)]
    pairs = [[2 * z, 2 * z + 1] for z in range(layers)]

    packed = pl.pallas_call(
        pack_kernel,
        in_specs=[HBM, HBM],
        out_specs=HBM,
        out_shape=jax.ShapeDtypeStruct((layers, depth + PHASE_ROWS, own), BF16),
        scratch_shapes=[
            pltpu.VMEM((depth + PHASE_ROWS, own), BF16),
            pltpu.VMEM((1, own), BF16),
            pltpu.SemaphoreType.DMA((2 + layers,)),
        ],
        compiler_params=params(60),
        name="pack",
    )(inducing_freq, inducing_phase.reshape(1, own))
    packed, cov, turned = together((packed, visit_cov, node_cov))
    near_freq = lax.all_to_all(packed, "col", 0, 0, tiled=True, axis_index_groups=same_core)
    cov = stage(cov, "stage_cov")
    by_node = turned.transpose(1, 0, 2).reshape(nodes * patients, depth)
    count = nodes * patients // 2
    height = (SPARE * nodes * patients) // 4
    by_node = lax.dynamic_slice_in_dim(by_node, core[0] * count, count, 0)
    near_freq, cov, by_node = together((near_freq, cov, by_node))

    half = inducing // 2
    first = int(rows * KEPT)
    kept, rest, sent = pl.pallas_call(
        near_kernel,
        in_specs=[VMEM] * 4,
        out_specs=[VMEM, HBM, VMEM],
        out_shape=[
            jax.ShapeDtypeStruct((first, half), BF16),
            jax.ShapeDtypeStruct((SPARE * rows, half), BF16),
            jax.ShapeDtypeStruct((blocks, tall // 2, LANES), F32),
        ],
        scratch_shapes=[
            pltpu.VMEM((rows - first, half), BF16),
            pltpu.VMEM((16, half), F32),
            pltpu.VMEM((tall // 2, LANES), F32),
            pltpu.SemaphoreType.DMA((PARTS,)),
        ],
        compiler_params=params(),
        name="near_features",
    )(cov, near_freq, weight, size)
    sent, late_freq = together((sent, near_freq))
    arrived = lax.all_to_all(sent, "blk", 0, 0, tiled=True)
    freq = lax.all_gather(late_freq, "col", axis_index_groups=pairs)
    far = far_features(core, cov, freq)
    arrived, far = together((arrived, far))
    halves = lax.all_gather(arrived, "col", axis_index_groups=pairs)

    message = jax.ShapeDtypeStruct((blocks, tall, LANES), F32)
    vector = jax.ShapeDtypeStruct((tall, LANES), F32)
    fetched = [pltpu.VMEM((rows - first, half), BF16), pltpu.SemaphoreType.DMA((PARTS,))]
    scratch = [pltpu.VMEM((16, inducing), F32), pltpu.VMEM((tall, LANES), F32)] + fetched
    work = cost(64 * rows * inducing, 2 * rows * inducing)

    sent, before, rhs = pl.pallas_call(
        functools.partial(first_kernel, scale, 1.0 / math.sqrt(rows * blocks)),
        in_specs=[SMEM, VMEM, VMEM, HBM, VMEM, VMEM],
        out_specs=[VMEM] * 3,
        out_shape=[message, jax.ShapeDtypeStruct((1, rows), F32), vector],
        scratch_shapes=scratch,
        compiler_params=params(),
        cost_estimate=work,
        name="first_product",
    )(core, halves, kept, rest, far, weight)
    sent, node_cov_now = together((sent, by_node))
    arrived = lax.all_to_all(sent, "blk", 0, 0, tiled=True)
    node_phi = node_features(core, node_cov_now, freq, None, 0, height, "node_features_a")
    arrived, node_phi = together((arrived, node_phi))

    sent, fit, solution, residual, direction = pl.pallas_call(
        functools.partial(second_kernel, scale),
        in_specs=[VMEM] * 4 + [HBM, VMEM, VMEM],
        out_specs=[VMEM] * 5,
        out_shape=[message, jax.ShapeDtypeStruct((2, rows), F32), vector, vector, vector],
        scratch_shapes=scratch,
        compiler_params=params(),
        cost_estimate=work,
        name="second_product",
    )(arrived, rhs, before, kept, rest, far, weight)
    arrived = lax.all_to_all(sent, "blk", 0, 0, tiled=True)
    sent, both, norm = pl.pallas_call(
        functools.partial(third_kernel, scale, fit_scale),
        in_specs=[VMEM] * 6 + [HBM] + [VMEM] * 5,
        out_specs=[VMEM] * 3,
        out_shape=[
            jax.ShapeDtypeStruct((blocks, 4, patients), F32),
            jax.ShapeDtypeStruct((2, tall, LANES), F32),
            jax.ShapeDtypeStruct((8, LANES), F32),
        ],
        scratch_shapes=fetched,
        compiler_params=params(),
        cost_estimate=work,
        name="third_product",
    )(arrived, solution, residual, direction, fit, kept, rest, far, weight, size, owner, patient)
    sent, both = together((sent, both))
    arrived = lax.all_to_all(sent, "blk", 0, 0, tiled=True)
    node_values = pl.pallas_call(
        nodes_kernel,
        grid=(count // NODE_ROWS,),
        in_specs=[
            pl.BlockSpec(both.shape, lambda i: (0, 0, 0)),
            pl.BlockSpec((NODE_ROWS, inducing), lambda i: (i, 0)),
        ],
        out_specs=pl.BlockSpec((2, NODE_ROWS), lambda i: (0, i)),
        out_shape=jax.ShapeDtypeStruct((2, count), F32),
        scratch_shapes=[pltpu.VMEM((16, inducing), BF16)],
        compiler_params=params(),
        cost_estimate=cost(64 * 2 * count * inducing, 4 * count * inducing),
        name="node_values",
    )(both, node_phi)
    node_values = lax.all_gather(node_values, "col", axis_index_groups=pairs)
    arrived, node_values = together((arrived, node_values))

    loglik, weights = pl.pallas_call(
        functools.partial(last_kernel, fit_scale),
        in_specs=[SMEM] + [VMEM] * 6,
        out_specs=[VMEM, VMEM],
        out_shape=[
            jax.ShapeDtypeStruct((1, patients), F32),
            jax.ShapeDtypeStruct((1, own), F32),
        ],
        scratch_shapes=[pltpu.VMEM((tall, LANES), F32)],
        compiler_params=params(),
        name="last",
    )(
        layer,
        arrived,
        both,
        norm,
        node_values,
        event_time.reshape(1, patients),
        event_flag.reshape(1, patients),
    )
    return loglik.reshape(patients), weights.reshape(own)


def solution(mesh):
    in_specs = (
        P("blk", None),
        P("blk"),
        P("blk"),
        P("blk", None),
        P("blk"),
        P(None, "col"),
        P("col"),
        P("blk", None, None),
        P("blk"),
        P("blk"),
    )
    out_specs = (P("blk"), P("col"))
    return jax.shard_map(
        on_device, mesh=mesh, in_specs=in_specs, out_specs=out_specs, check_vma=False
    )
```
